32 devices in a mesh: half: 2 (over x), cells: 16 (over z, y, core).
Axes of the slice: x: 2, y: 2, z: 4, core: 2. Of those that a mesh axis runs over, the one named last changes fastest.
Arguments:
- tokens: bfloat16 [2, 32, 1024, 512], P('half', 'cells'), may hold values from -6 to 6
- known_len: int32 [32], P('cells'), may hold values from 256 to 1024, as said below
- unknown_len: int32 [32], P('cells'), may hold values from 256 to 1024, as said below
- query_weight: bfloat16 [512, 512], replicated, may hold values from -0.25 to 0.25
- query_bias: float32 [512], replicated, may hold values from -1.75 to 1.75
- key_weight: bfloat16 [512, 512], replicated, may hold values from -0.25 to 0.25
- value_weight: bfloat16 [512, 512], replicated, may hold values from -0.25 to 0.25
- value_bias: float32 [512], replicated, may hold values from -1.75 to 1.75
- output_weight: bfloat16 [512, 512], replicated, may hold values from -1 to 1
- output_bias: float32 [512], replicated, may hold values from -1.75 to 1.75
- first_gain: float32 [512], replicated, may hold values from 0.5 to 1.5
- first_shift: float32 [512], replicated, may hold values from -1.75 to 1.75
- hidden_weight: bfloat16 [512, 512], replicated, may hold values from -0.25 to 0.25
- hidden_bias: float32 [512], replicated, may hold values from -1.75 to 1.75
- return_weight: bfloat16 [512, 512], replicated, may hold values from -0.25 to 0.25
- return_bias: float32 [512], replicated, may hold values from -1.75 to 1.75
- second_gain: float32 [512], replicated, may hold values from 0.5 to 1.5
- second_shift: float32 [512], replicated, may hold values from -1.75 to 1.75
- cotangent: bfloat16 [2, 32, 1024, 512], P('half', 'cells'), may hold values from -6 to 6
Outputs:
- layer_out: bfloat16 [2, 32, 1024, 512], P('half', 'cells')
- grad_tokens: bfloat16 [2, 32, 1024, 512], P('half', 'cells')
- grad_query_weight: float32 [512, 512], replicated
- grad_query_bias: float32 [512], replicated
- grad_key_weight: float32 [512, 512], replicated
- grad_value_weight: float32 [512, 512], replicated
- grad_value_bias: float32 [512], replicated
- grad_output_weight: float32 [512, 512], replicated
- grad_output_bias: float32 [512], replicated
- grad_first_gain: float32 [512], replicated
- grad_first_shift: float32 [512], replicated
- grad_hidden_weight: float32 [512, 512], replicated
- grad_hidden_bias: float32 [512], replicated
- grad_return_weight: float32 [512, 512], replicated
- grad_return_bias: float32 [512], replicated
- grad_second_gain: float32 [512], replicated
- grad_second_shift: float32 [512], replicated
The draws below stay inside these ranges and needn't reach their ends.
Inputs may be any that keep to these rules, and one draw needn't show every extreme that they name: `known_len`: live known tokens of each cell; some cell has exactly 1024. `unknown_len`: live unknown tokens of each cell; some cell has exactly 1024.
All inputs are finite; a program needn't handle non-finite values.
Results may differ from the reference program's by a relative error of at most 0.013.
Values may be sent and summed in bfloat16 or wider, within the bound.
A program may use at most 320 MiB of HBM per device.

```python
import math
import jax
import jax.numpy as jnp
from jax import lax

D = 512
FF = 512
HEADS = 8
HDIM = 64
SLOTS = 1024
CELLS = 32
N_HALF = 2


def draw_known_len(key, part):
    key = jax.random.fold_in(key, 11)
    counts = jax.random.randint(key, (CELLS,), max(SLOTS // 4, 1), SLOTS + 1)
    return counts.at[0].set(SLOTS).astype(jnp.int32)


def draw_unknown_len(key, part):
    key = jax.random.fold_in(key, 23)
    counts = jax.random.randint(key, (CELLS,), max(SLOTS // 4, 1), SLOTS + 1)
    return counts.at[CELLS - 1].set(SLOTS).astype(jnp.int32)


def steps_of(key, dims, cuts, smallest, largest):
    loudness, own = 1.0, jax.random.fold_in(key, 6)
    for position, parts in cuts:
        draws = jnp.exp(jax.random.uniform(jax.random.fold_in(own, position), (parts,), jnp.float32, smallest / len(cuts), largest / len(cuts)))
        loudness = loudness * jnp.repeat(draws, dims[position] // parts).reshape([-1 if axis == position else 1 for axis in range(len(dims))])
    return loudness


def scatter_about(rng, dims, deviation, bound, cuts=(), kind=jnp.bfloat16):
    drawn = jax.random.normal(rng, dims, jnp.float32) * deviation
    if len(cuts) > 0:
        drawn = steps_of(rng, dims, cuts, -0.22, 0.18) * drawn
    return jnp.clip(drawn, min=-bound, max=bound).astype(kind)


def setup_inputs(seed: int = 0) -> dict:
    streams_of = jax.random.split(jax.random.key(seed), 20)
    tokens = scatter_about(streams_of[0], (N_HALF, CELLS, SLOTS, D), 1.0, 6.0, ((0, 2), (1, 16)))
    known_len = draw_known_len(jax.random.fold_in(streams_of[19], 71), 0)
    unknown_len = draw_unknown_len(jax.random.fold_in(streams_of[19], 71), 0)
    query_weight = scatter_about(streams_of[3], (D, D), D ** -0.5, 0.25)
    query_bias = scatter_about(streams_of[4], (D,), 0.3, 1.75, (), jnp.float32)
    key_weight = scatter_about(streams_of[5], (D, D), D ** -0.5, 0.25)
    value_weight = scatter_about(streams_of[6], (D, D), D ** -0.5, 0.25)
    value_bias = scatter_about(streams_of[7], (D,), 0.3, 1.75, (), jnp.float32)
    output_weight = scatter_about(streams_of[8], (D, D), (max(D // 16, 1)) ** -0.5, 1.0)
    output_bias = scatter_about(streams_of[9], (D,), 0.3, 1.75, (), jnp.float32)
    first_gain = jnp.clip(1.0 + 0.1 * jax.random.normal(streams_of[10], (D,), jnp.float32), 0.5, 1.5)
    first_shift = scatter_about(streams_of[11], (D,), 0.3, 1.75, (), jnp.float32)
    hidden_weight = scatter_about(streams_of[12], (D, FF), D ** -0.5, 0.25)
    hidden_bias = scatter_about(streams_of[13], (FF,), 0.3, 1.75, (), jnp.float32)
    return_weight = scatter_about(streams_of[14], (FF, D), FF ** -0.5, 0.25)
    return_bias = scatter_about(streams_of[15], (D,), 0.3, 1.75, (), jnp.float32)
    second_gain = jnp.clip(1.0 + 0.1 * jax.random.normal(streams_of[16], (D,), jnp.float32), 0.5, 1.5)
    second_shift = scatter_about(streams_of[17], (D,), 0.3, 1.75, (), jnp.float32)
    cotangent = scatter_about(streams_of[18], (N_HALF, CELLS, SLOTS, D), 1.0, 6.0, ((0, 2), (1, 16)))
    return dict(tokens=tokens, known_len=known_len, unknown_len=unknown_len, query_weight=query_weight, query_bias=query_bias, key_weight=key_weight, value_weight=value_weight, value_bias=value_bias, output_weight=output_weight, output_bias=output_bias, first_gain=first_gain, first_shift=first_shift, hidden_weight=hidden_weight, hidden_bias=hidden_bias, return_weight=return_weight, return_bias=return_bias, second_gain=second_gain, second_shift=second_shift, cotangent=cotangent)


@jax.custom_vjp
def low(v):
    return lax.optimization_barrier(v.astype(jnp.bfloat16)).astype(jnp.float32)

@jax.custom_vjp
def low_back(v):
    return v

def low_keep(v):
    return (low(v), None)

def low_pass(kept, grad):
    return (grad,)

def back_keep(v):
    return (v, None)

def back_low(kept, grad):
    return (low(grad),)
low.defvjp(low_keep, low_pass)
low_back.defvjp(back_keep, back_low)
EPS = 1e-05
HIGH = lax.Precision.HIGHEST
NEGATIVE = -1e+30

def layer_norm(resid, gain, shift):
    row_mean = lax.optimization_barrier(jnp.mean(resid, axis=-1, keepdims=True))
    centred = resid - row_mean
    row_var = lax.optimization_barrier(jnp.mean(centred * centred, axis=-1, keepdims=True))
    return centred * lax.rsqrt(row_var + EPS) * gain + shift

def project(left, right):
    return jnp.einsum('...d,df->...f', left, right, precision=HIGH)

def group_layer(params, block_in):
    query_weight, query_bias, key_weight, value_weight, value_bias, output_weight, output_bias, first_gain, first_shift, hidden_weight, hidden_bias, return_weight, return_bias, second_gain, second_shift = params
    inputs, known_block, unknown_block = block_in
    group = inputs.shape[1]
    slot_index = jnp.arange(SLOTS, dtype=jnp.int32)
    known_live = slot_index[None, :] < known_block[:, None]
    unknown_live = slot_index[None, :] < unknown_block[:, None]
    live_rows = jnp.stack([known_live, unknown_live]).astype(jnp.float32)
    queries = low(low_back(project(inputs, query_weight) + query_bias))
    keys_all = low(low_back(project(inputs, key_weight)))
    vals_all = low(low_back(project(inputs, value_weight) + value_bias))
    far_in = low_back(inputs[0])
    far_keys = low(low_back(project(far_in, key_weight)))
    far_vals = low(low_back(project(far_in, value_weight) + value_bias))
    shape_heads = (2, group, SLOTS, HEADS, HDIM)
    query_h = queries.reshape(shape_heads)
    key_h = keys_all.reshape(shape_heads)
    value_h = vals_all.reshape(shape_heads)
    far_key_h = far_keys.reshape(shape_heads[1:])
    far_value_h = far_vals.reshape(shape_heads[1:])
    score_scale = HDIM ** (-0.5)
    known_scores = low_back(jnp.einsum('gqhe,gkhe->ghqk', query_h[0], key_h[0], precision=HIGH) * score_scale)
    unknown_scores = low_back(jnp.einsum('gqhe,gkhe->ghqk', query_h[1], far_key_h, precision=HIGH) * score_scale)
    self_scores = low_back(jnp.einsum('gqhe,gqhe->ghq', query_h[1], key_h[1], precision=HIGH) * score_scale)
    key_mask = known_live[:, None, None, :]
    known_masked = jnp.where(key_mask, known_scores, NEGATIVE)
    unknown_masked = jnp.where(key_mask, unknown_scores, NEGATIVE)
    known_probs = low(jax.nn.softmax(known_masked, axis=-1))
    unknown_all = jnp.concatenate([unknown_masked, self_scores[..., None]], axis=-1)
    unknown_probs = low(jax.nn.softmax(unknown_all, axis=-1))
    known_context = jnp.einsum('ghqk,gkhe->gqhe', known_probs, value_h[0], precision=HIGH)
    self_weight = jnp.transpose(unknown_probs[..., SLOTS], (0, 2, 1))[..., None]
    unknown_context = jnp.einsum('ghqk,gkhe->gqhe', unknown_probs[..., :SLOTS], far_value_h, precision=HIGH) + self_weight * value_h[1]
    context = jnp.stack([known_context, unknown_context]).reshape(2, group, SLOTS, D)
    context = low(low_back(context))
    attn = low_back(project(context, output_weight) + output_bias)
    norm_one = layer_norm(inputs + attn, first_gain, first_shift)
    pre_act = low_back(project(low(norm_one), hidden_weight) + hidden_bias)
    act = low(jax.nn.gelu(pre_act, approximate=False))
    branch = low_back(project(act, return_weight) + return_bias)
    return layer_norm(norm_one + branch, second_gain, second_shift) * live_rows[..., None]

def reference(tokens, known_len, unknown_len, query_weight, query_bias, key_weight, value_weight, value_bias, output_weight, output_bias, first_gain, first_shift, hidden_weight, hidden_bias, return_weight, return_bias, second_gain, second_shift, cotangent):
    params = tuple((array.astype(jnp.float32) for array in (query_weight, query_bias, key_weight, value_weight, value_bias, output_weight, output_bias, first_gain, first_shift, hidden_weight, hidden_bias, return_weight, return_bias, second_gain, second_shift)))
    inputs = tokens.astype(jnp.float32)
    group = math.gcd(CELLS, 2)
    blocks_count = CELLS // group

    def forward(inputs, params):
        blocks = inputs.reshape(N_HALF, blocks_count, group, SLOTS, D).transpose(1, 0, 2, 3, 4)
        known_blocks = known_len.reshape(blocks_count, group)
        unknown_blocks = unknown_len.reshape(blocks_count, group)

        def step(carry, block_in):
            return (carry, jax.checkpoint(group_layer)(params, block_in))
        _, results = lax.scan(step, jnp.zeros((), jnp.float32), (blocks, known_blocks, unknown_blocks))
        return results.transpose(1, 0, 2, 3, 4).reshape(N_HALF, CELLS, SLOTS, D)
    layer_out, pullback = jax.vjp(forward, inputs, params)
    grad_inputs, grads = pullback(cotangent.astype(jnp.float32))
    grad_query_weight, grad_query_bias, grad_key_weight, grad_value_weight, grad_value_bias, grad_output_weight, grad_output_bias, grad_first_gain, grad_first_shift, grad_hidden_weight, grad_hidden_bias, grad_return_weight, grad_return_bias, grad_second_gain, grad_second_shift = grads
    return (layer_out.astype(jnp.bfloat16), grad_inputs.astype(jnp.bfloat16), grad_query_weight, grad_query_bias, grad_key_weight, grad_value_weight, grad_value_bias, grad_output_weight, grad_output_bias, grad_first_gain, grad_first_shift, grad_hidden_weight, grad_hidden_bias, grad_return_weight, grad_return_bias, grad_second_gain, grad_second_shift)
```

```python
import functools

import jax
import jax.numpy as jnp
from jax import lax
from jax.experimental import pallas as pl
from jax.experimental.pallas import tpu as pltpu
from jax.sharding import PartitionSpec as P

HEADS = 8
EPS = 1e-05
NEGATIVE = -1e30
LOG2E = 1.4426950408889634
BF = jnp.bfloat16
F32 = jnp.float32
SAFE = 60.0
DENSE_TURNS = (0, 2, 6, 8, 10, 13, 14, 15)
VMEM_LIMIT = 58 * 2**20
STEP = 256


def nn(a, b):
    return lax.dot_general(a, b, (((1,), (0,)), ((), ())), preferred_element_type=F32)


def nt(a, b):
    return lax.dot_general(a, b, (((1,), (1,)), ((), ())), preferred_element_type=F32)


def tn(a, b):
    return lax.dot_general(a, b, (((0,), (0,)), ((), ())), preferred_element_type=F32)


def cells_of(info):
    return (info.shape[0] - 1) // 2


def params(**more):
    return pltpu.CompilerParams(vmem_limit_bytes=VMEM_LIMIT, **more)


def column(vector, lanes):
    n = vector.shape[1]
    tile = jnp.broadcast_to(vector, (128, n)).T
    return jnp.concatenate([tile] * (lanes // 128), axis=1)


def head_norms(array, head_dim):
    width, tokens = array.shape
    squares = (array * array).reshape(width // head_dim, head_dim, tokens)
    return jnp.max(jnp.sum(squares, axis=1))


def own_kernel(head_dim, x_hbm, x, wq, bq, wk, wv, bv, qt, kt, vt, again, norm, far, *scratch):
    wqt, wkt, wvt, bqc, bvc, sent, arrived = scratch
    cell, block = pl.program_id(0), pl.program_id(1)
    rows = x.shape[1]
    half_at = lax.axis_index("half")
    is_known = half_at == 0
    other = {"half": 1 - half_at, "cells": lax.axis_index("cells")}
    copy = pltpu.make_async_remote_copy(
        src_ref=x_hbm.at[0],
        dst_ref=far,
        send_sem=sent,
        recv_sem=arrived,
        device_id=other,
        device_id_type=pl.DeviceIdType.MESH,
    )

    @pl.when((cell == 0) & (block == 0))
    def _():
        barrier = pltpu.get_barrier_semaphore()
        pl.semaphore_signal(barrier, inc=1, device_id=other, device_id_type=pl.DeviceIdType.MESH)
        pl.semaphore_wait(barrier, 1)

        @pl.when(is_known)
        def _():
            copy.start()

        wqt[...] = wq[...].T
        wkt[...] = wk[...].T
        wvt[...] = wv[...].T
        bqc[...] = column(bq[...], rows)
        bvc[...] = column(bv[...], rows)

    @pl.when(block == 0)
    def _():
        norm[0, cell] = 0.0
        norm[1, cell] = 0.0

    again[...] = x[0]
    queries = (nt(wqt[...], x[0]) + bqc[...]) * (LOG2E * head_dim**-0.5)
    qt[0] = queries.astype(BF)
    norm[0, cell] = jnp.maximum(norm[0, cell], head_norms(queries, head_dim))

    @pl.when(jnp.logical_not(is_known))
    def _():
        keys = nt(wkt[...], x[0])
        kt[0] = keys.astype(BF)
        norm[1, cell] = jnp.maximum(norm[1, cell], head_norms(keys, head_dim))
        vt[0] = (nt(wvt[...], x[0]) + bvc[...]).astype(BF)

    @pl.when((cell == pl.num_programs(0) - 1) & (block == pl.num_programs(1) - 1))
    def _():
        @pl.when(is_known)
        def _():
            copy.wait_send()

        @pl.when(jnp.logical_not(is_known))
        def _():
            copy.wait_recv()


def project_own(x, wq, bq, wk, wv, bv, rows=512):
    cells, slots, width = x.shape
    head_dim = width // HEADS
    weight = pl.BlockSpec((width, width), lambda c, i: (0, 0))
    bias = pl.BlockSpec((1, width), lambda c, i: (0, 0))
    out = pl.BlockSpec((1, width, rows), lambda c, i: (c, 0, i))
    hbm = pl.BlockSpec(memory_space=pl.ANY)
    last = cells - 1
    return pl.pallas_call(
        functools.partial(own_kernel, head_dim),
        grid=(cells, slots // rows),
        in_specs=[
            hbm,
            pl.BlockSpec((1, rows, width), lambda c, i: (c, i, 0)),
            weight,
            bias,
            weight,
            weight,
            bias,
        ],
        out_specs=[
            out,
            out,
            out,
            pl.BlockSpec((rows, width), lambda c, i: (lax.div(c, last) * i, 0)),
            pl.BlockSpec(memory_space=pltpu.SMEM),
            hbm,
        ],
        out_shape=[jax.ShapeDtypeStruct((cells, width, slots), BF)] * 3
        + [
            jax.ShapeDtypeStruct((slots, width), BF),
            jax.ShapeDtypeStruct((2, cells), F32),
            jax.ShapeDtypeStruct((slots, width), BF),
        ],
        scratch_shapes=[pltpu.VMEM((width, width), BF)] * 3
        + [pltpu.VMEM((width, rows), F32)] * 2
        + [pltpu.SemaphoreType.DMA] * 2,
        compiler_params=params(collective_id=1, has_side_effects=True),
        name="project_own",
    )(x, x, wq, bq, wk, wv, bv)


def steps_in(length):
    return lax.div(length + STEP - 1, STEP)


def sized(count, steps, body):
    for n in range(1, count + 1):
        pl.when(steps == n)(functools.partial(body, n * STEP))


def sized_pair(count, key_steps, own_steps, body):
    for a in range(1, count + 1):
        for b in range(1, count + 1):
            pl.when((key_steps == a) & (own_steps == b))(functools.partial(body, a * STEP, b * STEP))


def in_turns(chains):
    waiting = [iter(chain) for chain in chains]
    running = []
    while waiting or running:
        if waiting:
            running.append(waiting.pop(0))
        running = [chain for chain in running if next(chain, None) is not None]


def fold_rows(values):
    rows, width = values.shape
    return jnp.sum(values.reshape(rows // 8, 8, width), axis=0)


def fetch(pairs, semaphores):
    copies = [
        pltpu.make_async_copy(source, target, semaphores.at[i]) for i, (source, target) in enumerate(pairs)
    ]
    for copy in copies:
        copy.start()
    return copies


def wait(*copies):
    for copy in copies:
        copy.wait()


def taker(refs):
    place = 0

    def take(count):
        nonlocal place
        place += count
        return refs[place - count : place]

    return take


def cell_kernel(cell, first, whole, *refs):
    take = taker(refs)
    info, own_norm, x_hbm, far_hbm, cot_hbm, qt_hbm, skt_hbm, svt_hbm = take(8)
    wk_hbm, wv_hbm, wo_hbm, wh_hbm, wr_hbm = take(5)
    (wq_hbm,) = take(1) if whole else (None,)
    bv, bo, g1, s1, bh, br, g2, s2 = take(8)
    sums_before, vecs_before, back_before, back_vecs_before = None, None, None, None
    if not first:
        _, sums_before, vecs_before = take(3)
        if whole:
            back_before, back_vecs_before = take(2)
    if whole:
        out_hbm, sums_hbm, vecs, grad_hbm, far_grad_hbm, back_hbm, back_vecs = take(7)
    else:
        out_hbm, sums_hbm, vecs, pt_hbm, kt_hbm, vt_hbm, dot_hbm, gres_hbm, inverse, self_exp, delta = take(11)
    x, far, cot, qt, skt, svt, wk, wv, wo, wh, wr = take(11)
    kt, vt, ot, dot_t, low1, act, gb, gpre, gres, out, sums, pt, wkt, wvt, bvc = take(15)
    if whole:
        wq, wqt, back_sums, inverse, self_exp, delta = take(6)
    in_sem, out_sem, pt_sem = take(3)

    slots, width = x.shape
    head_dim = width // HEADS
    is_known = info[0] == 1
    cells = (info.shape[0] - 1) // 2
    key_len, own_len = info[1 + cell], info[1 + cells + cell]
    key_steps, own_steps = steps_in(key_len), steps_in(own_len)
    blocks = slots // STEP

    loads = fetch(
        [(wk_hbm, wk), (wv_hbm, wv), (x_hbm.at[cell], x), (far_hbm, far)],
        in_sem,
    )
    wait(*loads)
    loads += fetch(
        [
            (qt_hbm.at[cell], qt),
            (skt_hbm.at[cell], skt),
            (svt_hbm.at[cell], svt),
            (wo_hbm, wo),
            (wh_hbm, wh),
            (wr_hbm, wr),
            (cot_hbm.at[cell], cot),
        ]
        + ([] if first else [(sums_before, sums)])
        + ([(wq_hbm, wq)] if whole else [])
        + ([(back_before, back_sums)] if whole and not first else []),
        in_sem.at[pl.ds(4, 10)],
    )

    wkt[...] = wk[...].T
    wvt[...] = wv[...].T
    bvc[...] = column(bv[...], STEP)

    def project(block, largest):
        part = pl.ds(pl.multiple_of(block * STEP, STEP), STEP)
        source = jnp.where(is_known, x[part], far[part])
        keys = nt(wkt[...], source)
        kt[:, part] = keys.astype(BF)
        vt[:, part] = (nt(wvt[...], source) + bvc[...]).astype(BF)
        return jnp.maximum(largest, head_norms(keys, head_dim))

    def blank(targets, block, carry):
        part = pl.ds(pl.multiple_of(block * STEP, STEP), STEP)
        for target in targets:
            if target.shape[0] == slots:
                target[part] = jnp.zeros((STEP, width), BF)
            else:
                target[:, part] = jnp.zeros((target.shape[0], STEP), target.dtype)
        return carry

    largest = lax.fori_loop(0, key_steps, project, jnp.float32(0.0))
    lax.fori_loop(key_steps, blocks, functools.partial(blank, (kt, vt)), 0)

    if whole:
        lax.fori_loop(own_steps, blocks, functools.partial(blank, (out,)), 0)
    else:

        @pl.when((key_steps < blocks) | (own_steps < blocks))
        def _():
            pt[...] = jnp.zeros_like(pt)

        lax.fori_loop(
            own_steps, blocks, functools.partial(blank, (out, gres, dot_t, inverse, self_exp, delta)), 0
        )
    out_copies = [] if whole else fetch([(kt, kt_hbm), (vt, vt_hbm)], out_sem)

    wait(*loads[4:7])
    largest = jnp.maximum(largest, own_norm[1, cell])
    safe = own_norm[0, cell] * largest < SAFE * SAFE

    def attend(head, slot, use_max, keys, queries):
        band = pl.ds(pl.multiple_of(head * head_dim, head_dim), head_dim)
        index = lax.broadcasted_iota(jnp.int32, (16, keys), 1)
        first_row = lax.broadcasted_iota(jnp.int32, (16, keys), 0) == 0
        masked = jnp.where(first_row & (index >= key_len), NEGATIVE, 0.0).astype(BF)
        key_part = jnp.concatenate([kt[band, :keys], masked], axis=0)
        q = qt[band, :queries]
        query_part = jnp.concatenate([q, jnp.ones((16, queries), BF)], axis=0)
        value_part = jnp.concatenate([vt[band, :keys], jnp.ones((16, keys), BF)], axis=0)
        scores = tn(key_part, query_part)
        own = jnp.sum(q.astype(F32) * skt[band, :queries].astype(F32), axis=0, keepdims=True)
        own = jnp.where(is_known, NEGATIVE, own)
        if use_max:
            top = jnp.maximum(jnp.max(scores, axis=0, keepdims=True), own)
            scores = scores - top
            own = own - top
        weights = jnp.exp2(scores).astype(BF)
        pt[slot, :keys, :queries] = weights
        own = jnp.exp2(own)
        total = nn(value_part, weights)
        inv = 1.0 / (total[head_dim : head_dim + 1] + own)
        own_values = jnp.where(is_known, 0.0, svt[band, :queries].astype(F32))
        ot[band, :queries] = ((total[:head_dim] + own * own_values) * inv).astype(BF)
        row = pl.ds(head, 1)
        inverse[row, :queries] = inv
        self_exp[row, :queries] = own

    def keep(head, slot):
        return pltpu.make_async_copy(pt.at[slot], pt_hbm.at[head], pt_sem.at[slot])

    def one_head(head, carry):
        slot = head if whole else lax.rem(head, 2)
        if not whole:

            @pl.when(head >= 2)
            def _():
                keep(head - 2, slot).wait()

        @pl.when(safe)
        def _():
            sized_pair(blocks, key_steps, own_steps, functools.partial(attend, head, slot, False))

        @pl.when(jnp.logical_not(safe))
        def _():
            attend(head, slot, True, slots, slots)

        if not whole:
            keep(head, slot).start()
        return carry

    lax.fori_loop(0, HEADS, one_head, 0)

    wait(*loads[7:11])
    scale = 1.0 / width
    if first:
        vecs[...] = jnp.zeros_like(vecs)
    else:
        vecs[...] = vecs_before[...]

    def mean(values):
        return jnp.sum(values, axis=1, keepdims=True) * scale

    def chain(block):
        start = pl.multiple_of(block * STEP, STEP)
        part = pl.ds(start, STEP)
        slot_index = lax.broadcasted_iota(jnp.int32, (STEP, 1), 0) + start
        live = (slot_index < own_len).astype(F32)
        context = ot[:, part]
        r1 = tn(context, wo[...])
        yield 1
        r1 = r1 + x[part].astype(F32) + bo[...]
        centred = r1 - mean(r1)
        inv1 = lax.rsqrt(mean(centred * centred) + EPS)
        hat1 = centred * inv1
        norm1 = hat1 * g1[...] + s1[...]
        low = norm1.astype(BF)
        low1[part] = low
        yield 2
        pre = nn(low, wh[...])
        yield 3
        pre = pre + bh[...]
        cdf = 0.5 + 0.5 * lax.erf(pre * (0.5**0.5))
        active = (pre * cdf).astype(BF)
        act[part] = active
        slope = cdf + pre * (jnp.exp(-0.5 * pre * pre) * 0.3989422804014327)
        yield 4
        r2 = nn(active, wr[...])
        yield 5
        r2 = r2 + norm1 + br[...]
        centred = r2 - mean(r2)
        inv2 = lax.rsqrt(mean(centred * centred) + EPS)
        hat2 = centred * inv2
        out[part] = ((hat2 * g2[...] + s2[...]) * live).astype(BF)
        go = cot[part].astype(F32) * live
        vecs[0] += fold_rows(go * hat2)
        vecs[1] += fold_rows(go)
        gx = go * g2[...]
        gr2 = inv2 * (gx - mean(gx) - hat2 * mean(gx * hat2))
        grad_branch = gr2.astype(BF)
        gb[part] = grad_branch
        vecs[2] += fold_rows(grad_branch.astype(F32))
        yield 6
        grad_act = nt(grad_branch, wr[...])
        yield 7
        grad_pre = (grad_act * slope).astype(BF)
        gpre[part] = grad_pre
        vecs[3] += fold_rows(grad_pre.astype(F32))
        yield 8
        gn = nt(grad_pre, wh[...])
        yield 9
        gn = gr2 + gn
        vecs[4] += fold_rows(gn * hat1)
        vecs[5] += fold_rows(gn)
        gx = gn * g1[...]
        gr1 = inv1 * (gx - mean(gx) - hat1 * mean(gx * hat1))
        grad_attn = gr1.astype(BF)
        gres[part] = grad_attn
        vecs[6] += fold_rows(grad_attn.astype(F32))
        yield 10
        back = nt(wo[...], grad_attn)
        yield 11
        low_back = back.astype(BF)
        dot_t[:, part] = low_back
        product = low_back.astype(F32) * context.astype(F32)
        delta[:, part] = jnp.sum(product.reshape(HEADS, head_dim, STEP), axis=1)

    def pair(index, carry):
        in_turns([chain(2 * index), chain(2 * index + 1)])
        return carry

    lax.fori_loop(0, lax.div(own_steps, 2), pair, 0)

    @pl.when(lax.rem(own_steps, 2) == 1)
    def _():
        in_turns([chain(own_steps - 1)])

    out_copies += fetch(
        [(out, out_hbm.at[cell])] + ([] if whole else [(dot_t, dot_hbm), (gres, gres_hbm)]), out_sem.at[pl.ds(2, 3)]
    )
    if not first:
        wait(loads[11])

    def weight_sums(rows):
        for i, value in enumerate(
            (
                lambda: nn(ot[:, :rows], gres[:rows]),
                lambda: tn(low1[:rows], gpre[:rows]),
                lambda: tn(act[:rows], gb[:rows]),
            )
        ):
            sums[i] = value() if first else sums[i] + value()

    sized(blocks, own_steps, weight_sums)
    out_copies += fetch([(sums, sums_hbm)], out_sem.at[pl.ds(5, 1)])
    if not whole:
        for slot in range(2):
            keep(HEADS - 2 + slot, slot).wait()
        wait(*out_copies)
        return

    def attend_back(head, keys, queries):
        band = pl.ds(pl.multiple_of(head * head_dim, head_dim), head_dim)
        row = pl.ds(head, 1)
        q = qt[band, :queries]
        inv = inverse[row, :queries]
        grads = dot_t[band, :queries].astype(F32)
        scaled = (grads * inv).astype(BF)
        inner = delta[row, :queries]
        inner_scaled = inner * inv
        high = inner_scaled.astype(BF)
        rest = (inner_scaled - high.astype(F32)).astype(BF)
        wide = jnp.concatenate(
            [scaled, jnp.broadcast_to(high, (8, queries)), jnp.broadcast_to(rest, (8, queries))], axis=0
        )
        signs = jnp.where(lax.broadcasted_iota(jnp.int32, (16, STEP), 0) % 8 == 0, -1.0, 0.0).astype(BF)
        total = 0.0
        for start in range(0, keys, STEP):
            part = slice(start, start + STEP)
            weights = pt[head, part, :queries]
            grad_probs = tn(jnp.concatenate([vt[band, part], signs], axis=0), wide)
            grad_scores = (weights.astype(F32) * grad_probs).astype(BF)
            total = total + nn(kt[band, part], grad_scores)
            vt[band, part] = nt(scaled, weights).astype(BF)
            kt[band, part] = (nt(q, grad_scores) * (1.0 / LOG2E)).astype(BF)
        prob = self_exp[row, :queries] * inv
        own_keys = jnp.where(is_known, 0.0, skt[band, :queries].astype(F32))
        own_values = jnp.where(is_known, 0.0, svt[band, :queries].astype(F32))
        grad_prob = jnp.sum(grads * own_values, axis=0, keepdims=True)
        grad_score = prob * (grad_prob - inner)
        qt[band, :queries] = ((total + grad_score * own_keys) * head_dim**-0.5).astype(BF)
        skt[band, :queries] = (q.astype(F32) * (grad_score * (1.0 / LOG2E))).astype(BF)
        svt[band, :queries] = (grads * prob).astype(BF)

    def one_head_back(head, carry):
        sized_pair(blocks, key_steps, own_steps, functools.partial(attend_back, head))
        return carry

    lax.fori_loop(0, HEADS, one_head_back, 0)

    grad, far_grad = act, gb
    wait(*loads[11 + (not first) :])
    wqt[...] = wq[...].T
    back_vecs[...] = jnp.zeros_like(back_vecs) if first else back_vecs_before[...]

    def far_rows(rows):
        for start in range(0, rows, STEP):
            part = slice(start, start + STEP)
            far_grad[part] = (tn(kt[:, part], wkt[...]) + tn(vt[:, part], wvt[...])).astype(BF)

    def far_sums(rows):
        back_vecs[1] += nt(jnp.ones((8, rows), BF), vt[:, :rows])
        back_sums[1] += nn(kt[:, :rows], far[:rows])
        back_sums[2] += nn(vt[:, :rows], far[:rows])

    def own_rows(rows):
        grad_k = jnp.where(is_known, kt[:, :rows], skt[:, :rows])
        grad_v = jnp.where(is_known, vt[:, :rows], svt[:, :rows])
        grad_q = qt[:, :rows]
        ones = jnp.ones((8, rows), BF)
        back_vecs[0] += nt(ones, grad_q)
        back_vecs[1] += nt(ones, grad_v)
        for i, part in enumerate((grad_q, grad_k, grad_v)):
            back_sums[i] = nn(part, x[:rows]) if first else back_sums[i] + nn(part, x[:rows])
        for start in range(0, rows, STEP):
            part = slice(start, start + STEP)
            total = gres[part].astype(F32) + tn(grad_q[:, part], wqt[...])
            total = total + tn(grad_k[:, part], wkt[...]) + tn(grad_v[:, part], wvt[...])
            grad[part] = total.astype(BF)

    @pl.when(jnp.logical_not(is_known))
    def _():
        sized(blocks, key_steps, far_rows)

    lax.fori_loop(key_steps, blocks, functools.partial(blank, (far_grad,)), 0)
    out_copies += fetch([(far_grad, far_grad_hbm)], out_sem.at[pl.ds(0, 1)])
    sized(blocks, own_steps, own_rows)
    lax.fori_loop(own_steps, blocks, functools.partial(blank, (grad,)), 0)
    out_copies += fetch([(grad, grad_hbm)], out_sem.at[pl.ds(1, 1)])

    @pl.when(jnp.logical_not(is_known))
    def _():
        sized(blocks, key_steps, far_sums)

    out_copies += fetch([(back_sums, back_hbm)], out_sem.at[pl.ds(3, 1)])
    wait(*out_copies)


def run_cell(info, cell, whole, own_norm, x, far, cot, qt, skt, svt, weights, vectors, carried):
    cells, slots, width = x.shape
    smem = pl.BlockSpec(memory_space=pltpu.SMEM)
    vmem = pl.BlockSpec(memory_space=pltpu.VMEM)
    hbm = pl.BlockSpec(memory_space=pl.ANY)
    first = not carried
    across, along = (width, slots), (slots, width)
    square = (width, width)
    matrices = jax.ShapeDtypeStruct((3, width, width), F32)
    stats = (HEADS, slots)
    if whole:
        extra_specs = [hbm, hbm, hbm, vmem]
        extra = [jax.ShapeDtypeStruct(along, BF)] * 2 + [matrices, jax.ShapeDtypeStruct((2, 8, width), F32)]
        last = [pltpu.VMEM(square, BF)] * 2 + [pltpu.VMEM((3, width, width), F32)] + [pltpu.VMEM(stats, F32)] * 3
    else:
        weights = weights[:5]
        carried = carried[:3]
        extra_specs = [hbm] * 5 + [vmem] * 3
        extra = (
            [jax.ShapeDtypeStruct((HEADS, slots, slots), BF)]
            + [jax.ShapeDtypeStruct(across, BF)] * 3
            + [jax.ShapeDtypeStruct(along, BF)]
            + [jax.ShapeDtypeStruct(stats, F32)] * 3
        )
        last = []
    carried_specs = [hbm, hbm, vmem, hbm, vmem][: len(carried)]
    scratch = [along] * 3 + [across] * 3 + [square] * 5 + [across] * 4 + [along] * 6
    return pl.pallas_call(
        functools.partial(cell_kernel, cell, first, whole),
        in_specs=[smem, smem] + [hbm] * (6 + len(weights)) + [vmem] * 8 + carried_specs,
        out_specs=[hbm, hbm, vmem] + extra_specs,
        out_shape=[
            jax.ShapeDtypeStruct((cells, slots, width), BF),
            matrices,
            jax.ShapeDtypeStruct((8, 8, width), F32),
        ]
        + extra,
        scratch_shapes=[pltpu.VMEM(shape, BF) for shape in scratch]
        + [
            pltpu.VMEM((3, width, width), F32),
            pltpu.VMEM((HEADS if whole else 2, slots, slots), BF),
            pltpu.VMEM(square, BF),
            pltpu.VMEM(square, BF),
            pltpu.VMEM((width, STEP), F32),
        ]
        + last
        + [
            pltpu.SemaphoreType.DMA((14,)),
            pltpu.SemaphoreType.DMA((6,)),
            pltpu.SemaphoreType.DMA((2,)),
        ],
        input_output_aliases={} if first else {16 + len(weights): 0},
        compiler_params=params(),
        name="cell_whole" if whole else "cell_forward",
    )(info, own_norm, x, far, cot, qt, skt, svt, *weights, *vectors, *carried)


class Places:
    def __init__(self):
        cells = lax.axis_size("cells")
        self.half, self.cell = lax.axis_index("half"), lax.axis_index("cells")
        bits = [lax.rem(lax.div(self.cell, 2**power), 2) for power in range(cells.bit_length() - 1)]
        self.bits = [bits[0], self.half] + bits[1:]
        self.spans = [1, 0] + [2**power for power in range(1, len(bits))]

    def partner(self, flips):
        cell = self.cell
        for dim in flips:
            cell = cell + (1 - 2 * self.bits[dim]) * self.spans[dim]
        return {"half": 1 - self.half if 1 in flips else self.half, "cells": cell}

    def member(self, group, flips=()):
        index = 0
        for dim in group:
            index = 2 * index + (1 - self.bits[dim] if dim in flips else self.bits[dim])
        return index

    def send(self, flips, source, target, sent, arrived):
        copy = pltpu.make_async_remote_copy(
            src_ref=source,
            dst_ref=target,
            send_sem=sent,
            recv_sem=arrived,
            device_id=self.partner(flips),
            device_id_type=pl.DeviceIdType.MESH,
        )
        copy.start()
        return copy


def dims_of():
    return 1 + lax.axis_size("cells").bit_length() - 1


def groups_of(dims):
    rest = list(range(2, dims)) + [1]
    return [[0]] + [rest[start : start + 2] for start in range(0, len(rest), 2)]


def flips_of(group):
    return [tuple(group)] if len(group) == 1 else [(group[1],), (group[0],), tuple(group)]


def plan_of(order, rows):
    plan, base = [], 0
    for group in order:
        split = rows % (16 * 2 ** len(group)) == 0
        rows = rows // 2 ** len(group) if split else rows
        plan.append((group, rows, split, base))
        base += rows * len(flips_of(group))
    return plan, base


def room_for(rows, dims):
    return plan_of(groups_of(dims), rows)[1]


def total_of(own, came):
    return own + came[0] if len(came) == 1 else (own + came[0]) + (came[1] + came[2])


def summed_over_devices(places, mats, out, sent, got, semaphores):
    send_sem, recv_sem, back_send, back_recv = semaphores
    count, rows = mats.shape[0], mats.shape[1]
    plans = [plan_of(order, rows)[0] for order in [groups_of(len(places.bits))] * count]
    steps = len(plans[0])
    at_row = [jnp.int32(0)] * count
    started = [()] * count

    def at(place, length):
        return pl.ds(pl.multiple_of(place, 16), length)

    def finish(i, step):
        group, length, split, base = plans[i][step]
        wait(*started[i])
        here = at(at_row[i], length)
        kept = mats[i, here] if split else sent[i, base : base + length].astype(F32)
        came = [
            got[i, base + k * length : base + (k + 1) * length].astype(F32) for k in range(len(flips_of(group)))
        ]
        mats[i, here] = total_of(kept, came)

    for step in range(steps):
        for i in range(count):
            if step > 0:
                finish(i, step - 1)
            group, length, split, base = plans[i][step]
            copies = []
            if not split:
                sent[i, base : base + length] = mats[i, at(at_row[i], length)].astype(BF)
            for k, flips in enumerate(flips_of(group)):
                part = pl.ds(base + k * length, length)
                if split:
                    away = at_row[i] + places.member(group, flips) * length
                    sent[i, part] = mats[i, at(away, length)].astype(BF)
                source = part if split else pl.ds(base, length)
                copies.append(
                    places.send(
                        flips, sent.at[i, source], got.at[i, part], send_sem.at[i, step, k], recv_sem.at[i, step, k]
                    )
                )
            started[i] = copies
            if split:
                at_row[i] = at_row[i] + places.member(group) * length
        yield step
    for i in range(count):
        finish(i, steps - 1)
        here = at(at_row[i], plans[i][-1][1])
        out[i, here] = mats[i, here].astype(BF)
        started[i] = ()
    remaining = [[step for step in reversed(range(steps)) if plan[step][2]] for plan in plans]
    while any(remaining):
        for i in range(count):
            if not remaining[i]:
                continue
            step = remaining[i].pop(0)
            group, length, _, _ = plans[i][step]
            wait(*started[i])
            part = at(at_row[i], length)
            started[i] = [
                places.send(
                    flips, out.at[i, part], out.at[i, part], back_send.at[i, step, k], back_recv.at[i, step, k]
                )
                for k, flips in enumerate(flips_of(group))
            ]
            at_row[i] = at_row[i] - places.member(group) * length
        yield 0
    for i in range(count):
        wait(*started[i])


def vectors_over_devices(places, vec, out, sent, got, send_sem, recv_sem):
    for step, group in enumerate(groups_of(len(places.bits))):
        sent[step] = vec
        copies = [
            places.send(flips, sent.at[step], got.at[step, k], send_sem.at[step, k], recv_sem.at[step, k])
            for k, flips in enumerate(flips_of(group))
        ]
        yield step
        wait(*copies)
        vec = total_of(vec, [got[step, k] for k in range(len(copies))])
    out[...] = vec


def backward_kernel(cells, *refs):
    take = taker(refs)
    mats_hbm, x_hbm, qt_hbm, skt_hbm, svt_hbm, wq_hbm, wk_hbm, wv_hbm, dense_vecs = take(9)
    far_hbm, pt_hbm, kt_hbm, vt_hbm, dot_hbm, gres_hbm, inverse, self_exp, delta = (
        take(cells) for _ in range(9)
    )
    grad_hbm, dense_out, back_out, vecs_out = take(4)
    x, far, far_grad, grad, qt, skt, svt, kt, vt, dot_t, dq, pt = take(12)
    wq, wk, wv, wqt, wkt, wvt, dense_mats, back_mats, vecs = take(9)
    dense_bufs, low_bufs, high_bufs, vec_bufs = take(2), take(2), take(2), take(2)
    dense_sems, low_sems, high_sems, vec_sems = take(4), take(4), take(4), take(2)
    in_sem, out_sem, pt_sem, far_send, far_recv = take(5)

    _, slots, width = x.shape
    head_dim = width // HEADS
    halfway = slots // 2
    half_at = lax.axis_index("half")
    is_known = half_at == 0

    places = Places()
    barrier = pltpu.get_barrier_semaphore()
    neighbours = [flips for group in groups_of(len(places.bits)) for flips in flips_of(group)]
    if (1,) not in neighbours:
        neighbours.append((1,))
    for flips in neighbours:
        pl.semaphore_signal(
            barrier, inc=1, device_id=places.partner(flips), device_id_type=pl.DeviceIdType.MESH
        )

    steps = cells * 2 * HEADS
    slots_kept = pt.shape[0]

    def bring(n, begin):
        head, slot = lax.rem(n, HEADS), lax.rem(n, slots_kept)
        part = pl.ds(pl.multiple_of(lax.rem(lax.div(n, HEADS), 2) * halfway, halfway), halfway)
        for cell in range(cells):

            @pl.when(lax.div(n, 2 * HEADS) == cell)
            def _():
                copy = pltpu.make_async_copy(
                    pt_hbm[cell].at[head, part], pt.at[slot], pt_sem.at[slot]
                )
                if begin:
                    copy.start()
                else:
                    copy.wait()

    for n in range(slots_kept - 1):
        bring(jnp.int32(n), True)
    urgent = fetch(
        [
            (vt_hbm[0], vt.at[0]),
            (dot_hbm[0], dot_t.at[0]),
            (kt_hbm[0], kt.at[0]),
            (qt_hbm.at[0], qt.at[0]),
        ],
        in_sem,
    )
    wait(*urgent)
    pairs = [(mats_hbm, dense_mats), (skt_hbm.at[0], skt.at[0]), (svt_hbm.at[0], svt.at[0])]
    pairs += [(wk_hbm, wk), (wv_hbm, wv), (wq_hbm, wq)]
    for cell in range(1, cells):
        pairs += [
            (vt_hbm[cell], vt.at[cell]),
            (dot_hbm[cell], dot_t.at[cell]),
            (kt_hbm[cell], kt.at[cell]),
            (qt_hbm.at[cell], qt.at[cell]),
            (skt_hbm.at[cell], skt.at[cell]),
            (svt_hbm.at[cell], svt.at[cell]),
        ]
    pairs.append((x_hbm, x))
    pairs += [(gres_hbm[cell], grad.at[cell]) for cell in range(cells)]
    loads = fetch(pairs, in_sem.at[pl.ds(4, len(pairs))])

    def far_loads():
        return [
            pltpu.make_async_copy(far_hbm[cell], far.at[cell], in_sem.at[4 + len(pairs) + cell])
            for cell in range(cells)
        ]

    @pl.when(jnp.logical_not(is_known))
    def _():
        for copy in far_loads():
            copy.start()

    pl.semaphore_wait(barrier, len(neighbours))
    dense_sum = summed_over_devices(places, dense_mats, dense_out, *dense_bufs, dense_sems)
    low_sum = summed_over_devices(places, back_mats.at[0], back_out.at[0], *low_bufs, low_sems)
    high_sum = summed_over_devices(places, back_mats.at[1], back_out.at[1], *high_bufs, high_sems)

    def attend(cell, half, n):
        head, slot = lax.rem(n, HEADS), lax.rem(n, slots_kept)
        band = pl.ds(pl.multiple_of(head * head_dim, head_dim), head_dim)
        row = pl.ds(head, 1)
        q = qt[cell, band]
        inv = inverse[cell][row]
        grads = dot_t[cell, band].astype(F32)
        scaled = (grads * inv).astype(BF)
        inner = delta[cell][row]
        inner_scaled = inner * inv
        high = inner_scaled.astype(BF)
        rest = (inner_scaled - high.astype(F32)).astype(BF)
        wide = jnp.concatenate(
            [scaled, jnp.broadcast_to(high, (8, slots)), jnp.broadcast_to(rest, (8, slots))], axis=0
        )
        signs = jnp.where(lax.broadcasted_iota(jnp.int32, (16, STEP), 0) % 8 == 0, -1.0, 0.0).astype(BF)
        total = dq[band] if half == 1 else 0.0
        for start in range(0, halfway, STEP):
            part = slice(half * halfway + start, half * halfway + start + STEP)
            weights = pt[slot, start : start + STEP]
            grad_probs = tn(jnp.concatenate([vt[cell, band, part], signs], axis=0), wide)
            grad_scores = (weights.astype(F32) * grad_probs).astype(BF)
            keys = kt[cell, band, part]
            vt[cell, band, part] = nt(scaled, weights).astype(BF)
            kt[cell, band, part] = (nt(q, grad_scores) * (1.0 / LOG2E)).astype(BF)
            total = total + nn(keys, grad_scores)
        if half == 0:
            dq[band] = total
            return
        prob = self_exp[cell][row] * inv
        own_keys = jnp.where(is_known, 0.0, skt[cell, band].astype(F32))
        own_values = jnp.where(is_known, 0.0, svt[cell, band].astype(F32))
        grad_prob = jnp.sum(grads * own_values, axis=0, keepdims=True)
        grad_score = prob * (grad_prob - inner)
        qt[cell, band] = ((total + grad_score * own_keys) * head_dim**-0.5).astype(BF)
        skt[cell, band] = (q.astype(F32) * (grad_score * (1.0 / LOG2E))).astype(BF)
        svt[cell, band] = (grads * prob).astype(BF)

    def far_copy(cell, half):
        part = pl.ds(half * halfway, halfway)
        return pltpu.make_async_remote_copy(
            src_ref=far_grad.at[cell, part],
            dst_ref=far.at[cell, part],
            send_sem=far_send.at[cell, half],
            recv_sem=far_recv.at[cell, half],
            device_id=places.partner((1,)),
            device_id_type=pl.DeviceIdType.MESH,
        )

    def send_far(cell, half):
        @pl.when(jnp.logical_not(is_known))
        def _():
            for start in range(half * halfway, (half + 1) * halfway, STEP):
                part = slice(start, start + STEP)
                total = tn(kt[cell, :, part], wkt[...]) + tn(vt[cell, :, part], wvt[...])
                far_grad[cell, part] = total.astype(BF)
            far_copy(cell, half).start()

    def weight_sums(cell, level):
        band = slice(level * width // 2, (level + 1) * width // 2)
        grad_k = jnp.where(is_known, kt[cell, band], skt[cell, band])
        grad_v = jnp.where(is_known, vt[cell, band], svt[cell, band])
        for i, part in enumerate((qt[cell, band], grad_k, grad_v)):
            value = nn(part, x[cell])
            back_mats[level, i] = value if cell == 0 else back_mats[level, i] + value

        @pl.when(jnp.logical_not(is_known))
        def _():
            back_mats[level, 1] += nn(kt[cell, band], far[cell])
            back_mats[level, 2] += nn(vt[cell, band], far[cell])

    def bias_sums(cell):
        ones = jnp.ones((8, slots), BF)
        grad_v = jnp.where(is_known, vt[cell], svt[cell])
        vecs[8:9] += nt(ones, qt[cell])[:1]
        vecs[9:10] += nt(ones, grad_v)[:1]

        @pl.when(jnp.logical_not(is_known))
        def _():
            vecs[9:10] += nt(ones, vt[cell])[:1]

    def own_rows(cell, start):
        part = slice(start, start + STEP)
        grad_k = jnp.where(is_known, kt[cell, :, part], skt[cell, :, part])
        grad_v = jnp.where(is_known, vt[cell, :, part], svt[cell, :, part])
        total = grad[cell, part].astype(F32) + tn(qt[cell, :, part], wqt[...])
        total = total + tn(grad_k, wkt[...]) + tn(grad_v, wvt[...])
        grad[cell, part] = total.astype(BF)

    group = 2
    per_pass = HEADS // group
    for index in range(steps // group):
        cell, half, turn = index // (2 * per_pass), (index // per_pass) % 2, index % per_pass

        def one(i, carry):
            n = index * group + i

            @pl.when(n + slots_kept - 1 < steps)
            def _():
                bring(n + slots_kept - 1, True)

            bring(n, False)
            attend(cell, half, n)
            return carry

        lax.fori_loop(0, group, one, 0)
        if index == 0:
            wait(loads[0])
        if index in DENSE_TURNS:
            next(dense_sum, None)
        if index == 0:
            vecs[:8] = jnp.sum(dense_vecs[...], axis=1)
            vecs[8:] = jnp.zeros((8, width), F32)
            wait(*loads[1:])

            @pl.when(jnp.logical_not(is_known))
            def _():
                wait(*far_loads())

            wqt[...] = wq[...].T
            wkt[...] = wk[...].T
            wvt[...] = wv[...].T
        if turn == per_pass - 1:
            send_far(cell, half)
        if half == 1 and turn == per_pass // 2 - 1:
            weight_sums(cell, 0)
            if cell == cells - 1:
                next(low_sum)
        elif cell == cells - 1 and half == 1 and turn == per_pass - 1:
            next(low_sum)
        if half == 1 and turn == per_pass - 1:
            weight_sums(cell, 1)
            bias_sums(cell)
    vec_sum = vectors_over_devices(places, vecs[...], vecs_out, *vec_bufs, *vec_sems)
    running = [high_sum, vec_sum, low_sum, dense_sum]
    for chain in running[:2]:
        next(chain)
    for start in range(0, slots, STEP):
        for cell in range(cells):
            own_rows(cell, start)
        running = [chain for chain in running if next(chain, None) is not None]
    while running:
        running = [chain for chain in running if next(chain, None) is not None]
    out_copies = []
    for cell in range(cells):
        for half in range(2):

            @pl.when(is_known)
            def _():
                far_copy(cell, half).wait_recv()
                part = pl.ds(half * halfway, halfway)
                grad[cell, part] = (grad[cell, part].astype(F32) + far[cell, part].astype(F32)).astype(BF)

        out_copies += fetch([(grad.at[cell], grad_hbm.at[cell])], out_sem.at[pl.ds(cell, 1)])

    @pl.when(jnp.logical_not(is_known))
    def _():
        for cell in range(cells):
            for half in range(2):
                far_copy(cell, half).wait_send()

    wait(*out_copies)


def backward(mats, x, qt, skt, svt, weights, dense_vecs, fars, kept):
    cells, slots, width = x.shape
    dims = dims_of()
    turns = len(groups_of(dims))
    vmem = pl.BlockSpec(memory_space=pltpu.VMEM)
    hbm = pl.BlockSpec(memory_space=pl.ANY)
    across, along = (cells, width, slots), (cells, slots, width)
    square = (width, width)
    whole, part = room_for(width, dims), room_for(width // 2, dims)
    sums = pltpu.SemaphoreType.DMA((3, turns, 3))
    loads = 6 * cells + 5 + 2 * cells
    return pl.pallas_call(
        functools.partial(backward_kernel, cells),
        in_specs=[hbm] * 8 + [vmem] + [hbm] * (6 * cells) + [vmem] * (3 * cells),
        out_specs=[hbm] + [vmem] * 3,
        out_shape=[
            jax.ShapeDtypeStruct((cells, slots, width), BF),
            jax.ShapeDtypeStruct((3, width, width), BF),
            jax.ShapeDtypeStruct((2, 3, width // 2, width), BF),
            jax.ShapeDtypeStruct((16, width), F32),
        ],
        scratch_shapes=[pltpu.VMEM(along, BF)] * 4
        + [pltpu.VMEM(across, BF)] * 6
        + [pltpu.VMEM((width, slots), F32), pltpu.VMEM((3, slots // 2, slots), BF)]
        + [pltpu.VMEM(square, BF)] * 6
        + [
            pltpu.VMEM((3, width, width), F32),
            pltpu.VMEM((2, 3, width // 2, width), F32),
            pltpu.VMEM((16, width), F32),
        ]
        + [pltpu.VMEM((3, whole, width), BF)] * 2
        + [pltpu.VMEM((3, part, width), BF)] * 4
        + [pltpu.VMEM((turns, 16, width), F32), pltpu.VMEM((turns, 3, 16, width), F32)]
        + [sums] * 12
        + [pltpu.SemaphoreType.DMA((turns, 3))] * 2
        + [
            pltpu.SemaphoreType.DMA((loads,)),
            pltpu.SemaphoreType.DMA((cells,)),
            pltpu.SemaphoreType.DMA((3,)),
            pltpu.SemaphoreType.DMA((cells, 2)),
            pltpu.SemaphoreType.DMA((cells, 2)),
        ],
        compiler_params=params(collective_id=0, has_side_effects=True),
        name="backward",
    )(mats, x, qt, skt, svt, *weights, dense_vecs, *fars, *(kept_of for column_of in zip(*kept) for kept_of in column_of))


def finish_kernel(grad, dense_mats, back_mats, vecs, *refs):
    grad_out, wq, bq, wk, wv, bv, wo, bo, g1, s1, wh, bh, wr, br, g2, s2 = refs[:16]
    kept, dense_in, back_in, results, in_sem, out_sem = refs[16:]
    cells = kept.shape[0]
    loads = fetch(
        [(back_mats, back_in), (dense_mats, dense_in)] + [(grad.at[c], kept.at[c]) for c in range(cells)], in_sem
    )
    wait(loads[0])
    copies = []
    for i, target in enumerate((wq, wk, wv, wo, wh, wr)):
        if i == 3:
            wait(loads[1])
        if i < 3:
            whole = jnp.concatenate([back_in[0, i], back_in[1, i]], axis=0).astype(F32).T
        else:
            whole = dense_in[i - 3].astype(F32)
        results[i] = whole
        copies += fetch([(results.at[i], target)], out_sem.at[pl.ds(i, 1)])
    for c in range(cells):
        wait(loads[2 + c])
        copies += fetch([(kept.at[c], grad_out.at[c])], out_sem.at[pl.ds(6 + c, 1)])
    for i, target in enumerate((g2, s2, br, bh, g1, s1, bo, None, bq, bv)):
        if target is not None:
            target[...] = vecs[i]
    wait(*copies)


def finish(grad, dense_mats, back_mats, vecs):
    cells = grad.shape[0]
    width = vecs.shape[1]
    vmem = pl.BlockSpec(memory_space=pltpu.VMEM)
    hbm = pl.BlockSpec(memory_space=pl.ANY)
    matrix = jax.ShapeDtypeStruct((width, width), F32)
    vector = jax.ShapeDtypeStruct((width,), F32)
    shapes = [matrix, vector, matrix, matrix, vector, matrix, vector, vector, vector]
    shapes += [matrix, vector, matrix, vector, vector, vector]
    return pl.pallas_call(
        finish_kernel,
        in_specs=[hbm, hbm, hbm, vmem],
        out_specs=[hbm] + [hbm if shape is matrix else vmem for shape in shapes],
        out_shape=[jax.ShapeDtypeStruct(grad.shape, BF)] + shapes,
        scratch_shapes=[
            pltpu.VMEM(grad.shape, BF),
            pltpu.VMEM(dense_mats.shape, BF),
            pltpu.VMEM(back_mats.shape, BF),
            pltpu.VMEM((6, width, width), F32),
            pltpu.SemaphoreType.DMA((2 + cells,)),
            pltpu.SemaphoreType.DMA((6 + cells,)),
        ],
        compiler_params=params(),
        name="finish",
    )(grad, dense_mats, back_mats, vecs)


def passed_along(value, axis, by):
    count = lax.axis_size(axis)
    pairs = [(i, i + by) for i in range(count) if 0 <= i + by < count]
    return lax.ppermute(value, axis, pairs)


def local(
    tokens,
    known_len,
    unknown_len,
    query_weight,
    query_bias,
    key_weight,
    value_weight,
    value_bias,
    output_weight,
    output_bias,
    first_gain,
    first_shift,
    hidden_weight,
    hidden_bias,
    return_weight,
    return_bias,
    second_gain,
    second_shift,
    cotangent,
):
    _, cells, slots, width = tokens.shape
    is_known = lax.axis_index("half") == 0
    x = tokens.reshape(cells, slots, width)
    cot = cotangent.reshape(cells, slots, width)
    own_len = jnp.where(is_known, known_len, unknown_len)
    info = jnp.concatenate([is_known.astype(jnp.int32)[None], known_len, own_len])

    def row(vector):
        return vector.reshape(1, width)

    qt, skt, svt, last_tokens, own_norm, far = project_own(
        x, query_weight, row(query_bias), key_weight, value_weight, row(value_bias)
    )
    fars = [far] + [
        passed_along(last_tokens if c == cells - 1 else x[c], "half", 1) for c in range(1, cells)
    ]
    weights = (key_weight, value_weight, output_weight, hidden_weight, return_weight, query_weight)
    vectors = [
        row(vector)
        for vector in (
            value_bias,
            output_bias,
            first_gain,
            first_shift,
            hidden_bias,
            return_bias,
            second_gain,
            second_shift,
        )
    ]
    carried = ()
    kept = []
    for c in range(cells):
        layer_out, sums, vecs, pt, kt, vt, dot_t, gres, *stats = run_cell(
            info, c, False, own_norm, x, fars[c], cot, qt, skt, svt, weights, vectors, carried
        )
        carried = (layer_out, sums, vecs)
        kept.append((pt, kt, vt, dot_t, gres, *stats))
    weights = (query_weight, key_weight, value_weight)
    grad, *sums = backward(sums, x, qt, skt, svt, weights, vecs, fars, kept)
    grad, *summed = finish(grad, *sums)
    out_shape = (1, cells, slots, width)
    return (layer_out.reshape(out_shape), grad.reshape(out_shape), *summed)


def solution(mesh):
    placed = (
        (P("half", "cells", None, None), P("cells"), P("cells"))
        + (P(),) * 15
        + (P("half", "cells", None, None),)
    )
    return jax.shard_map(
        local,
        mesh=mesh,
        in_specs=placed,
        out_specs=(P("half", "cells", None, None),) * 2 + (P(),) * 15,
        check_vma=False,
    )
```

```python
import functools

import jax
import jax.numpy as jnp
from jax import lax
from jax.experimental import pallas as pl
from jax.experimental.pallas import tpu as pltpu
from jax.sharding import PartitionSpec as P

HEADS = 8
EPS = 1e-05
NEGATIVE = -1e30
LOG2E = 1.4426950408889634
BF = jnp.bfloat16
F32 = jnp.float32
SAFE = 60.0
DENSE_TURNS = (0, 2, 7, 9, 11)
PIECES = ((0, 8),)
VMEM_LIMIT = 58 * 2**20
STEP = 256


def nn(a, b):
    return lax.dot_general(a, b, (((1,), (0,)), ((), ())), preferred_element_type=F32)


def nt(a, b):
    return lax.dot_general(a, b, (((1,), (1,)), ((), ())), preferred_element_type=F32)


def tn(a, b):
    return lax.dot_general(a, b, (((0,), (0,)), ((), ())), preferred_element_type=F32)


def cells_of(info):
    return (info.shape[0] - 1) // 2


def params(**more):
    return pltpu.CompilerParams(vmem_limit_bytes=VMEM_LIMIT, **more)


def column(vector, lanes):
    n = vector.shape[1]
    tile = jnp.broadcast_to(vector, (128, n)).T
    return jnp.concatenate([tile] * (lanes // 128), axis=1)


def head_norms(array, head_dim):
    width, tokens = array.shape
    squares = (array * array).reshape(width // head_dim, head_dim, tokens)
    return jnp.max(jnp.sum(squares, axis=1))


def own_kernel(head_dim, x_hbm, x, wq, bq, wk, wv, bv, qt, kt, vt, again, norm, far, *scratch):
    wqt, wkt, wvt, bqc, bvc, sent, arrived = scratch
    cell, block = pl.program_id(0), pl.program_id(1)
    rows = x.shape[1]
    half_at = lax.axis_index("half")
    is_known = half_at == 0
    other = {"half": 1 - half_at, "cells": lax.axis_index("cells")}
    copy = pltpu.make_async_remote_copy(
        src_ref=x_hbm.at[0],
        dst_ref=far,
        send_sem=sent,
        recv_sem=arrived,
        device_id=other,
        device_id_type=pl.DeviceIdType.MESH,
    )

    @pl.when((cell == 0) & (block == 0))
    def _():
        barrier = pltpu.get_barrier_semaphore()
        pl.semaphore_signal(barrier, inc=1, device_id=other, device_id_type=pl.DeviceIdType.MESH)
        pl.semaphore_wait(barrier, 1)

        @pl.when(is_known)
        def _():
            copy.start()

        wqt[...] = wq[...].T
        wkt[...] = wk[...].T
        wvt[...] = wv[...].T
        bqc[...] = column(bq[...], rows)
        bvc[...] = column(bv[...], rows)

    @pl.when(block == 0)
    def _():
        norm[0, cell] = 0.0
        norm[1, cell] = 0.0

    again[...] = x[0]
    queries = (nt(wqt[...], x[0]) + bqc[...]) * (LOG2E * head_dim**-0.5)
    qt[0] = queries.astype(BF)
    norm[0, cell] = jnp.maximum(norm[0, cell], head_norms(queries, head_dim))

    @pl.when(jnp.logical_not(is_known))
    def _():
        keys = nt(wkt[...], x[0])
        kt[0] = keys.astype(BF)
        norm[1, cell] = jnp.maximum(norm[1, cell], head_norms(keys, head_dim))
        vt[0] = (nt(wvt[...], x[0]) + bvc[...]).astype(BF)

    @pl.when((cell == pl.num_programs(0) - 1) & (block == pl.num_programs(1) - 1))
    def _():
        @pl.when(is_known)
        def _():
            copy.wait_send()

        @pl.when(jnp.logical_not(is_known))
        def _():
            copy.wait_recv()


def project_own(x, wq, bq, wk, wv, bv, rows=512):
    cells, slots, width = x.shape
    head_dim = width // HEADS
    weight = pl.BlockSpec((width, width), lambda c, i: (0, 0))
    bias = pl.BlockSpec((1, width), lambda c, i: (0, 0))
    out = pl.BlockSpec((1, width, rows), lambda c, i: (c, 0, i))
    hbm = pl.BlockSpec(memory_space=pl.ANY)
    last = cells - 1
    return pl.pallas_call(
        functools.partial(own_kernel, head_dim),
        grid=(cells, slots // rows),
        in_specs=[
            hbm,
            pl.BlockSpec((1, rows, width), lambda c, i: (c, i, 0)),
            weight,
            bias,
            weight,
            weight,
            bias,
        ],
        out_specs=[
            out,
            out,
            out,
            pl.BlockSpec((rows, width), lambda c, i: (lax.div(c, last) * i, 0)),
            pl.BlockSpec(memory_space=pltpu.SMEM),
            hbm,
        ],
        out_shape=[jax.ShapeDtypeStruct((cells, width, slots), BF)] * 3
        + [
            jax.ShapeDtypeStruct((slots, width), BF),
            jax.ShapeDtypeStruct((2, cells), F32),
            jax.ShapeDtypeStruct((slots, width), BF),
        ],
        scratch_shapes=[pltpu.VMEM((width, width), BF)] * 3
        + [pltpu.VMEM((width, rows), F32)] * 2
        + [pltpu.SemaphoreType.DMA] * 2,
        compiler_params=params(collective_id=1, has_side_effects=True),
        name="project_own",
    )(x, x, wq, bq, wk, wv, bv)


def steps_in(length):
    return lax.div(length + STEP - 1, STEP)


def sized(count, steps, body):
    for n in range(1, count + 1):
        pl.when(steps == n)(functools.partial(body, n * STEP))


def sized_pair(count, key_steps, own_steps, body):
    for a in range(1, count + 1):
        for b in range(1, count + 1):
            pl.when((key_steps == a) & (own_steps == b))(functools.partial(body, a * STEP, b * STEP))


def in_turns(chains):
    waiting = [iter(chain) for chain in chains]
    running = []
    while waiting or running:
        if waiting:
            running.append(waiting.pop(0))
        running = [chain for chain in running if next(chain, None) is not None]


def fold_rows(values):
    rows, width = values.shape
    return jnp.sum(values.reshape(rows // 8, 8, width), axis=0)


def fetch(pairs, semaphores):
    copies = [
        pltpu.make_async_copy(source, target, semaphores.at[i]) for i, (source, target) in enumerate(pairs)
    ]
    for copy in copies:
        copy.start()
    return copies


def wait(*copies):
    for copy in copies:
        copy.wait()


def taker(refs):
    place = 0

    def take(count):
        nonlocal place
        place += count
        return refs[place - count : place]

    return take


def cell_kernel(cell, first, *refs):
    take = taker(refs)
    info, own_norm, x_hbm, far_hbm, cot_hbm, qt_hbm, skt_hbm, svt_hbm = take(8)
    wk_hbm, wv_hbm, wo_hbm, wh_hbm, wr_hbm = take(5)
    bv, bo, g1, s1, bh, br, g2, s2 = take(8)
    _, sums_before, vecs_before = (None, None, None) if first else take(3)
    out_hbm, sums_hbm, vecs, pt_hbm, kt_hbm, vt_hbm, dot_hbm, gres_hbm, inverse, self_exp, delta = take(11)
    x, source, cot, qt, skt, svt, wk, wv, wo, wh, wr = take(11)
    kt, vt, ot, dot_t, low1, act, gb, gpre, gres, out, sums, pt, wkt, wvt, bvc = take(15)
    in_sem, out_sem, block_sem, pt_sem = take(4)

    slots, width = x.shape
    head_dim = width // HEADS
    is_known = info[0] == 1
    cells = (info.shape[0] - 1) // 2
    key_len, own_len = info[1 + cell], info[1 + cells + cell]
    key_steps, own_steps = steps_in(key_len), steps_in(own_len)
    blocks = slots // STEP

    known_source = pltpu.make_async_copy(x_hbm.at[cell], source, in_sem.at[0])
    far_source = pltpu.make_async_copy(far_hbm, source, in_sem.at[0])
    own_keys = [
        pltpu.make_async_copy(skt_hbm.at[cell], skt, in_sem.at[1]),
        pltpu.make_async_copy(svt_hbm.at[cell], svt, in_sem.at[2]),
    ]

    @pl.when(is_known)
    def _():
        known_source.start()

    @pl.when(jnp.logical_not(is_known))
    def _():
        far_source.start()

    loads = fetch([(wk_hbm, wk), (wv_hbm, wv)], in_sem.at[pl.ds(3, 2)])

    @pl.when(is_known)
    def _():
        known_source.wait()

    @pl.when(jnp.logical_not(is_known))
    def _():
        far_source.wait()
        for copy in own_keys:
            copy.start()

    wait(*loads)
    loads = fetch(
        [(qt_hbm.at[cell], qt), (wo_hbm, wo), (x_hbm.at[cell], x), (wh_hbm, wh), (wr_hbm, wr), (cot_hbm.at[cell], cot)]
        + ([] if first else [(sums_before, sums)]),
        in_sem.at[pl.ds(5, 7)],
    )

    def block_copies(block):
        part = pl.ds(block * STEP if isinstance(block, int) else pl.multiple_of(block * STEP, STEP), STEP)
        return [
            pltpu.make_async_copy(out.at[part], out_hbm.at[cell, part], block_sem.at[0, block]),
            pltpu.make_async_copy(dot_t.at[:, part], dot_hbm.at[:, part], block_sem.at[1, block]),
            pltpu.make_async_copy(gres.at[part], gres_hbm.at[part], block_sem.at[2, block]),
        ]

    wkt[...] = wk[...].T
    wvt[...] = wv[...].T
    bvc[...] = column(bv[...], STEP)

    def project(block, largest):
        part = pl.ds(pl.multiple_of(block * STEP, STEP), STEP)
        tokens = source[part]
        keys = nt(wkt[...], tokens)
        kt[:, part] = keys.astype(BF)
        vt[:, part] = (nt(wvt[...], tokens) + bvc[...]).astype(BF)
        return jnp.maximum(largest, head_norms(keys, head_dim))

    def blank(targets, block, carry):
        part = pl.ds(pl.multiple_of(block * STEP, STEP), STEP)
        for target in targets:
            if target.shape[0] == slots:
                target[part] = jnp.zeros((STEP, width), BF)
            else:
                target[:, part] = jnp.zeros((target.shape[0], STEP), target.dtype)
        return carry

    largest = lax.fori_loop(0, key_steps, project, jnp.float32(0.0))
    lax.fori_loop(key_steps, blocks, functools.partial(blank, (kt, vt)), 0)

    out_copies = fetch([(kt, kt_hbm), (vt, vt_hbm)], out_sem)

    @pl.when((key_steps < blocks) | (own_steps < blocks))
    def _():
        pt[...] = jnp.zeros_like(pt)

    def blank_block(block, carry):
        blank((out, gres, dot_t, inverse, self_exp, delta), block, carry)
        for copy in block_copies(block):
            copy.start()
        return carry

    lax.fori_loop(own_steps, blocks, blank_block, 0)

    wait(loads[0])

    @pl.when(jnp.logical_not(is_known))
    def _():
        wait(*own_keys)

    largest = jnp.maximum(largest, own_norm[1, cell])
    safe = own_norm[0, cell] * largest < SAFE * SAFE

    def attend(head, slot, use_max, keys, queries):
        band = pl.ds(pl.multiple_of(head * head_dim, head_dim), head_dim)
        index = lax.broadcasted_iota(jnp.int32, (16, keys), 1)
        first_row = lax.broadcasted_iota(jnp.int32, (16, keys), 0) == 0
        masked = jnp.where(first_row & (index >= key_len), NEGATIVE, 0.0).astype(BF)
        key_part = jnp.concatenate([kt[band, :keys], masked], axis=0)
        q = qt[band, :queries]
        query_part = jnp.concatenate([q, jnp.ones((16, queries), BF)], axis=0)
        value_part = jnp.concatenate([vt[band, :keys], jnp.ones((16, keys), BF)], axis=0)
        scores = tn(key_part, query_part)
        own = jnp.sum(q.astype(F32) * skt[band, :queries].astype(F32), axis=0, keepdims=True)
        own = jnp.where(is_known, NEGATIVE, own)
        if use_max:
            top = jnp.maximum(jnp.max(scores, axis=0, keepdims=True), own)
            scores = scores - top
            own = own - top
        weights = jnp.exp2(scores).astype(BF)
        pt[slot, :keys, :queries] = weights
        own = jnp.exp2(own)
        total = nn(value_part, weights)
        inv = 1.0 / (total[head_dim : head_dim + 1] + own)
        own_values = jnp.where(is_known, 0.0, svt[band, :queries].astype(F32))
        ot[band, :queries] = ((total[:head_dim] + own * own_values) * inv).astype(BF)
        row = pl.ds(head, 1)
        inverse[row, :queries] = inv
        self_exp[row, :queries] = own

    def keep(head, slot):
        return pltpu.make_async_copy(pt.at[slot], pt_hbm.at[head], pt_sem.at[slot])

    def one_head(head, carry):
        slot = lax.rem(head, 2)

        @pl.when(head >= 2)
        def _():
            keep(head - 2, slot).wait()

        @pl.when(safe)
        def _():
            sized_pair(blocks, key_steps, own_steps, functools.partial(attend, head, slot, False))

        @pl.when(jnp.logical_not(safe))
        def _():
            attend(head, slot, True, slots, slots)

        keep(head, slot).start()
        return carry

    lax.fori_loop(0, HEADS, one_head, 0)

    wait(*loads[1:6])
    scale = 1.0 / width
    if first:
        vecs[...] = jnp.zeros_like(vecs)
    else:
        vecs[...] = vecs_before[...]

    def mean(values):
        return jnp.sum(values, axis=1, keepdims=True) * scale

    def chain(block):
        start = pl.multiple_of(block * STEP, STEP)
        part = pl.ds(start, STEP)
        slot_index = lax.broadcasted_iota(jnp.int32, (STEP, 1), 0) + start
        live = (slot_index < own_len).astype(F32)
        context = ot[:, part]
        r1 = tn(context, wo[...])
        yield 1
        r1 = r1 + x[part].astype(F32) + bo[...]
        centred = r1 - mean(r1)
        inv1 = lax.rsqrt(mean(centred * centred) + EPS)
        hat1 = centred * inv1
        norm1 = hat1 * g1[...] + s1[...]
        low = norm1.astype(BF)
        low1[part] = low
        yield 2
        pre = nn(low, wh[...])
        yield 3
        pre = pre + bh[...]
        cdf = 0.5 + 0.5 * lax.erf(pre * (0.5**0.5))
        active = (pre * cdf).astype(BF)
        act[part] = active
        slope = cdf + pre * (jnp.exp(-0.5 * pre * pre) * 0.3989422804014327)
        yield 4
        r2 = nn(active, wr[...])
        yield 5
        r2 = r2 + norm1 + br[...]
        centred = r2 - mean(r2)
        inv2 = lax.rsqrt(mean(centred * centred) + EPS)
        hat2 = centred * inv2
        out[part] = ((hat2 * g2[...] + s2[...]) * live).astype(BF)
        go = cot[part].astype(F32) * live
        vecs[0] += fold_rows(go * hat2)
        vecs[1] += fold_rows(go)
        gx = go * g2[...]
        gr2 = inv2 * (gx - mean(gx) - hat2 * mean(gx * hat2))
        grad_branch = gr2.astype(BF)
        gb[part] = grad_branch
        vecs[2] += fold_rows(grad_branch.astype(F32))
        yield 6
        grad_act = nt(grad_branch, wr[...])
        yield 7
        grad_pre = (grad_act * slope).astype(BF)
        gpre[part] = grad_pre
        vecs[3] += fold_rows(grad_pre.astype(F32))
        yield 8
        gn = nt(grad_pre, wh[...])
        yield 9
        gn = gr2 + gn
        vecs[4] += fold_rows(gn * hat1)
        vecs[5] += fold_rows(gn)
        gx = gn * g1[...]
        gr1 = inv1 * (gx - mean(gx) - hat1 * mean(gx * hat1))
        grad_attn = gr1.astype(BF)
        gres[part] = grad_attn
        vecs[6] += fold_rows(grad_attn.astype(F32))
        yield 10
        back = nt(wo[...], grad_attn)
        yield 11
        low_back = back.astype(BF)
        dot_t[:, part] = low_back
        product = low_back.astype(F32) * context.astype(F32)
        delta[:, part] = jnp.sum(product.reshape(HEADS, head_dim, STEP), axis=1)
        for copy in block_copies(block):
            copy.start()

    def pair(index, carry):
        in_turns([chain(2 * index), chain(2 * index + 1)])
        return carry

    lax.fori_loop(0, lax.div(own_steps, 2), pair, 0)

    @pl.when(lax.rem(own_steps, 2) == 1)
    def _():
        in_turns([chain(own_steps - 1)])

    if not first:
        wait(loads[6])

    def weight_sum(i, rows):
        if i == 0:
            value = nn(ot[:, :rows], gres[:rows])
        elif i == 1:
            value = tn(low1[:rows], gpre[:rows])
        else:
            value = tn(act[:rows], gb[:rows])
        sums[i] = value if first else sums[i] + value

    for i in range(3):
        sized(blocks, own_steps, functools.partial(weight_sum, i))
        out_copies += fetch([(sums.at[i], sums_hbm.at[i])], out_sem.at[pl.ds(2 + i, 1)])
    for slot in range(2):
        keep(HEADS - 2 + slot, slot).wait()
    for block in range(blocks):
        wait(*block_copies(block))
    wait(*out_copies)


def run_cell(info, cell, own_norm, x, far, cot, qt, skt, svt, weights, vectors, carried):
    cells, slots, width = x.shape
    smem = pl.BlockSpec(memory_space=pltpu.SMEM)
    vmem = pl.BlockSpec(memory_space=pltpu.VMEM)
    hbm = pl.BlockSpec(memory_space=pl.ANY)
    first = not carried
    across, along = (width, slots), (slots, width)
    square = (width, width)
    stats = (HEADS, slots)
    scratch = [along] * 3 + [across] * 3 + [square] * 5 + [across] * 4 + [along] * 6
    return pl.pallas_call(
        functools.partial(cell_kernel, cell, first),
        in_specs=[smem, smem] + [hbm] * 11 + [vmem] * 8 + ([] if first else [hbm, hbm, vmem]),
        out_specs=[hbm, hbm, vmem] + [hbm] * 5 + [vmem] * 3,
        out_shape=[
            jax.ShapeDtypeStruct((cells, slots, width), BF),
            jax.ShapeDtypeStruct((3, width, width), F32),
            jax.ShapeDtypeStruct((8, 8, width), F32),
            jax.ShapeDtypeStruct((HEADS, slots, slots), BF),
        ]
        + [jax.ShapeDtypeStruct(across, BF)] * 3
        + [jax.ShapeDtypeStruct(along, BF)]
        + [jax.ShapeDtypeStruct(stats, F32)] * 3,
        scratch_shapes=[pltpu.VMEM(shape, BF) for shape in scratch]
        + [
            pltpu.VMEM((3, width, width), F32),
            pltpu.VMEM((2, slots, slots), BF),
            pltpu.VMEM(square, BF),
            pltpu.VMEM(square, BF),
            pltpu.VMEM((width, STEP), F32),
            pltpu.SemaphoreType.DMA((12,)),
            pltpu.SemaphoreType.DMA((5,)),
            pltpu.SemaphoreType.DMA((3, slots // STEP)),
            pltpu.SemaphoreType.DMA((2,)),
        ],
        input_output_aliases={} if first else {21: 0},
        compiler_params=params(),
        name="cell_forward",
    )(info, own_norm, x, far, cot, qt, skt, svt, *weights, *vectors, *carried)


class Places:
    def __init__(self):
        cells = lax.axis_size("cells")
        self.half, self.cell = lax.axis_index("half"), lax.axis_index("cells")
        bits = [lax.rem(lax.div(self.cell, 2**power), 2) for power in range(cells.bit_length() - 1)]
        self.bits = [bits[0], self.half] + bits[1:]
        self.spans = [1, 0] + [2**power for power in range(1, len(bits))]

    def partner(self, flips):
        cell = self.cell
        for dim in flips:
            cell = cell + (1 - 2 * self.bits[dim]) * self.spans[dim]
        return {"half": 1 - self.half if 1 in flips else self.half, "cells": cell}

    def member(self, group, flips=()):
        index = 0
        for dim in group:
            index = 2 * index + (1 - self.bits[dim] if dim in flips else self.bits[dim])
        return index

    def send(self, flips, source, target, sent, arrived):
        copy = pltpu.make_async_remote_copy(
            src_ref=source,
            dst_ref=target,
            send_sem=sent,
            recv_sem=arrived,
            device_id=self.partner(flips),
            device_id_type=pl.DeviceIdType.MESH,
        )
        copy.start()
        return copy


def dims_of():
    return 1 + lax.axis_size("cells").bit_length() - 1


def groups_of(dims):
    rest = list(range(2, dims)) + [1]
    return [[0]] + [rest[start : start + 2] for start in range(0, len(rest), 2)]


def flips_of(group):
    return [tuple(group)] if len(group) == 1 else [(group[1],), (group[0],), tuple(group)]


def plan_of(order, rows):
    plan, base = [], 0
    for group in order:
        split = rows % (16 * 2 ** len(group)) == 0
        rows = rows // 2 ** len(group) if split else rows
        plan.append((group, rows, split, base))
        base += rows * len(flips_of(group))
    return plan, base


def room_for(rows, dims):
    return plan_of(groups_of(dims), rows)[1]


def total_of(own, came):
    return own + came[0] if len(came) == 1 else (own + came[0]) + (came[1] + came[2])


def summed_over_devices(places, mats, out, sent, got, semaphores):
    send_sem, recv_sem, back_send, back_recv = semaphores
    count, rows = mats.shape[0], mats.shape[1]
    plans = [plan_of(order, rows)[0] for order in [groups_of(len(places.bits))] * count]
    steps = len(plans[0])
    at_row = [jnp.int32(0)] * count
    started = [()] * count

    def at(place, length):
        return pl.ds(pl.multiple_of(place, 16), length)

    def finish(i, step):
        group, length, split, base = plans[i][step]
        wait(*started[i])
        here = at(at_row[i], length)
        kept = mats[i, here] if split else sent[i, base : base + length].astype(F32)
        came = [
            got[i, base + k * length : base + (k + 1) * length].astype(F32) for k in range(len(flips_of(group)))
        ]
        mats[i, here] = total_of(kept, came)

    for step in range(steps):
        for i in range(count):
            if step > 0:
                finish(i, step - 1)
            group, length, split, base = plans[i][step]
            copies = []
            if not split:
                sent[i, base : base + length] = mats[i, at(at_row[i], length)].astype(BF)
            for k, flips in enumerate(flips_of(group)):
                part = pl.ds(base + k * length, length)
                if split:
                    away = at_row[i] + places.member(group, flips) * length
                    sent[i, part] = mats[i, at(away, length)].astype(BF)
                source = part if split else pl.ds(base, length)
                copies.append(
                    places.send(
                        flips, sent.at[i, source], got.at[i, part], send_sem.at[i, step, k], recv_sem.at[i, step, k]
                    )
                )
            started[i] = copies
            if split:
                at_row[i] = at_row[i] + places.member(group) * length
        yield step
    for i in range(count):
        finish(i, steps - 1)
        here = at(at_row[i], plans[i][-1][1])
        out[i, here] = mats[i, here].astype(BF)
        started[i] = ()
    remaining = [[step for step in reversed(range(steps)) if plan[step][2]] for plan in plans]
    while any(remaining):
        for i in range(count):
            if not remaining[i]:
                continue
            step = remaining[i].pop(0)
            group, length, _, _ = plans[i][step]
            wait(*started[i])
            part = at(at_row[i], length)
            started[i] = [
                places.send(
                    flips, out.at[i, part], out.at[i, part], back_send.at[i, step, k], back_recv.at[i, step, k]
                )
                for k, flips in enumerate(flips_of(group))
            ]
            at_row[i] = at_row[i] - places.member(group) * length
        yield 0
    for i in range(count):
        wait(*started[i])


def vectors_over_devices(places, vec, out, sent, got, send_sem, recv_sem):
    for step, group in enumerate(groups_of(len(places.bits))):
        sent[step] = vec
        copies = [
            places.send(flips, sent.at[step], got.at[step, k], send_sem.at[step, k], recv_sem.at[step, k])
            for k, flips in enumerate(flips_of(group))
        ]
        yield step
        wait(*copies)
        vec = total_of(vec, [got[step, k] for k in range(len(copies))])
    out[...] = vec


def backward_kernel(cells, *refs):
    take = taker(refs)
    mats_hbm, x_hbm, qt_hbm, skt_hbm, svt_hbm, wq_hbm, wk_hbm, wv_hbm, dense_vecs = take(9)
    far_hbm, pt_hbm, kt_hbm, vt_hbm, dot_hbm, gres_hbm, inverse, self_exp, delta = (
        take(cells) for _ in range(9)
    )
    grad_hbm, dense_out, vecs_out = take(3)
    back_out = take(len(PIECES))
    x, far, far_grad, grad, qt, skt, svt, kt, vt, dot_t, dq, pt = take(12)
    wq, wk, wv, wqt, wkt, wvt, dense_mats, vecs = take(8)
    back_mats = take(len(PIECES))
    dense_bufs, vec_bufs, dense_sems, vec_sems = take(2), take(2), take(4), take(2)
    back_bufs = [take(2) for _ in PIECES]
    back_sems = [take(4) for _ in PIECES]
    in_sem, out_sem, pt_sem, far_send, far_recv = take(5)

    _, slots, width = x.shape
    head_dim = width // HEADS
    halfway = slots // 2
    half_at = lax.axis_index("half")
    is_known = half_at == 0

    places = Places()
    barrier = pltpu.get_barrier_semaphore()
    neighbours = [flips for group in groups_of(len(places.bits)) for flips in flips_of(group)]
    if (1,) not in neighbours:
        neighbours.append((1,))
    for flips in neighbours:
        pl.semaphore_signal(
            barrier, inc=1, device_id=places.partner(flips), device_id_type=pl.DeviceIdType.MESH
        )

    steps = cells * 2 * HEADS
    slots_kept = pt.shape[0]

    def bring(n, begin):
        head, slot = lax.rem(n, HEADS), lax.rem(n, slots_kept)
        part = pl.ds(pl.multiple_of(lax.rem(lax.div(n, HEADS), 2) * halfway, halfway), halfway)
        for cell in range(cells):

            @pl.when(lax.div(n, 2 * HEADS) == cell)
            def _():
                copy = pltpu.make_async_copy(
                    pt_hbm[cell].at[head, part], pt.at[slot], pt_sem.at[slot]
                )
                if begin:
                    copy.start()
                else:
                    copy.wait()

    for n in range(slots_kept - 1):
        bring(jnp.int32(n), True)
    urgent = fetch(
        [
            (vt_hbm[0], vt.at[0]),
            (dot_hbm[0], dot_t.at[0]),
            (kt_hbm[0], kt.at[0]),
            (qt_hbm.at[0], qt.at[0]),
        ],
        in_sem,
    )
    wait(*urgent)
    pairs = [(mats_hbm, dense_mats), (skt_hbm.at[0], skt.at[0]), (svt_hbm.at[0], svt.at[0])]
    pairs += [(wk_hbm, wk), (wv_hbm, wv), (wq_hbm, wq)]
    for cell in range(1, cells):
        pairs += [
            (vt_hbm[cell], vt.at[cell]),
            (dot_hbm[cell], dot_t.at[cell]),
            (kt_hbm[cell], kt.at[cell]),
            (qt_hbm.at[cell], qt.at[cell]),
            (skt_hbm.at[cell], skt.at[cell]),
            (svt_hbm.at[cell], svt.at[cell]),
        ]
    pairs.append((x_hbm, x))
    pairs += [(gres_hbm[cell], grad.at[cell]) for cell in range(cells)]
    loads = fetch(pairs, in_sem.at[pl.ds(4, len(pairs))])

    def far_loads():
        return [
            pltpu.make_async_copy(far_hbm[cell], far.at[cell], in_sem.at[4 + len(pairs) + cell])
            for cell in range(cells)
        ]

    @pl.when(jnp.logical_not(is_known))
    def _():
        for copy in far_loads():
            copy.start()

    pl.semaphore_wait(barrier, len(neighbours))
    dense_sum = summed_over_devices(places, dense_mats, dense_out, *dense_bufs, dense_sems)
    back_sums = [
        summed_over_devices(places, back_mats[i], back_out[i], *back_bufs[i], back_sems[i])
        for i in range(len(PIECES))
    ]

    def attend(cell, half, n):
        head, slot = lax.rem(n, HEADS), lax.rem(n, slots_kept)
        band = pl.ds(pl.multiple_of(head * head_dim, head_dim), head_dim)
        row = pl.ds(head, 1)
        q = qt[cell, band]
        inv = inverse[cell][row]
        grads = dot_t[cell, band].astype(F32)
        scaled = (grads * inv).astype(BF)
        inner = delta[cell][row]
        inner_scaled = inner * inv
        high = inner_scaled.astype(BF)
        rest = (inner_scaled - high.astype(F32)).astype(BF)
        wide = jnp.concatenate(
            [scaled, jnp.broadcast_to(high, (8, slots)), jnp.broadcast_to(rest, (8, slots))], axis=0
        )
        signs = jnp.where(lax.broadcasted_iota(jnp.int32, (16, STEP), 0) % 8 == 0, -1.0, 0.0).astype(BF)
        total = dq[band] if half == 1 else 0.0
        for start in range(0, halfway, STEP):
            part = slice(half * halfway + start, half * halfway + start + STEP)
            weights = pt[slot, start : start + STEP]
            grad_probs = tn(jnp.concatenate([vt[cell, band, part], signs], axis=0), wide)
            grad_scores = (weights.astype(F32) * grad_probs).astype(BF)
            keys = kt[cell, band, part]
            vt[cell, band, part] = nt(scaled, weights).astype(BF)
            kt[cell, band, part] = (nt(q, grad_scores) * (1.0 / LOG2E)).astype(BF)
            total = total + nn(keys, grad_scores)
        if half == 0:
            dq[band] = total
            return
        prob = self_exp[cell][row] * inv
        own_keys = jnp.where(is_known, 0.0, skt[cell, band].astype(F32))
        own_values = jnp.where(is_known, 0.0, svt[cell, band].astype(F32))
        grad_prob = jnp.sum(grads * own_values, axis=0, keepdims=True)
        grad_score = prob * (grad_prob - inner)
        qt[cell, band] = ((total + grad_score * own_keys) * head_dim**-0.5).astype(BF)
        skt[cell, band] = (q.astype(F32) * (grad_score * (1.0 / LOG2E))).astype(BF)
        svt[cell, band] = (grads * prob).astype(BF)

    def far_copy(cell, half):
        part = pl.ds(half * halfway, halfway)
        return pltpu.make_async_remote_copy(
            src_ref=far_grad.at[cell, part],
            dst_ref=far.at[cell, part],
            send_sem=far_send.at[cell, half],
            recv_sem=far_recv.at[cell, half],
            device_id=places.partner((1,)),
            device_id_type=pl.DeviceIdType.MESH,
        )

    def send_far(cell, half):
        @pl.when(jnp.logical_not(is_known))
        def _():
            for start in range(half * halfway, (half + 1) * halfway, STEP):
                part = slice(start, start + STEP)
                total = tn(kt[cell, :, part], wkt[...]) + tn(vt[cell, :, part], wvt[...])
                far_grad[cell, part] = total.astype(BF)
            far_copy(cell, half).start()

    def weight_sums(cell, pieces):
        begin = PIECES[pieces[0]][0] * head_dim
        band = slice(begin, (PIECES[pieces[-1]][0] + PIECES[pieces[-1]][1]) * head_dim)

        def add(i, value, anew):
            for piece in pieces:
                start = PIECES[piece][0] * head_dim - begin
                part = value[start : start + PIECES[piece][1] * head_dim]
                back_mats[piece][i] = part if anew else back_mats[piece][i] + part

        grad_k = jnp.where(is_known, kt[cell, band], skt[cell, band])
        grad_v = jnp.where(is_known, vt[cell, band], svt[cell, band])
        for i, part in enumerate((qt[cell, band], grad_k, grad_v)):
            add(i, nn(part, x[cell]), cell == 0)

        @pl.when(jnp.logical_not(is_known))
        def _():
            add(1, nn(kt[cell, band], far[cell]), False)
            add(2, nn(vt[cell, band], far[cell]), False)

    def bias_sums(cell):
        ones = jnp.ones((8, slots), BF)
        grad_v = jnp.where(is_known, vt[cell], svt[cell])
        vecs[8:9] += nt(ones, qt[cell])[:1]
        vecs[9:10] += nt(ones, grad_v)[:1]

        @pl.when(jnp.logical_not(is_known))
        def _():
            vecs[9:10] += nt(ones, vt[cell])[:1]

    def own_rows(cell, start):
        part = slice(start, start + STEP)
        grad_k = jnp.where(is_known, kt[cell, :, part], skt[cell, :, part])
        grad_v = jnp.where(is_known, vt[cell, :, part], svt[cell, :, part])
        total = grad[cell, part].astype(F32) + tn(qt[cell, :, part], wqt[...])
        total = total + tn(grad_k, wkt[...]) + tn(grad_v, wvt[...])
        grad[cell, part] = total.astype(BF)

    group = 2
    per_pass = HEADS // group
    for index in range(steps // group):
        cell, half, turn = index // (2 * per_pass), (index // per_pass) % 2, index % per_pass

        def one(i, carry):
            n = index * group + i

            @pl.when(n + slots_kept - 1 < steps)
            def _():
                bring(n + slots_kept - 1, True)

            bring(n, False)
            attend(cell, half, n)
            return carry

        lax.fori_loop(0, group, one, 0)
        if index == 0:
            wait(loads[0])
        if index in DENSE_TURNS:
            next(dense_sum, None)
        if index == 0:
            vecs[:8] = jnp.sum(dense_vecs[...], axis=1)
            vecs[8:] = jnp.zeros((8, width), F32)
            wait(*loads[1:])

            @pl.when(jnp.logical_not(is_known))
            def _():
                wait(*far_loads())

            wqt[...] = wq[...].T
            wkt[...] = wk[...].T
            wvt[...] = wv[...].T
        every = list(range(len(PIECES)))
        if half == 1 and cell < cells - 1 and turn == per_pass - 1:
            weight_sums(cell, every)
            bias_sums(cell)
        if half == 1 and cell == cells - 1:
            for piece in every:
                if sum(PIECES[piece]) == (turn + 1) * group:
                    weight_sums(cell, [piece])
                    next(back_sums[piece])
        if turn == per_pass - 1:
            send_far(cell, half)
    next(back_sums[0])
    bias_sums(cells - 1)
    vec_sum = vectors_over_devices(places, vecs[...], vecs_out, *vec_bufs, *vec_sems)
    next(vec_sum)
    running = [*back_sums[::-1], vec_sum, dense_sum]
    out_copies = []
    for cell in range(cells):
        for start in range(0, slots, STEP):
            own_rows(cell, start)
            if start % halfway > 0:
                running = [chain for chain in running if next(chain, None) is not None]
        if cell == cells - 1:
            while running:
                running = [chain for chain in running if next(chain, None) is not None]

        @pl.when(is_known)
        def _():
            for half in range(2):
                far_copy(cell, half).wait_recv()
            grad[cell] = (grad[cell].astype(F32) + far[cell].astype(F32)).astype(BF)

        out_copies += fetch([(grad.at[cell], grad_hbm.at[cell])], out_sem.at[pl.ds(cell, 1)])

    @pl.when(jnp.logical_not(is_known))
    def _():
        for cell in range(cells):
            for half in range(2):
                far_copy(cell, half).wait_send()

    wait(*out_copies)


def backward(mats, x, qt, skt, svt, weights, dense_vecs, fars, kept):
    cells, slots, width = x.shape
    dims = dims_of()
    turns = len(groups_of(dims))
    vmem = pl.BlockSpec(memory_space=pltpu.VMEM)
    hbm = pl.BlockSpec(memory_space=pl.ANY)
    across, along = (cells, width, slots), (cells, slots, width)
    square = (width, width)
    head_dim = width // HEADS
    rows = [count * head_dim for _, count in PIECES]
    sums = pltpu.SemaphoreType.DMA((3, turns, 3))
    loads = 6 * cells + 5 + 2 * cells
    return pl.pallas_call(
        functools.partial(backward_kernel, cells),
        in_specs=[hbm] * 8 + [vmem] + [hbm] * (6 * cells) + [vmem] * (3 * cells),
        out_specs=[hbm] + [vmem] * (2 + len(rows)),
        out_shape=[
            jax.ShapeDtypeStruct((cells, slots, width), BF),
            jax.ShapeDtypeStruct((3, width, width), BF),
            jax.ShapeDtypeStruct((16, width), F32),
        ]
        + [jax.ShapeDtypeStruct((3, n, width), BF) for n in rows],
        scratch_shapes=[pltpu.VMEM(along, BF)] * 4
        + [pltpu.VMEM(across, BF)] * 6
        + [pltpu.VMEM((width, slots), F32), pltpu.VMEM((3, slots // 2, slots), BF)]
        + [pltpu.VMEM(square, BF)] * 6
        + [pltpu.VMEM((3, width, width), F32), pltpu.VMEM((16, width), F32)]
        + [pltpu.VMEM((3, n, width), F32) for n in rows]
        + [pltpu.VMEM((3, room_for(width, dims), width), BF)] * 2
        + [pltpu.VMEM((turns, 16, width), F32), pltpu.VMEM((turns, 3, 16, width), F32)]
        + [sums] * 4
        + [pltpu.SemaphoreType.DMA((turns, 3))] * 2
        + [pltpu.VMEM((3, room_for(n, dims), width), BF) for n in rows for _ in range(2)]
        + [sums] * (4 * len(rows))
        + [
            pltpu.SemaphoreType.DMA((loads,)),
            pltpu.SemaphoreType.DMA((cells,)),
            pltpu.SemaphoreType.DMA((3,)),
            pltpu.SemaphoreType.DMA((cells, 2)),
            pltpu.SemaphoreType.DMA((cells, 2)),
        ],
        compiler_params=params(collective_id=0, has_side_effects=True),
        name="backward",
    )(mats, x, qt, skt, svt, *weights, dense_vecs, *fars, *(kept_of for column_of in zip(*kept) for kept_of in column_of))


def finish_kernel(grad, dense_mats, vecs, *refs):
    take = taker(refs)
    back_mats = take(len(PIECES))
    grad_out, wq, bq, wk, wv, bv, wo, bo, g1, s1, wh, bh, wr, br, g2, s2 = take(16)
    back_in = take(len(PIECES))
    kept, dense_in, results, in_sem, out_sem = take(5)
    cells = kept.shape[0]
    loads = fetch(
        list(zip(back_mats, back_in)) + [(dense_mats, dense_in)] + [(grad.at[c], kept.at[c]) for c in range(cells)],
        in_sem,
    )
    pieces = len(PIECES)
    wait(*loads[:pieces])
    copies = []
    for i, target in enumerate((wq, wk, wv, wo, wh, wr)):
        if i == 3:
            wait(loads[pieces])
        if i < 3:
            whole = jnp.concatenate([piece[i] for piece in back_in], axis=0).astype(F32).T
        else:
            whole = dense_in[i - 3].astype(F32)
        results[i] = whole
        copies += fetch([(results.at[i], target)], out_sem.at[pl.ds(i, 1)])
    for c in range(cells):
        wait(loads[pieces + 1 + c])
        copies += fetch([(kept.at[c], grad_out.at[c])], out_sem.at[pl.ds(6 + c, 1)])
    for i, target in enumerate((g2, s2, br, bh, g1, s1, bo, None, bq, bv)):
        if target is not None:
            target[...] = vecs[i]
    wait(*copies)


def finish(grad, dense_mats, vecs, *back_mats):
    cells = grad.shape[0]
    width = vecs.shape[1]
    vmem = pl.BlockSpec(memory_space=pltpu.VMEM)
    hbm = pl.BlockSpec(memory_space=pl.ANY)
    matrix = jax.ShapeDtypeStruct((width, width), F32)
    vector = jax.ShapeDtypeStruct((width,), F32)
    shapes = [matrix, vector, matrix, matrix, vector, matrix, vector, vector, vector]
    shapes += [matrix, vector, matrix, vector, vector, vector]
    return pl.pallas_call(
        finish_kernel,
        in_specs=[hbm, hbm, vmem] + [hbm] * len(back_mats),
        out_specs=[hbm] + [hbm if shape is matrix else vmem for shape in shapes],
        out_shape=[jax.ShapeDtypeStruct(grad.shape, BF)] + shapes,
        scratch_shapes=[pltpu.VMEM(piece.shape, BF) for piece in back_mats]
        + [
            pltpu.VMEM(grad.shape, BF),
            pltpu.VMEM(dense_mats.shape, BF),
            pltpu.VMEM((6, width, width), F32),
            pltpu.SemaphoreType.DMA((1 + len(back_mats) + cells,)),
            pltpu.SemaphoreType.DMA((6 + cells,)),
        ],
        compiler_params=params(),
        name="finish",
    )(grad, dense_mats, vecs, *back_mats)


def passed_along(value, axis, by):
    count = lax.axis_size(axis)
    pairs = [(i, i + by) for i in range(count) if 0 <= i + by < count]
    return lax.ppermute(value, axis, pairs)


def local(
    tokens,
    known_len,
    unknown_len,
    query_weight,
    query_bias,
    key_weight,
    value_weight,
    value_bias,
    output_weight,
    output_bias,
    first_gain,
    first_shift,
    hidden_weight,
    hidden_bias,
    return_weight,
    return_bias,
    second_gain,
    second_shift,
    cotangent,
):
    _, cells, slots, width = tokens.shape
    is_known = lax.axis_index("half") == 0
    x = tokens.reshape(cells, slots, width)
    cot = cotangent.reshape(cells, slots, width)
    own_len = jnp.where(is_known, known_len, unknown_len)
    info = jnp.concatenate([is_known.astype(jnp.int32)[None], known_len, own_len])

    def row(vector):
        return vector.reshape(1, width)

    qt, skt, svt, last_tokens, own_norm, far = project_own(
        x, query_weight, row(query_bias), key_weight, value_weight, row(value_bias)
    )
    fars = [far] + [
        passed_along(last_tokens if c == cells - 1 else x[c], "half", 1) for c in range(1, cells)
    ]
    weights = (key_weight, value_weight, output_weight, hidden_weight, return_weight)
    vectors = [
        row(vector)
        for vector in (
            value_bias,
            output_bias,
            first_gain,
            first_shift,
            hidden_bias,
            return_bias,
            second_gain,
            second_shift,
        )
    ]
    carried = ()
    kept = []
    for c in range(cells):
        layer_out, sums, vecs, pt, kt, vt, dot_t, gres, *stats = run_cell(
            info, c, own_norm, x, fars[c], cot, qt, skt, svt, weights, vectors, carried
        )
        carried = (layer_out, sums, vecs)
        kept.append((pt, kt, vt, dot_t, gres, *stats))
    weights = (query_weight, key_weight, value_weight)
    grad, *sums = backward(sums, x, qt, skt, svt, weights, vecs, fars, kept)
    grad, *summed = finish(grad, *sums)
    out_shape = (1, cells, slots, width)
    return (layer_out.reshape(out_shape), grad.reshape(out_shape), *summed)


def solution(mesh):
    placed = (
        (P("half", "cells", None, None), P("cells"), P("cells"))
        + (P(),) * 15
        + (P("half", "cells", None, None),)
    )
    return jax.shard_map(
        local,
        mesh=mesh,
        in_specs=placed,
        out_specs=(P("half", "cells", None, None),) * 2 + (P(),) * 15,
        check_vma=False,
    )
```

```python
import functools

import jax
import jax.numpy as jnp
from jax import lax
from jax.experimental import pallas as pl
from jax.experimental.pallas import tpu as pltpu
from jax.sharding import PartitionSpec as P

HEADS = 8
EPS = 1e-05
NEGATIVE = -1e30
LOG2E = 1.4426950408889634
BF = jnp.bfloat16
F32 = jnp.float32
SAFE = 60.0
DENSE_TURNS = (0, 2, 7, 9, 11)
PIECES = ((0, 8),)
VMEM_LIMIT = 58 * 2**20
STEP = 256


def nn(a, b):
    return lax.dot_general(a, b, (((1,), (0,)), ((), ())), preferred_element_type=F32)


def nt(a, b):
    return lax.dot_general(a, b, (((1,), (1,)), ((), ())), preferred_element_type=F32)


def tn(a, b):
    return lax.dot_general(a, b, (((0,), (0,)), ((), ())), preferred_element_type=F32)


def cells_of(info):
    return (info.shape[0] - 1) // 2


def params(**more):
    return pltpu.CompilerParams(vmem_limit_bytes=VMEM_LIMIT, **more)


def column(vector, lanes):
    n = vector.shape[1]
    tile = jnp.broadcast_to(vector, (128, n)).T
    return jnp.concatenate([tile] * (lanes // 128), axis=1)


def head_norms(array, head_dim):
    width, tokens = array.shape
    squares = (array * array).reshape(width // head_dim, head_dim, tokens)
    return jnp.max(jnp.sum(squares, axis=1))


def own_kernel(head_dim, key_len, x_hbm, x, wq_hbm, bq, wk_hbm, wv_hbm, bv, *refs):
    take = taker(refs)
    qt, kt, vt, again, norm, far, pt_hbm, kt_hbm, vt_hbm, ot_hbm, inverse = take(11)
    wqt, wkt, wvt, bqc, bvc, first_qt, first_kt, first_vt, first_ot, pt, wq, wk, wv = take(13)
    sent, arrived, out_sem, pt_sem, in_sem = take(5)
    cell, block = pl.program_id(0), pl.program_id(1)
    rows = x.shape[1]
    half_at = lax.axis_index("half")
    is_known = half_at == 0
    other = {"half": 1 - half_at, "cells": lax.axis_index("cells")}
    copy = pltpu.make_async_remote_copy(
        src_ref=x_hbm.at[0],
        dst_ref=far,
        send_sem=sent,
        recv_sem=arrived,
        device_id=other,
        device_id_type=pl.DeviceIdType.MESH,
    )

    @pl.when((cell == 0) & (block == 0))
    def _():
        barrier = pltpu.get_barrier_semaphore()
        pl.semaphore_signal(barrier, inc=1, device_id=other, device_id_type=pl.DeviceIdType.MESH)
        loads = fetch([(wq_hbm, wq), (wk_hbm, wk), (wv_hbm, wv)], in_sem)
        pl.semaphore_wait(barrier, 1)

        @pl.when(is_known)
        def _():
            copy.start()

        wait(*loads)
        wqt[...] = wq[...].T
        wkt[...] = wk[...].T
        wvt[...] = wv[...].T
        bqc[...] = column(bq[...], rows)
        bvc[...] = column(bv[...], rows)

    @pl.when(block == 0)
    def _():
        norm[0, cell] = 0.0
        norm[1, cell] = 0.0

    again[...] = x[0]
    queries = (nt(wqt[...], x[0]) + bqc[...]) * (LOG2E * head_dim**-0.5)
    qt[0] = queries.astype(BF)
    norm[0, cell] = jnp.maximum(norm[0, cell], head_norms(queries, head_dim))

    @pl.when(jnp.logical_not(is_known))
    def _():
        keys = nt(wkt[...], x[0])
        kt[0] = keys.astype(BF)
        norm[1, cell] = jnp.maximum(norm[1, cell], head_norms(keys, head_dim))
        vt[0] = (nt(wvt[...], x[0]) + bvc[...]).astype(BF)

    @pl.when(is_known & (cell == 0))
    def _():
        part = pl.ds(pl.multiple_of(block * rows, rows), rows)
        first_qt[:, part] = queries.astype(BF)
        first_kt[:, part] = nt(wkt[...], x[0]).astype(BF)
        first_vt[:, part] = (nt(wvt[...], x[0]) + bvc[...]).astype(BF)

    def keep(head):
        slot = lax.rem(head, 2)
        return pltpu.make_async_copy(pt.at[slot], pt_hbm.at[head], pt_sem.at[slot])

    def attend(head, carry):
        slots = first_kt.shape[1]

        @pl.when(head >= 2)
        def _():
            keep(head - 2).wait()

        band = pl.ds(pl.multiple_of(head * head_dim, head_dim), head_dim)
        index = lax.broadcasted_iota(jnp.int32, (16, slots), 1)
        first_row = lax.broadcasted_iota(jnp.int32, (16, slots), 0) == 0
        masked = jnp.where(first_row & (index >= key_len[0]), NEGATIVE, 0.0).astype(BF)
        ones = jnp.ones((16, slots), BF)
        scores = tn(
            jnp.concatenate([first_kt[band], masked], axis=0), jnp.concatenate([first_qt[band], ones], axis=0)
        )
        weights = jnp.exp2(scores - jnp.max(scores, axis=0, keepdims=True)).astype(BF)
        pt[lax.rem(head, 2)] = weights
        total = nn(jnp.concatenate([first_vt[band], ones], axis=0), weights)
        inv = 1.0 / total[head_dim : head_dim + 1]
        first_ot[band] = (total[:head_dim] * inv).astype(BF)
        inverse[pl.ds(head, 1)] = inv
        keep(head).start()
        return carry

    @pl.when((cell == pl.num_programs(0) - 1) & (block == pl.num_programs(1) - 1))
    def _():
        @pl.when(is_known)
        def _():
            results = fetch([(first_kt, kt_hbm), (first_vt, vt_hbm)], out_sem)
            lax.fori_loop(0, HEADS, attend, 0)
            results += fetch([(first_ot, ot_hbm)], out_sem.at[pl.ds(2, 1)])
            for head in (HEADS - 2, HEADS - 1):
                keep(head).wait()
            wait(*results)
            copy.wait_send()

        @pl.when(jnp.logical_not(is_known))
        def _():
            inverse[...] = jnp.zeros_like(inverse)
            copy.wait_recv()


def project_own(known_len, x, wq, bq, wk, wv, bv, rows=512):
    cells, slots, width = x.shape
    head_dim = width // HEADS
    bias = pl.BlockSpec((1, width), lambda c, i: (0, 0))
    out = pl.BlockSpec((1, width, rows), lambda c, i: (c, 0, i))
    hbm = pl.BlockSpec(memory_space=pl.ANY)
    last = cells - 1
    return pl.pallas_call(
        functools.partial(own_kernel, head_dim),
        grid=(cells, slots // rows),
        in_specs=[
            pl.BlockSpec(memory_space=pltpu.SMEM),
            hbm,
            pl.BlockSpec((1, rows, width), lambda c, i: (c, i, 0)),
            hbm,
            bias,
            hbm,
            hbm,
            bias,
        ],
        out_specs=[
            out,
            out,
            out,
            pl.BlockSpec((rows, width), lambda c, i: (lax.div(c, last) * i, 0)),
            pl.BlockSpec(memory_space=pltpu.SMEM),
            hbm,
            hbm,
            hbm,
            hbm,
            hbm,
            pl.BlockSpec((HEADS, slots), lambda c, i: (0, 0)),
        ],
        out_shape=[jax.ShapeDtypeStruct((cells, width, slots), BF)] * 3
        + [
            jax.ShapeDtypeStruct((slots, width), BF),
            jax.ShapeDtypeStruct((2, cells), F32),
            jax.ShapeDtypeStruct((slots, width), BF),
            jax.ShapeDtypeStruct((HEADS, slots, slots), BF),
        ]
        + [jax.ShapeDtypeStruct((width, slots), BF)] * 3
        + [jax.ShapeDtypeStruct((HEADS, slots), F32)],
        scratch_shapes=[pltpu.VMEM((width, width), BF)] * 3
        + [pltpu.VMEM((width, rows), F32)] * 2
        + [pltpu.VMEM((width, slots), BF)] * 4
        + [pltpu.VMEM((2, slots, slots), BF)]
        + [pltpu.VMEM((width, width), BF)] * 3
        + [pltpu.SemaphoreType.DMA] * 2
        + [pltpu.SemaphoreType.DMA((3,)), pltpu.SemaphoreType.DMA((2,)), pltpu.SemaphoreType.DMA((3,))],
        compiler_params=params(collective_id=1, has_side_effects=True),
        name="project_own",
    )(known_len, x, x, wq, bq, wk, wv, bv)


def steps_in(length):
    return lax.div(length + STEP - 1, STEP)


def sized(count, steps, body):
    for n in range(1, count + 1):
        pl.when(steps == n)(functools.partial(body, n * STEP))


def sized_pair(count, key_steps, own_steps, body):
    for a in range(1, count + 1):
        for b in range(1, count + 1):
            pl.when((key_steps == a) & (own_steps == b))(functools.partial(body, a * STEP, b * STEP))


def in_turns(chains):
    waiting = [iter(chain) for chain in chains]
    running = []
    while waiting or running:
        if waiting:
            running.append(waiting.pop(0))
        running = [chain for chain in running if next(chain, None) is not None]


def fold_rows(values):
    rows, width = values.shape
    return jnp.sum(values.reshape(rows // 8, 8, width), axis=0)


def fetch(pairs, semaphores):
    copies = [
        pltpu.make_async_copy(source, target, semaphores.at[i]) for i, (source, target) in enumerate(pairs)
    ]
    for copy in copies:
        copy.start()
    return copies


def wait(*copies):
    for copy in copies:
        copy.wait()


def taker(refs):
    place = 0

    def take(count):
        nonlocal place
        place += count
        return refs[place - count : place]

    return take


def cell_kernel(cell, first, *refs):
    take = taker(refs)
    info, own_norm, x_hbm, far_hbm, cot_hbm, qt_hbm, skt_hbm, svt_hbm = take(8)
    wk_hbm, wv_hbm, wo_hbm, wh_hbm, wr_hbm = take(5)
    bv, bo, g1, s1, bh, br, g2, s2 = take(8)
    _, sums_before, vecs_before = (None, None, None) if first else take(3)
    given_ot, given_inverse, *_ = take(5) if first else (None, None)
    out_hbm, sums_hbm, vecs, pt_hbm, kt_hbm, vt_hbm, dot_hbm, gres_hbm, inverse, self_exp, delta = take(11)
    x, source, cot, qt, skt, svt, wk, wv, wo, wh, wr = take(11)
    kt, vt, ot, dot_t, low1, act, gb, gpre, gres, out, sums, pt, wkt, wvt, bvc = take(15)
    in_sem, out_sem, block_sem, pt_sem = take(4)

    slots, width = x.shape
    head_dim = width // HEADS
    is_known = info[0] == 1
    cells = (info.shape[0] - 1) // 2
    key_len, own_len = info[1 + cell], info[1 + cells + cell]
    key_steps, own_steps = steps_in(key_len), steps_in(own_len)
    blocks = slots // STEP

    ready = is_known if first else jnp.bool_(False)
    heads = jnp.where(ready, 0, HEADS)

    if first:
        ot_load = pltpu.make_async_copy(given_ot, ot, in_sem.at[12])

        @pl.when(ready)
        def _():
            ot_load.start()
            inverse[...] = given_inverse[...]
            self_exp[...] = jnp.zeros_like(self_exp)

    known_source = pltpu.make_async_copy(x_hbm.at[cell], source, in_sem.at[0])
    far_source = pltpu.make_async_copy(far_hbm, source, in_sem.at[0])
    own_keys = [
        pltpu.make_async_copy(skt_hbm.at[cell], skt, in_sem.at[1]),
        pltpu.make_async_copy(svt_hbm.at[cell], svt, in_sem.at[2]),
    ]

    @pl.when(is_known)
    def _():
        known_source.start()

    @pl.when(jnp.logical_not(is_known))
    def _():
        far_source.start()

    loads = fetch([(wk_hbm, wk), (wv_hbm, wv)], in_sem.at[pl.ds(3, 2)])

    @pl.when(is_known)
    def _():
        known_source.wait()

    @pl.when(jnp.logical_not(is_known))
    def _():
        far_source.wait()
        for copy in own_keys:
            copy.start()

    wait(*loads)
    loads = fetch(
        [(qt_hbm.at[cell], qt), (wo_hbm, wo), (x_hbm.at[cell], x), (wh_hbm, wh), (wr_hbm, wr), (cot_hbm.at[cell], cot)]
        + ([] if first else [(sums_before, sums)]),
        in_sem.at[pl.ds(5, 7)],
    )

    def block_copies(block):
        part = pl.ds(block * STEP if isinstance(block, int) else pl.multiple_of(block * STEP, STEP), STEP)
        return [
            pltpu.make_async_copy(out.at[part], out_hbm.at[cell, part], block_sem.at[0, block]),
            pltpu.make_async_copy(dot_t.at[:, part], dot_hbm.at[:, part], block_sem.at[1, block]),
            pltpu.make_async_copy(gres.at[part], gres_hbm.at[part], block_sem.at[2, block]),
        ]

    wkt[...] = wk[...].T
    wvt[...] = wv[...].T
    bvc[...] = column(bv[...], STEP)

    def project(block, largest):
        part = pl.ds(pl.multiple_of(block * STEP, STEP), STEP)
        tokens = source[part]
        keys = nt(wkt[...], tokens)
        kt[:, part] = keys.astype(BF)
        vt[:, part] = (nt(wvt[...], tokens) + bvc[...]).astype(BF)
        return jnp.maximum(largest, head_norms(keys, head_dim))

    def blank(targets, block, carry):
        part = pl.ds(pl.multiple_of(block * STEP, STEP), STEP)
        for target in targets:
            if target.shape[0] == slots:
                target[part] = jnp.zeros((STEP, width), BF)
            else:
                target[:, part] = jnp.zeros((target.shape[0], STEP), target.dtype)
        return carry

    largest = lax.fori_loop(0, jnp.where(ready, 0, key_steps), project, jnp.float32(0.0))
    lax.fori_loop(key_steps, blocks, functools.partial(blank, (kt, vt)), 0)

    out_copies = []
    key_copies = [
        pltpu.make_async_copy(source, target, out_sem.at[i])
        for i, (source, target) in enumerate(((kt, kt_hbm), (vt, vt_hbm)))
    ]

    @pl.when(jnp.logical_not(ready))
    def _():
        for copy in key_copies:
            copy.start()

    @pl.when((key_steps < blocks) | (own_steps < blocks))
    def _():
        pt[...] = jnp.zeros_like(pt)

    def blank_block(block, carry):
        blank((out, gres, dot_t, delta), block, carry)

        @pl.when(jnp.logical_not(ready))
        def _():
            blank((inverse, self_exp), block, carry)

        for copy in block_copies(block):
            copy.start()
        return carry

    lax.fori_loop(own_steps, blocks, blank_block, 0)
    if first:
        pl.when(ready)(ot_load.wait)

    wait(loads[0])

    @pl.when(jnp.logical_not(is_known))
    def _():
        wait(*own_keys)

    largest = jnp.maximum(largest, own_norm[1, cell])
    safe = own_norm[0, cell] * largest < SAFE * SAFE

    def attend(head, slot, use_max, keys, queries):
        band = pl.ds(pl.multiple_of(head * head_dim, head_dim), head_dim)
        index = lax.broadcasted_iota(jnp.int32, (16, keys), 1)
        first_row = lax.broadcasted_iota(jnp.int32, (16, keys), 0) == 0
        masked = jnp.where(first_row & (index >= key_len), NEGATIVE, 0.0).astype(BF)
        key_part = jnp.concatenate([kt[band, :keys], masked], axis=0)
        q = qt[band, :queries]
        query_part = jnp.concatenate([q, jnp.ones((16, queries), BF)], axis=0)
        value_part = jnp.concatenate([vt[band, :keys], jnp.ones((16, keys), BF)], axis=0)
        scores = tn(key_part, query_part)
        own = jnp.sum(q.astype(F32) * skt[band, :queries].astype(F32), axis=0, keepdims=True)
        own = jnp.where(is_known, NEGATIVE, own)
        if use_max:
            top = jnp.maximum(jnp.max(scores, axis=0, keepdims=True), own)
            scores = scores - top
            own = own - top
        weights = jnp.exp2(scores).astype(BF)
        pt[slot, :keys, :queries] = weights
        own = jnp.exp2(own)
        total = nn(value_part, weights)
        inv = 1.0 / (total[head_dim : head_dim + 1] + own)
        own_values = jnp.where(is_known, 0.0, svt[band, :queries].astype(F32))
        ot[band, :queries] = ((total[:head_dim] + own * own_values) * inv).astype(BF)
        row = pl.ds(head, 1)
        inverse[row, :queries] = inv
        self_exp[row, :queries] = own

    def keep(head, slot):
        return pltpu.make_async_copy(pt.at[slot], pt_hbm.at[head], pt_sem.at[slot])

    def one_head(head, carry):
        slot = lax.rem(head, 2)

        @pl.when(head >= 2)
        def _():
            keep(head - 2, slot).wait()

        @pl.when(safe)
        def _():
            sized_pair(blocks, key_steps, own_steps, functools.partial(attend, head, slot, False))

        @pl.when(jnp.logical_not(safe))
        def _():
            attend(head, slot, True, slots, slots)

        keep(head, slot).start()
        return carry

    lax.fori_loop(0, heads, one_head, 0)

    wait(*loads[1:6])
    scale = 1.0 / width
    if first:
        vecs[...] = jnp.zeros_like(vecs)
    else:
        vecs[...] = vecs_before[...]

    def mean(values):
        return jnp.sum(values, axis=1, keepdims=True) * scale

    def chain(block):
        start = pl.multiple_of(block * STEP, STEP)
        part = pl.ds(start, STEP)
        slot_index = lax.broadcasted_iota(jnp.int32, (STEP, 1), 0) + start
        live = (slot_index < own_len).astype(F32)
        context = ot[:, part]
        r1 = tn(context, wo[...])
        yield 1
        r1 = r1 + x[part].astype(F32) + bo[...]
        centred = r1 - mean(r1)
        inv1 = lax.rsqrt(mean(centred * centred) + EPS)
        hat1 = centred * inv1
        norm1 = hat1 * g1[...] + s1[...]
        low = norm1.astype(BF)
        low1[part] = low
        yield 2
        pre = nn(low, wh[...])
        yield 3
        pre = pre + bh[...]
        cdf = 0.5 + 0.5 * lax.erf(pre * (0.5**0.5))
        active = (pre * cdf).astype(BF)
        act[part] = active
        slope = cdf + pre * (jnp.exp(-0.5 * pre * pre) * 0.3989422804014327)
        yield 4
        r2 = nn(active, wr[...])
        yield 5
        r2 = r2 + norm1 + br[...]
        centred = r2 - mean(r2)
        inv2 = lax.rsqrt(mean(centred * centred) + EPS)
        hat2 = centred * inv2
        out[part] = ((hat2 * g2[...] + s2[...]) * live).astype(BF)
        go = cot[part].astype(F32) * live
        vecs[0] += fold_rows(go * hat2)
        vecs[1] += fold_rows(go)
        gx = go * g2[...]
        gr2 = inv2 * (gx - mean(gx) - hat2 * mean(gx * hat2))
        grad_branch = gr2.astype(BF)
        gb[part] = grad_branch
        vecs[2] += fold_rows(grad_branch.astype(F32))
        yield 6
        grad_act = nt(grad_branch, wr[...])
        yield 7
        grad_pre = (grad_act * slope).astype(BF)
        gpre[part] = grad_pre
        vecs[3] += fold_rows(grad_pre.astype(F32))
        yield 8
        gn = nt(grad_pre, wh[...])
        yield 9
        gn = gr2 + gn
        vecs[4] += fold_rows(gn * hat1)
        vecs[5] += fold_rows(gn)
        gx = gn * g1[...]
        gr1 = inv1 * (gx - mean(gx) - hat1 * mean(gx * hat1))
        grad_attn = gr1.astype(BF)
        gres[part] = grad_attn
        vecs[6] += fold_rows(grad_attn.astype(F32))
        yield 10
        back = nt(wo[...], grad_attn)
        yield 11
        low_back = back.astype(BF)
        dot_t[:, part] = low_back
        product = low_back.astype(F32) * context.astype(F32)
        delta[:, part] = jnp.sum(product.reshape(HEADS, head_dim, STEP), axis=1)
        for copy in block_copies(block):
            copy.start()

    def pair(index, carry):
        in_turns([chain(2 * index), chain(2 * index + 1)])
        return carry

    lax.fori_loop(0, lax.div(own_steps, 2), pair, 0)

    @pl.when(lax.rem(own_steps, 2) == 1)
    def _():
        in_turns([chain(own_steps - 1)])

    if not first:
        wait(loads[6])

    def weight_sum(i, rows):
        if i == 0:
            value = nn(ot[:, :rows], gres[:rows])
        elif i == 1:
            value = tn(low1[:rows], gpre[:rows])
        else:
            value = tn(act[:rows], gb[:rows])
        sums[i] = value if first else sums[i] + value

    for i in range(3):
        sized(blocks, own_steps, functools.partial(weight_sum, i))
        out_copies += fetch([(sums.at[i], sums_hbm.at[i])], out_sem.at[pl.ds(2 + i, 1)])

    @pl.when(jnp.logical_not(ready))
    def _():
        for slot in range(2):
            keep(HEADS - 2 + slot, slot).wait()
        wait(*key_copies)

    for block in range(blocks):
        wait(*block_copies(block))
    wait(*out_copies)


def run_cell(info, cell, own_norm, x, far, cot, qt, skt, svt, weights, vectors, carried, given):
    cells, slots, width = x.shape
    smem = pl.BlockSpec(memory_space=pltpu.SMEM)
    vmem = pl.BlockSpec(memory_space=pltpu.VMEM)
    hbm = pl.BlockSpec(memory_space=pl.ANY)
    first = not carried
    across, along = (width, slots), (slots, width)
    square = (width, width)
    stats = (HEADS, slots)
    scratch = [along] * 3 + [across] * 3 + [square] * 5 + [across] * 4 + [along] * 6
    return pl.pallas_call(
        functools.partial(cell_kernel, cell, first),
        in_specs=[smem, smem] + [hbm] * 11 + [vmem] * 8 + ([hbm, vmem, hbm, hbm, hbm] if first else [hbm, hbm, vmem]),
        out_specs=[hbm, hbm, vmem] + [hbm] * 5 + [vmem] * 3,
        out_shape=[
            jax.ShapeDtypeStruct((cells, slots, width), BF),
            jax.ShapeDtypeStruct((3, width, width), F32),
            jax.ShapeDtypeStruct((8, 8, width), F32),
            jax.ShapeDtypeStruct((HEADS, slots, slots), BF),
        ]
        + [jax.ShapeDtypeStruct(across, BF)] * 3
        + [jax.ShapeDtypeStruct(along, BF)]
        + [jax.ShapeDtypeStruct(stats, F32)] * 3,
        scratch_shapes=[pltpu.VMEM(shape, BF) for shape in scratch]
        + [
            pltpu.VMEM((3, width, width), F32),
            pltpu.VMEM((2, slots, slots), BF),
            pltpu.VMEM(square, BF),
            pltpu.VMEM(square, BF),
            pltpu.VMEM((width, STEP), F32),
            pltpu.SemaphoreType.DMA((13,)),
            pltpu.SemaphoreType.DMA((5,)),
            pltpu.SemaphoreType.DMA((3, slots // STEP)),
            pltpu.SemaphoreType.DMA((2,)),
        ],
        input_output_aliases={23: 3, 24: 4, 25: 5} if first else {21: 0},
        compiler_params=params(),
        name="cell_forward",
    )(info, own_norm, x, far, cot, qt, skt, svt, *weights, *vectors, *carried, *given)


class Places:
    def __init__(self):
        cells = lax.axis_size("cells")
        self.half, self.cell = lax.axis_index("half"), lax.axis_index("cells")
        bits = [lax.rem(lax.div(self.cell, 2**power), 2) for power in range(cells.bit_length() - 1)]
        self.bits = [bits[0], self.half] + bits[1:]
        self.spans = [1, 0] + [2**power for power in range(1, len(bits))]

    def partner(self, flips):
        cell = self.cell
        for dim in flips:
            cell = cell + (1 - 2 * self.bits[dim]) * self.spans[dim]
        return {"half": 1 - self.half if 1 in flips else self.half, "cells": cell}

    def member(self, group, flips=()):
        index = 0
        for dim in group:
            index = 2 * index + (1 - self.bits[dim] if dim in flips else self.bits[dim])
        return index

    def send(self, flips, source, target, sent, arrived):
        copy = pltpu.make_async_remote_copy(
            src_ref=source,
            dst_ref=target,
            send_sem=sent,
            recv_sem=arrived,
            device_id=self.partner(flips),
            device_id_type=pl.DeviceIdType.MESH,
        )
        copy.start()
        return copy


def dims_of():
    return 1 + lax.axis_size("cells").bit_length() - 1


def groups_of(dims):
    rest = list(range(2, dims)) + [1]
    return [[0]] + [rest[start : start + 2] for start in range(0, len(rest), 2)]


def flips_of(group):
    return [tuple(group)] if len(group) == 1 else [(group[1],), (group[0],), tuple(group)]


def plan_of(order, rows):
    plan, base = [], 0
    for group in order:
        split = rows % (16 * 2 ** len(group)) == 0
        rows = rows // 2 ** len(group) if split else rows
        plan.append((group, rows, split, base))
        base += rows * len(flips_of(group))
    return plan, base


def room_for(rows, dims):
    return plan_of(groups_of(dims), rows)[1]


def total_of(own, came):
    return own + came[0] if len(came) == 1 else (own + came[0]) + (came[1] + came[2])


def summed_over_devices(places, mats, out, sent, got, semaphores):
    send_sem, recv_sem, back_send, back_recv = semaphores
    count, rows = mats.shape[0], mats.shape[1]
    plans = [plan_of(order, rows)[0] for order in [groups_of(len(places.bits))] * count]
    steps = len(plans[0])
    at_row = [jnp.int32(0)] * count
    started = [()] * count

    def at(place, length):
        return pl.ds(pl.multiple_of(place, 16), length)

    def finish(i, step):
        group, length, split, base = plans[i][step]
        wait(*started[i])
        here = at(at_row[i], length)
        kept = mats[i, here] if split else sent[i, base : base + length].astype(F32)
        came = [
            got[i, base + k * length : base + (k + 1) * length].astype(F32) for k in range(len(flips_of(group)))
        ]
        mats[i, here] = total_of(kept, came)

    for step in range(steps):
        for i in range(count):
            if step > 0:
                finish(i, step - 1)
            group, length, split, base = plans[i][step]
            copies = []
            if not split:
                sent[i, base : base + length] = mats[i, at(at_row[i], length)].astype(BF)
            for k, flips in enumerate(flips_of(group)):
                part = pl.ds(base + k * length, length)
                if split:
                    away = at_row[i] + places.member(group, flips) * length
                    sent[i, part] = mats[i, at(away, length)].astype(BF)
                source = part if split else pl.ds(base, length)
                copies.append(
                    places.send(
                        flips, sent.at[i, source], got.at[i, part], send_sem.at[i, step, k], recv_sem.at[i, step, k]
                    )
                )
            started[i] = copies
            if split:
                at_row[i] = at_row[i] + places.member(group) * length
        yield step
    for i in range(count):
        finish(i, steps - 1)
        here = at(at_row[i], plans[i][-1][1])
        out[i, here] = mats[i, here].astype(BF)
        started[i] = ()
    remaining = [[step for step in reversed(range(steps)) if plan[step][2]] for plan in plans]
    while any(remaining):
        for i in range(count):
            if not remaining[i]:
                continue
            step = remaining[i].pop(0)
            group, length, _, _ = plans[i][step]
            wait(*started[i])
            part = at(at_row[i], length)
            started[i] = [
                places.send(
                    flips, out.at[i, part], out.at[i, part], back_send.at[i, step, k], back_recv.at[i, step, k]
                )
                for k, flips in enumerate(flips_of(group))
            ]
            at_row[i] = at_row[i] - places.member(group) * length
        yield 0
    for i in range(count):
        wait(*started[i])


def vectors_over_devices(places, vec, out, sent, got, send_sem, recv_sem):
    for step, group in enumerate(groups_of(len(places.bits))):
        sent[step] = vec
        copies = [
            places.send(flips, sent.at[step], got.at[step, k], send_sem.at[step, k], recv_sem.at[step, k])
            for k, flips in enumerate(flips_of(group))
        ]
        yield step
        wait(*copies)
        vec = total_of(vec, [got[step, k] for k in range(len(copies))])
    out[...] = vec


def backward_kernel(cells, *refs):
    take = taker(refs)
    mats_hbm, x_hbm, qt_hbm, skt_hbm, svt_hbm, wq_hbm, wk_hbm, wv_hbm, dense_vecs = take(9)
    far_hbm, pt_hbm, kt_hbm, vt_hbm, dot_hbm, gres_hbm, inverse, self_exp, delta = (
        take(cells) for _ in range(9)
    )
    grad_hbm, dense_out, vecs_out = take(3)
    back_out = take(len(PIECES))
    x, far, far_grad, grad, qt, skt, svt, kt, vt, dot_t, dq, pt = take(12)
    wq, wk, wv, wqt, wkt, wvt, dense_mats, vecs = take(8)
    back_mats = take(len(PIECES))
    dense_bufs, vec_bufs, dense_sems, vec_sems = take(2), take(2), take(4), take(2)
    back_bufs = [take(2) for _ in PIECES]
    back_sems = [take(4) for _ in PIECES]
    in_sem, out_sem, pt_sem, far_send, far_recv = take(5)

    _, slots, width = x.shape
    head_dim = width // HEADS
    halfway = slots // 2
    half_at = lax.axis_index("half")
    is_known = half_at == 0

    places = Places()
    barrier = pltpu.get_barrier_semaphore()
    neighbours = [flips for group in groups_of(len(places.bits)) for flips in flips_of(group)]
    if (1,) not in neighbours:
        neighbours.append((1,))
    for flips in neighbours:
        pl.semaphore_signal(
            barrier, inc=1, device_id=places.partner(flips), device_id_type=pl.DeviceIdType.MESH
        )

    steps = cells * 2 * HEADS
    slots_kept = pt.shape[0]

    def bring(n, begin):
        head, slot = lax.rem(n, HEADS), lax.rem(n, slots_kept)
        part = pl.ds(pl.multiple_of(lax.rem(lax.div(n, HEADS), 2) * halfway, halfway), halfway)
        for cell in range(cells):

            @pl.when(lax.div(n, 2 * HEADS) == cell)
            def _():
                copy = pltpu.make_async_copy(
                    pt_hbm[cell].at[head, part], pt.at[slot], pt_sem.at[slot]
                )
                if begin:
                    copy.start()
                else:
                    copy.wait()

    for n in range(slots_kept - 1):
        bring(jnp.int32(n), True)
    urgent = fetch(
        [
            (vt_hbm[0], vt.at[0]),
            (dot_hbm[0], dot_t.at[0]),
            (kt_hbm[0], kt.at[0]),
            (qt_hbm.at[0], qt.at[0]),
        ],
        in_sem,
    )
    wait(*urgent)
    pairs = [(mats_hbm, dense_mats), (skt_hbm.at[0], skt.at[0]), (svt_hbm.at[0], svt.at[0])]
    pairs += [(wk_hbm, wk), (wv_hbm, wv), (wq_hbm, wq)]
    for cell in range(1, cells):
        pairs += [
            (vt_hbm[cell], vt.at[cell]),
            (dot_hbm[cell], dot_t.at[cell]),
            (kt_hbm[cell], kt.at[cell]),
            (qt_hbm.at[cell], qt.at[cell]),
            (skt_hbm.at[cell], skt.at[cell]),
            (svt_hbm.at[cell], svt.at[cell]),
        ]
    pairs.append((x_hbm, x))
    pairs += [(gres_hbm[cell], grad.at[cell]) for cell in range(cells)]
    loads = fetch(pairs, in_sem.at[pl.ds(4, len(pairs))])

    def far_loads():
        return [
            pltpu.make_async_copy(far_hbm[cell], far.at[cell], in_sem.at[4 + len(pairs) + cell])
            for cell in range(cells)
        ]

    @pl.when(jnp.logical_not(is_known))
    def _():
        for copy in far_loads():
            copy.start()

    pl.semaphore_wait(barrier, len(neighbours))
    dense_sum = summed_over_devices(places, dense_mats, dense_out, *dense_bufs, dense_sems)
    back_sums = [
        summed_over_devices(places, back_mats[i], back_out[i], *back_bufs[i], back_sems[i])
        for i in range(len(PIECES))
    ]

    def attend(cell, half, n):
        head, slot = lax.rem(n, HEADS), lax.rem(n, slots_kept)
        band = pl.ds(pl.multiple_of(head * head_dim, head_dim), head_dim)
        row = pl.ds(head, 1)
        q = qt[cell, band]
        inv = inverse[cell][row]
        grads = dot_t[cell, band].astype(F32)
        scaled = (grads * inv).astype(BF)
        inner = delta[cell][row]
        inner_scaled = inner * inv
        high = inner_scaled.astype(BF)
        rest = (inner_scaled - high.astype(F32)).astype(BF)
        wide = jnp.concatenate(
            [scaled, jnp.broadcast_to(high, (8, slots)), jnp.broadcast_to(rest, (8, slots))], axis=0
        )
        signs = jnp.where(lax.broadcasted_iota(jnp.int32, (16, STEP), 0) % 8 == 0, -1.0, 0.0).astype(BF)
        total = dq[band] if half == 1 else 0.0
        for start in range(0, halfway, STEP):
            part = slice(half * halfway + start, half * halfway + start + STEP)
            weights = pt[slot, start : start + STEP]
            grad_probs = tn(jnp.concatenate([vt[cell, band, part], signs], axis=0), wide)
            grad_scores = (weights.astype(F32) * grad_probs).astype(BF)
            keys = kt[cell, band, part]
            vt[cell, band, part] = nt(scaled, weights).astype(BF)
            kt[cell, band, part] = (nt(q, grad_scores) * (1.0 / LOG2E)).astype(BF)
            total = total + nn(keys, grad_scores)
        if half == 0:
            dq[band] = total
            return
        prob = self_exp[cell][row] * inv
        own_keys = jnp.where(is_known, 0.0, skt[cell, band].astype(F32))
        own_values = jnp.where(is_known, 0.0, svt[cell, band].astype(F32))
        grad_prob = jnp.sum(grads * own_values, axis=0, keepdims=True)
        grad_score = prob * (grad_prob - inner)
        qt[cell, band] = ((total + grad_score * own_keys) * head_dim**-0.5).astype(BF)
        skt[cell, band] = (q.astype(F32) * (grad_score * (1.0 / LOG2E))).astype(BF)
        svt[cell, band] = (grads * prob).astype(BF)

    def far_copy(cell, half):
        part = pl.ds(half * halfway, halfway)
        return pltpu.make_async_remote_copy(
            src_ref=far_grad.at[cell, part],
            dst_ref=far.at[cell, part],
            send_sem=far_send.at[cell, half],
            recv_sem=far_recv.at[cell, half],
            device_id=places.partner((1,)),
            device_id_type=pl.DeviceIdType.MESH,
        )

    def send_far(cell, half):
        @pl.when(jnp.logical_not(is_known))
        def _():
            for start in range(half * halfway, (half + 1) * halfway, STEP):
                part = slice(start, start + STEP)
                total = tn(kt[cell, :, part], wkt[...]) + tn(vt[cell, :, part], wvt[...])
                far_grad[cell, part] = total.astype(BF)
            far_copy(cell, half).start()

    def weight_sums(cell, pieces):
        begin = PIECES[pieces[0]][0] * head_dim
        band = slice(begin, (PIECES[pieces[-1]][0] + PIECES[pieces[-1]][1]) * head_dim)

        def add(i, value, anew):
            for piece in pieces:
                start = PIECES[piece][0] * head_dim - begin
                part = value[start : start + PIECES[piece][1] * head_dim]
                back_mats[piece][i] = part if anew else back_mats[piece][i] + part

        grad_k = jnp.where(is_known, kt[cell, band], skt[cell, band])
        grad_v = jnp.where(is_known, vt[cell, band], svt[cell, band])
        for i, part in enumerate((qt[cell, band], grad_k, grad_v)):
            add(i, nn(part, x[cell]), cell == 0)

        @pl.when(jnp.logical_not(is_known))
        def _():
            add(1, nn(kt[cell, band], far[cell]), False)
            add(2, nn(vt[cell, band], far[cell]), False)

    def bias_sums(cell):
        ones = jnp.ones((8, slots), BF)
        grad_v = jnp.where(is_known, vt[cell], svt[cell])
        vecs[8:9] += nt(ones, qt[cell])[:1]
        vecs[9:10] += nt(ones, grad_v)[:1]

        @pl.when(jnp.logical_not(is_known))
        def _():
            vecs[9:10] += nt(ones, vt[cell])[:1]

    def own_rows(cell, start):
        part = slice(start, start + STEP)
        grad_k = jnp.where(is_known, kt[cell, :, part], skt[cell, :, part])
        grad_v = jnp.where(is_known, vt[cell, :, part], svt[cell, :, part])
        total = grad[cell, part].astype(F32) + tn(qt[cell, :, part], wqt[...])
        total = total + tn(grad_k, wkt[...]) + tn(grad_v, wvt[...])
        grad[cell, part] = total.astype(BF)

    group = 2
    per_pass = HEADS // group
    for index in range(steps // group):
        cell, half, turn = index // (2 * per_pass), (index // per_pass) % 2, index % per_pass

        def one(i, carry):
            n = index * group + i

            @pl.when(n + slots_kept - 1 < steps)
            def _():
                bring(n + slots_kept - 1, True)

            bring(n, False)
            attend(cell, half, n)
            return carry

        lax.fori_loop(0, group, one, 0)
        if index == 0:
            wait(loads[0])
        if index in DENSE_TURNS:
            next(dense_sum, None)
        if index == 0:
            vecs[:8] = jnp.sum(dense_vecs[...], axis=1)
            vecs[8:] = jnp.zeros((8, width), F32)
            wait(*loads[1:])

            @pl.when(jnp.logical_not(is_known))
            def _():
                wait(*far_loads())

            wqt[...] = wq[...].T
            wkt[...] = wk[...].T
            wvt[...] = wv[...].T
        every = list(range(len(PIECES)))
        if half == 1 and cell < cells - 1 and turn == per_pass - 1:
            weight_sums(cell, every)
            bias_sums(cell)
        if half == 1 and cell == cells - 1:
            for piece in every:
                if sum(PIECES[piece]) == (turn + 1) * group:
                    weight_sums(cell, [piece])
                    next(back_sums[piece])
        if turn == per_pass - 1:
            send_far(cell, half)
    next(back_sums[0])
    bias_sums(cells - 1)
    vec_sum = vectors_over_devices(places, vecs[...], vecs_out, *vec_bufs, *vec_sems)
    next(vec_sum)
    running = [*back_sums[::-1], vec_sum, dense_sum]
    out_copies = []
    for cell in range(cells):
        for start in range(0, slots, STEP):
            own_rows(cell, start)
            if start % halfway > 0:
                running = [chain for chain in running if next(chain, None) is not None]
        if cell == cells - 1:
            while running:
                running = [chain for chain in running if next(chain, None) is not None]

        @pl.when(is_known)
        def _():
            for half in range(2):
                far_copy(cell, half).wait_recv()
            grad[cell] = (grad[cell].astype(F32) + far[cell].astype(F32)).astype(BF)

        out_copies += fetch([(grad.at[cell], grad_hbm.at[cell])], out_sem.at[pl.ds(cell, 1)])

    @pl.when(jnp.logical_not(is_known))
    def _():
        for cell in range(cells):
            for half in range(2):
                far_copy(cell, half).wait_send()

    wait(*out_copies)


def backward(mats, x, qt, skt, svt, weights, dense_vecs, fars, kept):
    cells, slots, width = x.shape
    dims = dims_of()
    turns = len(groups_of(dims))
    vmem = pl.BlockSpec(memory_space=pltpu.VMEM)
    hbm = pl.BlockSpec(memory_space=pl.ANY)
    across, along = (cells, width, slots), (cells, slots, width)
    square = (width, width)
    head_dim = width // HEADS
    rows = [count * head_dim for _, count in PIECES]
    sums = pltpu.SemaphoreType.DMA((3, turns, 3))
    loads = 6 * cells + 5 + 2 * cells
    return pl.pallas_call(
        functools.partial(backward_kernel, cells),
        in_specs=[hbm] * 8 + [vmem] + [hbm] * (6 * cells) + [vmem] * (3 * cells),
        out_specs=[hbm] + [vmem] * (2 + len(rows)),
        out_shape=[
            jax.ShapeDtypeStruct((cells, slots, width), BF),
            jax.ShapeDtypeStruct((3, width, width), BF),
            jax.ShapeDtypeStruct((16, width), F32),
        ]
        + [jax.ShapeDtypeStruct((3, n, width), BF) for n in rows],
        scratch_shapes=[pltpu.VMEM(along, BF)] * 4
        + [pltpu.VMEM(across, BF)] * 6
        + [pltpu.VMEM((width, slots), F32), pltpu.VMEM((3, slots // 2, slots), BF)]
        + [pltpu.VMEM(square, BF)] * 6
        + [pltpu.VMEM((3, width, width), F32), pltpu.VMEM((16, width), F32)]
        + [pltpu.VMEM((3, n, width), F32) for n in rows]
        + [pltpu.VMEM((3, room_for(width, dims), width), BF)] * 2
        + [pltpu.VMEM((turns, 16, width), F32), pltpu.VMEM((turns, 3, 16, width), F32)]
        + [sums] * 4
        + [pltpu.SemaphoreType.DMA((turns, 3))] * 2
        + [pltpu.VMEM((3, room_for(n, dims), width), BF) for n in rows for _ in range(2)]
        + [sums] * (4 * len(rows))
        + [
            pltpu.SemaphoreType.DMA((loads,)),
            pltpu.SemaphoreType.DMA((cells,)),
            pltpu.SemaphoreType.DMA((3,)),
            pltpu.SemaphoreType.DMA((cells, 2)),
            pltpu.SemaphoreType.DMA((cells, 2)),
        ],
        compiler_params=params(collective_id=0, has_side_effects=True),
        name="backward",
    )(mats, x, qt, skt, svt, *weights, dense_vecs, *fars, *(kept_of for column_of in zip(*kept) for kept_of in column_of))


def finish_kernel(grad, dense_mats, vecs, *refs):
    take = taker(refs)
    back_mats = take(len(PIECES))
    grad_out, wq, bq, wk, wv, bv, wo, bo, g1, s1, wh, bh, wr, br, g2, s2 = take(16)
    back_in = take(len(PIECES))
    kept, dense_in, results, in_sem, out_sem = take(5)
    cells = kept.shape[0]
    loads = fetch(
        list(zip(back_mats, back_in)) + [(dense_mats, dense_in)] + [(grad.at[c], kept.at[c]) for c in range(cells)],
        in_sem,
    )
    pieces = len(PIECES)
    wait(*loads[:pieces])
    copies = []
    for i, target in enumerate((wq, wk, wv, wo, wh, wr)):
        if i == 3:
            wait(loads[pieces])
        if i < 3:
            whole = jnp.concatenate([piece[i] for piece in back_in], axis=0).astype(F32).T
        else:
            whole = dense_in[i - 3].astype(F32)
        results[i] = whole
        copies += fetch([(results.at[i], target)], out_sem.at[pl.ds(i, 1)])
    for c in range(cells):
        wait(loads[pieces + 1 + c])
        copies += fetch([(kept.at[c], grad_out.at[c])], out_sem.at[pl.ds(6 + c, 1)])
    for i, target in enumerate((g2, s2, br, bh, g1, s1, bo, None, bq, bv)):
        if target is not None:
            target[...] = vecs[i]
    wait(*copies)


def finish(grad, dense_mats, vecs, *back_mats):
    cells = grad.shape[0]
    width = vecs.shape[1]
    vmem = pl.BlockSpec(memory_space=pltpu.VMEM)
    hbm = pl.BlockSpec(memory_space=pl.ANY)
    matrix = jax.ShapeDtypeStruct((width, width), F32)
    vector = jax.ShapeDtypeStruct((width,), F32)
    shapes = [matrix, vector, matrix, matrix, vector, matrix, vector, vector, vector]
    shapes += [matrix, vector, matrix, vector, vector, vector]
    return pl.pallas_call(
        finish_kernel,
        in_specs=[hbm, hbm, vmem] + [hbm] * len(back_mats),
        out_specs=[hbm] + [hbm if shape is matrix else vmem for shape in shapes],
        out_shape=[jax.ShapeDtypeStruct(grad.shape, BF)] + shapes,
        scratch_shapes=[pltpu.VMEM(piece.shape, BF) for piece in back_mats]
        + [
            pltpu.VMEM(grad.shape, BF),
            pltpu.VMEM(dense_mats.shape, BF),
            pltpu.VMEM((6, width, width), F32),
            pltpu.SemaphoreType.DMA((1 + len(back_mats) + cells,)),
            pltpu.SemaphoreType.DMA((6 + cells,)),
        ],
        compiler_params=params(),
        name="finish",
    )(grad, dense_mats, vecs, *back_mats)


def passed_along(value, axis, by):
    count = lax.axis_size(axis)
    pairs = [(i, i + by) for i in range(count) if 0 <= i + by < count]
    return lax.ppermute(value, axis, pairs)


def local(
    tokens,
    known_len,
    unknown_len,
    query_weight,
    query_bias,
    key_weight,
    value_weight,
    value_bias,
    output_weight,
    output_bias,
    first_gain,
    first_shift,
    hidden_weight,
    hidden_bias,
    return_weight,
    return_bias,
    second_gain,
    second_shift,
    cotangent,
):
    _, cells, slots, width = tokens.shape
    is_known = lax.axis_index("half") == 0
    x = tokens.reshape(cells, slots, width)
    cot = cotangent.reshape(cells, slots, width)
    own_len = jnp.where(is_known, known_len, unknown_len)
    info = jnp.concatenate([is_known.astype(jnp.int32)[None], known_len, own_len])

    def row(vector):
        return vector.reshape(1, width)

    qt, skt, svt, last_tokens, own_norm, far, pt, kt, vt, ot, inverse = project_own(
        known_len, x, query_weight, row(query_bias), key_weight, value_weight, row(value_bias)
    )
    fars = [far] + [
        passed_along(last_tokens if c == cells - 1 else x[c], "half", 1) for c in range(1, cells)
    ]
    weights = (key_weight, value_weight, output_weight, hidden_weight, return_weight)
    vectors = [
        row(vector)
        for vector in (
            value_bias,
            output_bias,
            first_gain,
            first_shift,
            hidden_bias,
            return_bias,
            second_gain,
            second_shift,
        )
    ]
    carried = ()
    kept = []
    for c in range(cells):
        layer_out, sums, vecs, pt, kt, vt, dot_t, gres, *stats = run_cell(
            info, c, own_norm, x, fars[c], cot, qt, skt, svt, weights, vectors, carried, () if carried else (ot, inverse, pt, kt, vt)
        )
        carried = (layer_out, sums, vecs)
        kept.append((pt, kt, vt, dot_t, gres, *stats))
    weights = (query_weight, key_weight, value_weight)
    grad, *sums = backward(sums, x, qt, skt, svt, weights, vecs, fars, kept)
    grad, *summed = finish(grad, *sums)
    out_shape = (1, cells, slots, width)
    return (layer_out.reshape(out_shape), grad.reshape(out_shape), *summed)


def solution(mesh):
    placed = (
        (P("half", "cells", None, None), P("cells"), P("cells"))
        + (P(),) * 15
        + (P("half", "cells", None, None),)
    )
    return jax.shard_map(
        local,
        mesh=mesh,
        in_specs=placed,
        out_specs=(P("half", "cells", None, None),) * 2 + (P(),) * 15,
        check_vma=False,
    )
```

```python
import functools

import jax
import jax.numpy as jnp
from jax import lax
from jax.experimental import pallas as pl
from jax.experimental.pallas import tpu as pltpu
from jax.sharding import PartitionSpec as P

HEADS = 8
EPS = 1e-05
NEGATIVE = -1e30
LOG2E = 1.4426950408889634
BF = jnp.bfloat16
F32 = jnp.float32
SAFE = 60.0
DENSE_TURNS = (0, 2, 7, 9, 15)
PIECES = ((0, 8),)
VMEM_LIMIT = 58 * 2**20
STEP = 256


def nn(a, b):
    return lax.dot_general(a, b, (((1,), (0,)), ((), ())), preferred_element_type=F32)


def nt(a, b):
    return lax.dot_general(a, b, (((1,), (1,)), ((), ())), preferred_element_type=F32)


def tn(a, b):
    return lax.dot_general(a, b, (((0,), (0,)), ((), ())), preferred_element_type=F32)


def cells_of(info):
    return (info.shape[0] - 1) // 2


def params(**more):
    return pltpu.CompilerParams(vmem_limit_bytes=VMEM_LIMIT, **more)


def column(vector, lanes):
    n = vector.shape[1]
    tile = jnp.broadcast_to(vector, (128, n)).T
    return jnp.concatenate([tile] * (lanes // 128), axis=1)


def head_norms(array, head_dim):
    width, tokens = array.shape
    squares = (array * array).reshape(width // head_dim, head_dim, tokens)
    return jnp.max(jnp.sum(squares, axis=1))


def own_kernel(head_dim, key_len, x_hbm, x, wq_hbm, bq, wk_hbm, wv_hbm, bv, *refs):
    take = taker(refs)
    qt, kt, vt, again, norm, far, pt_hbm, kt_hbm, vt_hbm, ot_hbm, inverse = take(11)
    wqt, wkt, wvt, bqc, bvc, first_qt, first_kt, first_vt, first_ot, pt, wq, wk, wv = take(13)
    sent, arrived, out_sem, pt_sem, in_sem = take(5)
    cell, block = pl.program_id(0), pl.program_id(1)
    rows = x.shape[1]
    half_at = lax.axis_index("half")
    is_known = half_at == 0
    other = {"half": 1 - half_at, "cells": lax.axis_index("cells")}
    copy = pltpu.make_async_remote_copy(
        src_ref=x_hbm.at[0],
        dst_ref=far,
        send_sem=sent,
        recv_sem=arrived,
        device_id=other,
        device_id_type=pl.DeviceIdType.MESH,
    )

    @pl.when((cell == 0) & (block == 0))
    def _():
        barrier = pltpu.get_barrier_semaphore()
        pl.semaphore_signal(barrier, inc=1, device_id=other, device_id_type=pl.DeviceIdType.MESH)
        loads = fetch([(wq_hbm, wq), (wk_hbm, wk), (wv_hbm, wv)], in_sem)
        pl.semaphore_wait(barrier, 1)

        @pl.when(is_known)
        def _():
            copy.start()

        wait(*loads)
        wqt[...] = wq[...].T
        wkt[...] = wk[...].T
        wvt[...] = wv[...].T
        bqc[...] = column(bq[...], rows)
        bvc[...] = column(bv[...], rows)

    @pl.when(block == 0)
    def _():
        norm[0, cell] = 0.0
        norm[1, cell] = 0.0

    again[...] = x[0]
    queries = (nt(wqt[...], x[0]) + bqc[...]) * (LOG2E * head_dim**-0.5)
    qt[0] = queries.astype(BF)
    norm[0, cell] = jnp.maximum(norm[0, cell], head_norms(queries, head_dim))

    @pl.when(jnp.logical_not(is_known))
    def _():
        keys = nt(wkt[...], x[0])
        kt[0] = keys.astype(BF)
        norm[1, cell] = jnp.maximum(norm[1, cell], head_norms(keys, head_dim))
        vt[0] = (nt(wvt[...], x[0]) + bvc[...]).astype(BF)

    @pl.when(is_known & (cell == 0))
    def _():
        part = pl.ds(pl.multiple_of(block * rows, rows), rows)
        first_qt[:, part] = queries.astype(BF)
        first_kt[:, part] = nt(wkt[...], x[0]).astype(BF)
        first_vt[:, part] = (nt(wvt[...], x[0]) + bvc[...]).astype(BF)

    def keep(head):
        slot = lax.rem(head, 2)
        return pltpu.make_async_copy(pt.at[slot], pt_hbm.at[head], pt_sem.at[slot])

    def attend(head, carry):
        slots = first_kt.shape[1]

        @pl.when(head >= 2)
        def _():
            keep(head - 2).wait()

        band = pl.ds(pl.multiple_of(head * head_dim, head_dim), head_dim)
        index = lax.broadcasted_iota(jnp.int32, (16, slots), 1)
        first_row = lax.broadcasted_iota(jnp.int32, (16, slots), 0) == 0
        masked = jnp.where(first_row & (index >= key_len[0]), NEGATIVE, 0.0).astype(BF)
        ones = jnp.ones((16, slots), BF)
        scores = tn(
            jnp.concatenate([first_kt[band], masked], axis=0), jnp.concatenate([first_qt[band], ones], axis=0)
        )
        weights = jnp.exp2(scores - jnp.max(scores, axis=0, keepdims=True)).astype(BF)
        pt[lax.rem(head, 2)] = weights
        total = nn(jnp.concatenate([first_vt[band], ones], axis=0), weights)
        inv = 1.0 / total[head_dim : head_dim + 1]
        first_ot[band] = (total[:head_dim] * inv).astype(BF)
        inverse[pl.ds(head, 1)] = inv
        keep(head).start()
        return carry

    @pl.when((cell == pl.num_programs(0) - 1) & (block == pl.num_programs(1) - 1))
    def _():
        @pl.when(is_known)
        def _():
            results = fetch([(first_kt, kt_hbm), (first_vt, vt_hbm)], out_sem)
            lax.fori_loop(0, HEADS, attend, 0)
            results += fetch([(first_ot, ot_hbm)], out_sem.at[pl.ds(2, 1)])
            for head in (HEADS - 2, HEADS - 1):
                keep(head).wait()
            wait(*results)
            copy.wait_send()

        @pl.when(jnp.logical_not(is_known))
        def _():
            inverse[...] = jnp.zeros_like(inverse)
            copy.wait_recv()


def project_own(known_len, x, wq, bq, wk, wv, bv, rows=512):
    cells, slots, width = x.shape
    head_dim = width // HEADS
    bias = pl.BlockSpec((1, width), lambda c, i: (0, 0))
    out = pl.BlockSpec((1, width, rows), lambda c, i: (c, 0, i))
    hbm = pl.BlockSpec(memory_space=pl.ANY)
    last = cells - 1
    return pl.pallas_call(
        functools.partial(own_kernel, head_dim),
        grid=(cells, slots // rows),
        in_specs=[
            pl.BlockSpec(memory_space=pltpu.SMEM),
            hbm,
            pl.BlockSpec((1, rows, width), lambda c, i: (c, i, 0)),
            hbm,
            bias,
            hbm,
            hbm,
            bias,
        ],
        out_specs=[
            out,
            out,
            out,
            pl.BlockSpec((rows, width), lambda c, i: (lax.div(c, last) * i, 0)),
            pl.BlockSpec(memory_space=pltpu.SMEM),
            hbm,
            hbm,
            hbm,
            hbm,
            hbm,
            pl.BlockSpec((HEADS, slots), lambda c, i: (0, 0)),
        ],
        out_shape=[jax.ShapeDtypeStruct((cells, width, slots), BF)] * 3
        + [
            jax.ShapeDtypeStruct((slots, width), BF),
            jax.ShapeDtypeStruct((2, cells), F32),
            jax.ShapeDtypeStruct((slots, width), BF),
            jax.ShapeDtypeStruct((HEADS, slots, slots), BF),
        ]
        + [jax.ShapeDtypeStruct((width, slots), BF)] * 3
        + [jax.ShapeDtypeStruct((HEADS, slots), F32)],
        scratch_shapes=[pltpu.VMEM((width, width), BF)] * 3
        + [pltpu.VMEM((width, rows), F32)] * 2
        + [pltpu.VMEM((width, slots), BF)] * 4
        + [pltpu.VMEM((2, slots, slots), BF)]
        + [pltpu.VMEM((width, width), BF)] * 3
        + [pltpu.SemaphoreType.DMA] * 2
        + [pltpu.SemaphoreType.DMA((3,)), pltpu.SemaphoreType.DMA((2,)), pltpu.SemaphoreType.DMA((3,))],
        compiler_params=params(collective_id=1, has_side_effects=True),
        name="project_own",
    )(known_len, x, x, wq, bq, wk, wv, bv)


def steps_in(length):
    return lax.div(length + STEP - 1, STEP)


def sized(count, steps, body):
    for n in range(1, count + 1):
        pl.when(steps == n)(functools.partial(body, n * STEP))


def sized_pair(count, key_steps, own_steps, body):
    for a in range(1, count + 1):
        for b in range(1, count + 1):
            pl.when((key_steps == a) & (own_steps == b))(functools.partial(body, a * STEP, b * STEP))


def in_turns(chains):
    waiting = [iter(chain) for chain in chains]
    running = []
    while waiting or running:
        if waiting:
            running.append(waiting.pop(0))
        running = [chain for chain in running if next(chain, None) is not None]


def fold_rows(values):
    rows, width = values.shape
    return jnp.sum(values.reshape(rows // 8, 8, width), axis=0)


def fetch(pairs, semaphores):
    copies = [
        pltpu.make_async_copy(source, target, semaphores.at[i]) for i, (source, target) in enumerate(pairs)
    ]
    for copy in copies:
        copy.start()
    return copies


def wait(*copies):
    for copy in copies:
        copy.wait()


def taker(refs):
    place = 0

    def take(count):
        nonlocal place
        place += count
        return refs[place - count : place]

    return take


def cell_kernel(cell, first, *refs):
    take = taker(refs)
    info, own_norm, x_hbm, far_hbm, cot_hbm, qt_hbm, skt_hbm, svt_hbm = take(8)
    wk_hbm, wv_hbm, wo_hbm, wh_hbm, wr_hbm = take(5)
    bv, bo, g1, s1, bh, br, g2, s2 = take(8)
    _, sums_before, vecs_before = (None, None, None) if first else take(3)
    given_ot, given_inverse, *_ = take(5) if first else (None, None)
    out_hbm, sums_hbm, vecs, pt_hbm, kt_hbm, vt_hbm, dot_hbm, gres_hbm, inverse, self_exp, delta = take(11)
    x, source, cot, qt, skt, svt, wk, wv, wo, wh, wr = take(11)
    kt, vt, ot, dot_t, low1, act, gb, gpre, gres, out, sums, pt, wkt, wvt, bvc = take(15)
    in_sem, out_sem, block_sem, pt_sem = take(4)

    slots, width = x.shape
    head_dim = width // HEADS
    is_known = info[0] == 1
    cells = (info.shape[0] - 1) // 2
    key_len, own_len = info[1 + cell], info[1 + cells + cell]
    key_steps, own_steps = steps_in(key_len), steps_in(own_len)
    blocks = slots // STEP

    ready = is_known if first else jnp.bool_(False)
    heads = jnp.where(ready, 0, HEADS)

    if first:
        ot_load = pltpu.make_async_copy(given_ot, ot, in_sem.at[12])

        @pl.when(ready)
        def _():
            ot_load.start()
            inverse[...] = given_inverse[...]
            self_exp[...] = jnp.zeros_like(self_exp)

    known_source = pltpu.make_async_copy(x_hbm.at[cell], source, in_sem.at[0])
    far_source = pltpu.make_async_copy(far_hbm, source, in_sem.at[0])
    own_keys = [
        pltpu.make_async_copy(skt_hbm.at[cell], skt, in_sem.at[1]),
        pltpu.make_async_copy(svt_hbm.at[cell], svt, in_sem.at[2]),
    ]

    @pl.when(is_known)
    def _():
        known_source.start()

    @pl.when(jnp.logical_not(is_known))
    def _():
        far_source.start()

    loads = fetch([(wk_hbm, wk), (wv_hbm, wv)], in_sem.at[pl.ds(3, 2)])

    @pl.when(is_known)
    def _():
        known_source.wait()

    @pl.when(jnp.logical_not(is_known))
    def _():
        far_source.wait()
        for copy in own_keys:
            copy.start()

    wait(*loads)
    loads = fetch(
        [(qt_hbm.at[cell], qt), (wo_hbm, wo), (x_hbm.at[cell], x), (wh_hbm, wh), (wr_hbm, wr), (cot_hbm.at[cell], cot)]
        + ([] if first else [(sums_before, sums)]),
        in_sem.at[pl.ds(5, 7)],
    )

    def block_copies(block):
        part = pl.ds(block * STEP if isinstance(block, int) else pl.multiple_of(block * STEP, STEP), STEP)
        return [
            pltpu.make_async_copy(out.at[part], out_hbm.at[cell, part], block_sem.at[0, block]),
            pltpu.make_async_copy(dot_t.at[:, part], dot_hbm.at[:, part], block_sem.at[1, block]),
            pltpu.make_async_copy(gres.at[part], gres_hbm.at[part], block_sem.at[2, block]),
        ]

    wkt[...] = wk[...].T
    wvt[...] = wv[...].T
    bvc[...] = column(bv[...], STEP)

    def project(block, largest):
        part = pl.ds(pl.multiple_of(block * STEP, STEP), STEP)
        tokens = source[part]
        keys = nt(wkt[...], tokens)
        kt[:, part] = keys.astype(BF)
        vt[:, part] = (nt(wvt[...], tokens) + bvc[...]).astype(BF)
        return jnp.maximum(largest, head_norms(keys, head_dim))

    def blank(targets, block, carry):
        part = pl.ds(pl.multiple_of(block * STEP, STEP), STEP)
        for target in targets:
            if target.shape[0] == slots:
                target[part] = jnp.zeros((STEP, width), BF)
            else:
                target[:, part] = jnp.zeros((target.shape[0], STEP), target.dtype)
        return carry

    largest = lax.fori_loop(0, jnp.where(ready, 0, key_steps), project, jnp.float32(0.0))
    lax.fori_loop(key_steps, blocks, functools.partial(blank, (kt, vt)), 0)

    out_copies = []
    key_copies = [
        pltpu.make_async_copy(source, target, out_sem.at[i])
        for i, (source, target) in enumerate(((kt, kt_hbm), (vt, vt_hbm)))
    ]

    @pl.when(jnp.logical_not(ready))
    def _():
        for copy in key_copies:
            copy.start()

    @pl.when((key_steps < blocks) | (own_steps < blocks))
    def _():
        pt[...] = jnp.zeros_like(pt)

    def blank_block(block, carry):
        blank((out, gres, dot_t, delta), block, carry)

        @pl.when(jnp.logical_not(ready))
        def _():
            blank((inverse, self_exp), block, carry)

        for copy in block_copies(block):
            copy.start()
        return carry

    lax.fori_loop(own_steps, blocks, blank_block, 0)
    if first:
        pl.when(ready)(ot_load.wait)

    wait(loads[0])

    @pl.when(jnp.logical_not(is_known))
    def _():
        wait(*own_keys)

    largest = jnp.maximum(largest, own_norm[1, cell])
    safe = own_norm[0, cell] * largest < SAFE * SAFE

    def attend(head, slot, use_max, keys, queries):
        band = pl.ds(pl.multiple_of(head * head_dim, head_dim), head_dim)
        index = lax.broadcasted_iota(jnp.int32, (16, keys), 1)
        first_row = lax.broadcasted_iota(jnp.int32, (16, keys), 0) == 0
        masked = jnp.where(first_row & (index >= key_len), NEGATIVE, 0.0).astype(BF)
        key_part = jnp.concatenate([kt[band, :keys], masked], axis=0)
        q = qt[band, :queries]
        query_part = jnp.concatenate([q, jnp.ones((16, queries), BF)], axis=0)
        value_part = jnp.concatenate([vt[band, :keys], jnp.ones((16, keys), BF)], axis=0)
        scores = tn(key_part, query_part)
        own = jnp.sum(q.astype(F32) * skt[band, :queries].astype(F32), axis=0, keepdims=True)
        own = jnp.where(is_known, NEGATIVE, own)
        if use_max:
            top = jnp.maximum(jnp.max(scores, axis=0, keepdims=True), own)
            scores = scores - top
            own = own - top
        weights = jnp.exp2(scores).astype(BF)
        pt[slot, :keys, :queries] = weights
        own = jnp.exp2(own)
        total = nn(value_part, weights)
        inv = 1.0 / (total[head_dim : head_dim + 1] + own)
        own_values = jnp.where(is_known, 0.0, svt[band, :queries].astype(F32))
        ot[band, :queries] = ((total[:head_dim] + own * own_values) * inv).astype(BF)
        row = pl.ds(head, 1)
        inverse[row, :queries] = inv
        self_exp[row, :queries] = own

    def keep(head, slot):
        return pltpu.make_async_copy(pt.at[slot], pt_hbm.at[head], pt_sem.at[slot])

    def one_head(head, carry):
        slot = lax.rem(head, 2)

        @pl.when(head >= 2)
        def _():
            keep(head - 2, slot).wait()

        @pl.when(safe)
        def _():
            sized_pair(blocks, key_steps, own_steps, functools.partial(attend, head, slot, False))

        @pl.when(jnp.logical_not(safe))
        def _():
            attend(head, slot, True, slots, slots)

        keep(head, slot).start()
        return carry

    lax.fori_loop(0, heads, one_head, 0)

    wait(*loads[1:6])
    scale = 1.0 / width
    if first:
        vecs[...] = jnp.zeros_like(vecs)
    else:
        vecs[...] = vecs_before[...]

    def mean(values):
        return jnp.sum(values, axis=1, keepdims=True) * scale

    def chain(block):
        start = pl.multiple_of(block * STEP, STEP)
        part = pl.ds(start, STEP)
        slot_index = lax.broadcasted_iota(jnp.int32, (STEP, 1), 0) + start
        live = (slot_index < own_len).astype(F32)
        context = ot[:, part]
        r1 = tn(context, wo[...])
        yield 1
        r1 = r1 + x[part].astype(F32) + bo[...]
        centred = r1 - mean(r1)
        inv1 = lax.rsqrt(mean(centred * centred) + EPS)
        hat1 = centred * inv1
        norm1 = hat1 * g1[...] + s1[...]
        low = norm1.astype(BF)
        low1[part] = low
        yield 2
        pre = nn(low, wh[...])
        yield 3
        pre = pre + bh[...]
        cdf = 0.5 + 0.5 * lax.erf(pre * (0.5**0.5))
        active = (pre * cdf).astype(BF)
        act[part] = active
        slope = cdf + pre * (jnp.exp(-0.5 * pre * pre) * 0.3989422804014327)
        yield 4
        r2 = nn(active, wr[...])
        yield 5
        r2 = r2 + norm1 + br[...]
        centred = r2 - mean(r2)
        inv2 = lax.rsqrt(mean(centred * centred) + EPS)
        hat2 = centred * inv2
        out[part] = ((hat2 * g2[...] + s2[...]) * live).astype(BF)
        go = cot[part].astype(F32) * live
        vecs[0] += fold_rows(go * hat2)
        vecs[1] += fold_rows(go)
        gx = go * g2[...]
        gr2 = inv2 * (gx - mean(gx) - hat2 * mean(gx * hat2))
        grad_branch = gr2.astype(BF)
        gb[part] = grad_branch
        vecs[2] += fold_rows(grad_branch.astype(F32))
        yield 6
        grad_act = nt(grad_branch, wr[...])
        yield 7
        grad_pre = (grad_act * slope).astype(BF)
        gpre[part] = grad_pre
        vecs[3] += fold_rows(grad_pre.astype(F32))
        yield 8
        gn = nt(grad_pre, wh[...])
        yield 9
        gn = gr2 + gn
        vecs[4] += fold_rows(gn * hat1)
        vecs[5] += fold_rows(gn)
        gx = gn * g1[...]
        gr1 = inv1 * (gx - mean(gx) - hat1 * mean(gx * hat1))
        grad_attn = gr1.astype(BF)
        gres[part] = grad_attn
        vecs[6] += fold_rows(grad_attn.astype(F32))
        yield 10
        back = nt(wo[...], grad_attn)
        yield 11
        low_back = back.astype(BF)
        dot_t[:, part] = low_back
        product = low_back.astype(F32) * context.astype(F32)
        delta[:, part] = jnp.sum(product.reshape(HEADS, head_dim, STEP), axis=1)
        for copy in block_copies(block):
            copy.start()

    def pair(index, carry):
        in_turns([chain(2 * index), chain(2 * index + 1)])
        return carry

    lax.fori_loop(0, lax.div(own_steps, 2), pair, 0)

    @pl.when(lax.rem(own_steps, 2) == 1)
    def _():
        in_turns([chain(own_steps - 1)])

    if not first:
        wait(loads[6])

    def weight_sum(i, rows):
        if i == 0:
            value = nn(ot[:, :rows], gres[:rows])
        elif i == 1:
            value = tn(low1[:rows], gpre[:rows])
        else:
            value = tn(act[:rows], gb[:rows])
        sums[i] = value if first else sums[i] + value

    for i in range(3):
        sized(blocks, own_steps, functools.partial(weight_sum, i))
        out_copies += fetch([(sums.at[i], sums_hbm.at[i])], out_sem.at[pl.ds(2 + i, 1)])

    @pl.when(jnp.logical_not(ready))
    def _():
        for slot in range(2):
            keep(HEADS - 2 + slot, slot).wait()
        wait(*key_copies)

    for block in range(blocks):
        wait(*block_copies(block))
    wait(*out_copies)


def run_cell(info, cell, own_norm, x, far, cot, qt, skt, svt, weights, vectors, carried, given):
    cells, slots, width = x.shape
    smem = pl.BlockSpec(memory_space=pltpu.SMEM)
    vmem = pl.BlockSpec(memory_space=pltpu.VMEM)
    hbm = pl.BlockSpec(memory_space=pl.ANY)
    first = not carried
    across, along = (width, slots), (slots, width)
    square = (width, width)
    stats = (HEADS, slots)
    scratch = [along] * 3 + [across] * 3 + [square] * 5 + [across] * 4 + [along] * 6
    return pl.pallas_call(
        functools.partial(cell_kernel, cell, first),
        in_specs=[smem, smem] + [hbm] * 11 + [vmem] * 8 + ([hbm, vmem, hbm, hbm, hbm] if first else [hbm, hbm, vmem]),
        out_specs=[hbm, hbm, vmem] + [hbm] * 5 + [vmem] * 3,
        out_shape=[
            jax.ShapeDtypeStruct((cells, slots, width), BF),
            jax.ShapeDtypeStruct((3, width, width), F32),
            jax.ShapeDtypeStruct((8, 8, width), F32),
            jax.ShapeDtypeStruct((HEADS, slots, slots), BF),
        ]
        + [jax.ShapeDtypeStruct(across, BF)] * 3
        + [jax.ShapeDtypeStruct(along, BF)]
        + [jax.ShapeDtypeStruct(stats, F32)] * 3,
        scratch_shapes=[pltpu.VMEM(shape, BF) for shape in scratch]
        + [
            pltpu.VMEM((3, width, width), F32),
            pltpu.VMEM((2, slots, slots), BF),
            pltpu.VMEM(square, BF),
            pltpu.VMEM(square, BF),
            pltpu.VMEM((width, STEP), F32),
            pltpu.SemaphoreType.DMA((13,)),
            pltpu.SemaphoreType.DMA((5,)),
            pltpu.SemaphoreType.DMA((3, slots // STEP)),
            pltpu.SemaphoreType.DMA((2,)),
        ],
        input_output_aliases={23: 3, 24: 4, 25: 5} if first else {21: 0},
        compiler_params=params(),
        name="cell_forward",
    )(info, own_norm, x, far, cot, qt, skt, svt, *weights, *vectors, *carried, *given)


class Places:
    def __init__(self):
        cells = lax.axis_size("cells")
        self.half, self.cell = lax.axis_index("half"), lax.axis_index("cells")
        bits = [lax.rem(lax.div(self.cell, 2**power), 2) for power in range(cells.bit_length() - 1)]
        self.bits = [bits[0], self.half] + bits[1:]
        self.spans = [1, 0] + [2**power for power in range(1, len(bits))]

    def partner(self, flips):
        cell = self.cell
        for dim in flips:
            cell = cell + (1 - 2 * self.bits[dim]) * self.spans[dim]
        return {"half": 1 - self.half if 1 in flips else self.half, "cells": cell}

    def member(self, group, flips=()):
        index = 0
        for dim in group:
            index = 2 * index + (1 - self.bits[dim] if dim in flips else self.bits[dim])
        return index

    def send(self, flips, source, target, sent, arrived):
        copy = pltpu.make_async_remote_copy(
            src_ref=source,
            dst_ref=target,
            send_sem=sent,
            recv_sem=arrived,
            device_id=self.partner(flips),
            device_id_type=pl.DeviceIdType.MESH,
        )
        copy.start()
        return copy


def dims_of():
    return 1 + lax.axis_size("cells").bit_length() - 1


def groups_of(dims):
    rest = list(range(2, dims)) + [1]
    return [[0]] + [rest[start : start + 2] for start in range(0, len(rest), 2)]


def flips_of(group):
    return [tuple(group)] if len(group) == 1 else [(group[1],), (group[0],), tuple(group)]


def plan_of(order, rows):
    plan, base = [], 0
    for group in order:
        split = rows % (16 * 2 ** len(group)) == 0
        rows = rows // 2 ** len(group) if split else rows
        plan.append((group, rows, split, base))
        base += rows * len(flips_of(group))
    return plan, base


def room_for(rows, dims):
    return plan_of(groups_of(dims), rows)[1]


def total_of(own, came):
    return own + came[0] if len(came) == 1 else (own + came[0]) + (came[1] + came[2])


def summed_over_devices(places, mats, out, sent, got, semaphores):
    send_sem, recv_sem, back_send, back_recv = semaphores
    count, rows = mats.shape[0], mats.shape[1]
    plans = [plan_of(order, rows)[0] for order in [groups_of(len(places.bits))] * count]
    steps = len(plans[0])
    at_row = [jnp.int32(0)] * count
    started = [()] * count

    def at(place, length):
        return pl.ds(pl.multiple_of(place, 16), length)

    def finish(i, step):
        group, length, split, base = plans[i][step]
        wait(*started[i])
        here = at(at_row[i], length)
        kept = mats[i, here] if split else sent[i, base : base + length].astype(F32)
        came = [
            got[i, base + k * length : base + (k + 1) * length].astype(F32) for k in range(len(flips_of(group)))
        ]
        mats[i, here] = total_of(kept, came)

    for step in range(steps):
        for i in range(count):
            if step > 0:
                finish(i, step - 1)
            group, length, split, base = plans[i][step]
            copies = []
            if not split:
                sent[i, base : base + length] = mats[i, at(at_row[i], length)].astype(BF)
            for k, flips in enumerate(flips_of(group)):
                part = pl.ds(base + k * length, length)
                if split:
                    away = at_row[i] + places.member(group, flips) * length
                    sent[i, part] = mats[i, at(away, length)].astype(BF)
                source = part if split else pl.ds(base, length)
                copies.append(
                    places.send(
                        flips, sent.at[i, source], got.at[i, part], send_sem.at[i, step, k], recv_sem.at[i, step, k]
                    )
                )
            started[i] = copies
            if split:
                at_row[i] = at_row[i] + places.member(group) * length
        yield step
    for i in range(count):
        finish(i, steps - 1)
        here = at(at_row[i], plans[i][-1][1])
        out[i, here] = mats[i, here].astype(BF)
        started[i] = ()
    remaining = [[step for step in reversed(range(steps)) if plan[step][2]] for plan in plans]
    while any(remaining):
        for i in range(count):
            if not remaining[i]:
                continue
            step = remaining[i].pop(0)
            group, length, _, _ = plans[i][step]
            wait(*started[i])
            part = at(at_row[i], length)
            started[i] = [
                places.send(
                    flips, out.at[i, part], out.at[i, part], back_send.at[i, step, k], back_recv.at[i, step, k]
                )
                for k, flips in enumerate(flips_of(group))
            ]
            at_row[i] = at_row[i] - places.member(group) * length
        yield 0
    for i in range(count):
        wait(*started[i])


def vectors_over_devices(places, vec, out, sent, got, send_sem, recv_sem):
    for step, group in enumerate(groups_of(len(places.bits))):
        sent[step] = vec
        copies = [
            places.send(flips, sent.at[step], got.at[step, k], send_sem.at[step, k], recv_sem.at[step, k])
            for k, flips in enumerate(flips_of(group))
        ]
        yield step
        wait(*copies)
        vec = total_of(vec, [got[step, k] for k in range(len(copies))])
    out[...] = vec


def backward_kernel(cells, *refs):
    take = taker(refs)
    mats_hbm, x_hbm, qt_hbm, skt_hbm, svt_hbm, wq_hbm, wk_hbm, wv_hbm, dense_vecs = take(9)
    far_hbm, pt_hbm, kt_hbm, vt_hbm, dot_hbm, gres_hbm, inverse, self_exp, delta = (
        take(cells) for _ in range(9)
    )
    grad_hbm, dense_hbm, vecs_out = take(3)
    back_out = take(len(PIECES))
    x, far, far_grad, grad, qt, skt, svt, kt, vt, dot_t, dq, pt = take(12)
    wq, wk, wv, wqt, wkt, wvt, dense_mats, vecs = take(8)
    back_mats = take(len(PIECES))
    dense_bufs, vec_bufs, dense_sems, vec_sems = take(2), take(2), take(4), take(2)
    back_bufs = [take(2) for _ in PIECES]
    back_sems = [take(4) for _ in PIECES]
    in_sem, out_sem, pt_sem, far_send, far_recv, dense_out = take(6)

    _, slots, width = x.shape
    head_dim = width // HEADS
    halfway = slots // 2
    half_at = lax.axis_index("half")
    is_known = half_at == 0

    places = Places()
    barrier = pltpu.get_barrier_semaphore()
    neighbours = [flips for group in groups_of(len(places.bits)) for flips in flips_of(group)]
    if (1,) not in neighbours:
        neighbours.append((1,))
    for flips in neighbours:
        pl.semaphore_signal(
            barrier, inc=1, device_id=places.partner(flips), device_id_type=pl.DeviceIdType.MESH
        )

    steps = cells * 2 * HEADS
    slots_kept = pt.shape[0]

    def bring(n, begin):
        head, slot = lax.rem(n, HEADS), lax.rem(n, slots_kept)
        part = pl.ds(pl.multiple_of(lax.rem(lax.div(n, HEADS), 2) * halfway, halfway), halfway)
        for cell in range(cells):

            @pl.when(lax.div(n, 2 * HEADS) == cell)
            def _():
                copy = pltpu.make_async_copy(
                    pt_hbm[cell].at[head, part], pt.at[slot], pt_sem.at[slot]
                )
                if begin:
                    copy.start()
                else:
                    copy.wait()

    for n in range(slots_kept - 1):
        bring(jnp.int32(n), True)
    urgent = fetch(
        [
            (vt_hbm[0], vt.at[0]),
            (dot_hbm[0], dot_t.at[0]),
            (kt_hbm[0], kt.at[0]),
            (qt_hbm.at[0], qt.at[0]),
        ],
        in_sem,
    )
    wait(*urgent)
    pairs = [(mats_hbm, dense_mats), (skt_hbm.at[0], skt.at[0]), (svt_hbm.at[0], svt.at[0])]
    pairs += [(wk_hbm, wk), (wv_hbm, wv), (wq_hbm, wq)]
    for cell in range(1, cells):
        pairs += [
            (vt_hbm[cell], vt.at[cell]),
            (dot_hbm[cell], dot_t.at[cell]),
            (kt_hbm[cell], kt.at[cell]),
            (qt_hbm.at[cell], qt.at[cell]),
            (skt_hbm.at[cell], skt.at[cell]),
            (svt_hbm.at[cell], svt.at[cell]),
        ]
    pairs.append((x_hbm, x))
    pairs += [(gres_hbm[cell], grad.at[cell]) for cell in range(cells)]
    loads = fetch(pairs, in_sem.at[pl.ds(4, len(pairs))])

    def far_loads():
        return [
            pltpu.make_async_copy(far_hbm[cell], far.at[cell], in_sem.at[4 + len(pairs) + cell])
            for cell in range(cells)
        ]

    @pl.when(jnp.logical_not(is_known))
    def _():
        for copy in far_loads():
            copy.start()

    pl.semaphore_wait(barrier, len(neighbours))
    dense_sum = summed_over_devices(places, dense_mats, dense_out, *dense_bufs, dense_sems)
    back_sums = [
        summed_over_devices(places, back_mats[i], back_out[i], *back_bufs[i], back_sems[i])
        for i in range(len(PIECES))
    ]

    def attend(cell, half, n):
        head, slot = lax.rem(n, HEADS), lax.rem(n, slots_kept)
        band = pl.ds(pl.multiple_of(head * head_dim, head_dim), head_dim)
        row = pl.ds(head, 1)
        q = qt[cell, band]
        inv = inverse[cell][row]
        grads = dot_t[cell, band].astype(F32)
        scaled = (grads * inv).astype(BF)
        inner = delta[cell][row]
        inner_scaled = inner * inv
        high = inner_scaled.astype(BF)
        rest = (inner_scaled - high.astype(F32)).astype(BF)
        wide = jnp.concatenate(
            [scaled, jnp.broadcast_to(high, (8, slots)), jnp.broadcast_to(rest, (8, slots))], axis=0
        )
        signs = jnp.where(lax.broadcasted_iota(jnp.int32, (16, STEP), 0) % 8 == 0, -1.0, 0.0).astype(BF)
        total = dq[band] if half == 1 else 0.0
        for start in range(0, halfway, STEP):
            part = slice(half * halfway + start, half * halfway + start + STEP)
            weights = pt[slot, start : start + STEP]
            grad_probs = tn(jnp.concatenate([vt[cell, band, part], signs], axis=0), wide)
            grad_scores = (weights.astype(F32) * grad_probs).astype(BF)
            keys = kt[cell, band, part]
            vt[cell, band, part] = nt(scaled, weights).astype(BF)
            kt[cell, band, part] = (nt(q, grad_scores) * (1.0 / LOG2E)).astype(BF)
            total = total + nn(keys, grad_scores)
        if half == 0:
            dq[band] = total
            return
        prob = self_exp[cell][row] * inv
        own_keys = jnp.where(is_known, 0.0, skt[cell, band].astype(F32))
        own_values = jnp.where(is_known, 0.0, svt[cell, band].astype(F32))
        grad_prob = jnp.sum(grads * own_values, axis=0, keepdims=True)
        grad_score = prob * (grad_prob - inner)
        qt[cell, band] = ((total + grad_score * own_keys) * head_dim**-0.5).astype(BF)
        skt[cell, band] = (q.astype(F32) * (grad_score * (1.0 / LOG2E))).astype(BF)
        svt[cell, band] = (grads * prob).astype(BF)

    def far_copy(cell, half):
        part = pl.ds(half * halfway, halfway)
        return pltpu.make_async_remote_copy(
            src_ref=far_grad.at[cell, part],
            dst_ref=far.at[cell, part],
            send_sem=far_send.at[cell, half],
            recv_sem=far_recv.at[cell, half],
            device_id=places.partner((1,)),
            device_id_type=pl.DeviceIdType.MESH,
        )

    def send_far(cell, half):
        @pl.when(jnp.logical_not(is_known))
        def _():
            for start in range(half * halfway, (half + 1) * halfway, STEP):
                part = slice(start, start + STEP)
                total = tn(kt[cell, :, part], wkt[...]) + tn(vt[cell, :, part], wvt[...])
                far_grad[cell, part] = total.astype(BF)
            far_copy(cell, half).start()

    def weight_sums(cell, pieces):
        begin = PIECES[pieces[0]][0] * head_dim
        band = slice(begin, (PIECES[pieces[-1]][0] + PIECES[pieces[-1]][1]) * head_dim)

        def add(i, value, anew):
            for piece in pieces:
                start = PIECES[piece][0] * head_dim - begin
                part = value[start : start + PIECES[piece][1] * head_dim]
                back_mats[piece][i] = part if anew else back_mats[piece][i] + part

        grad_k = jnp.where(is_known, kt[cell, band], skt[cell, band])
        grad_v = jnp.where(is_known, vt[cell, band], svt[cell, band])
        for i, part in enumerate((qt[cell, band], grad_k, grad_v)):
            add(i, nn(part, x[cell]), cell == 0)

        @pl.when(jnp.logical_not(is_known))
        def _():
            add(1, nn(kt[cell, band], far[cell]), False)
            add(2, nn(vt[cell, band], far[cell]), False)

    def bias_sums(cell):
        ones = jnp.ones((8, slots), BF)
        grad_v = jnp.where(is_known, vt[cell], svt[cell])
        vecs[8:9] += nt(ones, qt[cell])[:1]
        vecs[9:10] += nt(ones, grad_v)[:1]

        @pl.when(jnp.logical_not(is_known))
        def _():
            vecs[9:10] += nt(ones, vt[cell])[:1]

    def own_rows(cell, start):
        part = slice(start, start + STEP)
        grad_k = jnp.where(is_known, kt[cell, :, part], skt[cell, :, part])
        grad_v = jnp.where(is_known, vt[cell, :, part], svt[cell, :, part])
        total = grad[cell, part].astype(F32) + tn(qt[cell, :, part], wqt[...])
        total = total + tn(grad_k, wkt[...]) + tn(grad_v, wvt[...])
        grad[cell, part] = total.astype(BF)

    group = 2
    per_pass = HEADS // group
    for index in range(steps // group):
        cell, half, turn = index // (2 * per_pass), (index // per_pass) % 2, index % per_pass

        def one(i, carry):
            n = index * group + i

            @pl.when(n + slots_kept - 1 < steps)
            def _():
                bring(n + slots_kept - 1, True)

            bring(n, False)
            attend(cell, half, n)
            return carry

        lax.fori_loop(0, group, one, 0)
        if index == 0:
            wait(loads[0])
        if index in DENSE_TURNS:
            next(dense_sum, None)
        if index == 0:
            vecs[:8] = jnp.sum(dense_vecs[...], axis=1)
            vecs[8:] = jnp.zeros((8, width), F32)
            wait(*loads[1:])

            @pl.when(jnp.logical_not(is_known))
            def _():
                wait(*far_loads())

            wqt[...] = wq[...].T
            wkt[...] = wk[...].T
            wvt[...] = wv[...].T
        every = list(range(len(PIECES)))
        if half == 1 and cell < cells - 1 and turn == per_pass - 1:
            weight_sums(cell, every)
            bias_sums(cell)
        if half == 1 and cell == cells - 1:
            for piece in every:
                if sum(PIECES[piece]) == (turn + 1) * group:
                    weight_sums(cell, [piece])
                    next(back_sums[piece])
        if turn == per_pass - 1:
            send_far(cell, half)
    next(back_sums[0])
    bias_sums(cells - 1)
    vec_sum = vectors_over_devices(places, vecs[...], vecs_out, *vec_bufs, *vec_sems)
    next(vec_sum)
    running = [*back_sums[::-1], vec_sum, dense_sum]
    out_copies = []
    for cell in range(cells):
        for start in range(0, slots, STEP):
            own_rows(cell, start)
            if start % halfway > 0:
                running = [chain for chain in running if next(chain, None) is not None]
        if cell == 0:
            for _ in dense_sum:
                pass
            out_copies += fetch([(dense_out, dense_hbm)], out_sem.at[pl.ds(cells, 1)])
        if cell == cells - 1:
            while running:
                running = [chain for chain in running if next(chain, None) is not None]

        @pl.when(is_known)
        def _():
            for half in range(2):
                far_copy(cell, half).wait_recv()
            grad[cell] = (grad[cell].astype(F32) + far[cell].astype(F32)).astype(BF)

        out_copies += fetch([(grad.at[cell], grad_hbm.at[cell])], out_sem.at[pl.ds(cell, 1)])

    @pl.when(jnp.logical_not(is_known))
    def _():
        for cell in range(cells):
            for half in range(2):
                far_copy(cell, half).wait_send()

    wait(*out_copies)


def backward(mats, x, qt, skt, svt, weights, dense_vecs, fars, kept):
    cells, slots, width = x.shape
    dims = dims_of()
    turns = len(groups_of(dims))
    vmem = pl.BlockSpec(memory_space=pltpu.VMEM)
    hbm = pl.BlockSpec(memory_space=pl.ANY)
    across, along = (cells, width, slots), (cells, slots, width)
    square = (width, width)
    head_dim = width // HEADS
    rows = [count * head_dim for _, count in PIECES]
    sums = pltpu.SemaphoreType.DMA((3, turns, 3))
    loads = 6 * cells + 5 + 2 * cells
    return pl.pallas_call(
        functools.partial(backward_kernel, cells),
        in_specs=[hbm] * 8 + [vmem] + [hbm] * (6 * cells) + [vmem] * (3 * cells),
        out_specs=[hbm, hbm] + [vmem] * (1 + len(rows)),
        out_shape=[
            jax.ShapeDtypeStruct((cells, slots, width), BF),
            jax.ShapeDtypeStruct((3, width, width), BF),
            jax.ShapeDtypeStruct((16, width), F32),
        ]
        + [jax.ShapeDtypeStruct((3, n, width), BF) for n in rows],
        scratch_shapes=[pltpu.VMEM(along, BF)] * 4
        + [pltpu.VMEM(across, BF)] * 6
        + [pltpu.VMEM((width, slots), F32), pltpu.VMEM((3, slots // 2, slots), BF)]
        + [pltpu.VMEM(square, BF)] * 6
        + [pltpu.VMEM((3, width, width), F32), pltpu.VMEM((16, width), F32)]
        + [pltpu.VMEM((3, n, width), F32) for n in rows]
        + [pltpu.VMEM((3, room_for(width, dims), width), BF)] * 2
        + [pltpu.VMEM((turns, 16, width), F32), pltpu.VMEM((turns, 3, 16, width), F32)]
        + [sums] * 4
        + [pltpu.SemaphoreType.DMA((turns, 3))] * 2
        + [pltpu.VMEM((3, room_for(n, dims), width), BF) for n in rows for _ in range(2)]
        + [sums] * (4 * len(rows))
        + [
            pltpu.SemaphoreType.DMA((loads,)),
            pltpu.SemaphoreType.DMA((cells + 1,)),
            pltpu.SemaphoreType.DMA((3,)),
            pltpu.SemaphoreType.DMA((cells, 2)),
            pltpu.SemaphoreType.DMA((cells, 2)),
            pltpu.VMEM((3, width, width), BF),
        ],
        compiler_params=params(collective_id=0, has_side_effects=True),
        name="backward",
    )(mats, x, qt, skt, svt, *weights, dense_vecs, *fars, *(kept_of for column_of in zip(*kept) for kept_of in column_of))


def finish_kernel(grad, dense_mats, vecs, *refs):
    take = taker(refs)
    back_mats = take(len(PIECES))
    grad_out, wq, bq, wk, wv, bv, wo, bo, g1, s1, wh, bh, wr, br, g2, s2 = take(16)
    back_in = take(len(PIECES))
    kept, dense_in, results, in_sem, out_sem = take(5)
    cells = kept.shape[0]
    loads = fetch(
        list(zip(back_mats, back_in)) + [(dense_mats, dense_in)] + [(grad.at[c], kept.at[c]) for c in range(cells)],
        in_sem,
    )
    pieces = len(PIECES)
    wait(*loads[:pieces])
    copies = []
    for i, target in enumerate((wq, wk, wv, wo, wh, wr)):
        if i == 3:
            wait(loads[pieces])
        if i < 3:
            whole = jnp.concatenate([piece[i] for piece in back_in], axis=0).astype(F32).T
        else:
            whole = dense_in[i - 3].astype(F32)
        results[i] = whole
        copies += fetch([(results.at[i], target)], out_sem.at[pl.ds(i, 1)])
    for c in range(cells):
        wait(loads[pieces + 1 + c])
        copies += fetch([(kept.at[c], grad_out.at[c])], out_sem.at[pl.ds(6 + c, 1)])
    for i, target in enumerate((g2, s2, br, bh, g1, s1, bo, None, bq, bv)):
        if target is not None:
            target[...] = vecs[i]
    wait(*copies)


def finish(grad, dense_mats, vecs, *back_mats):
    cells = grad.shape[0]
    width = vecs.shape[1]
    vmem = pl.BlockSpec(memory_space=pltpu.VMEM)
    hbm = pl.BlockSpec(memory_space=pl.ANY)
    matrix = jax.ShapeDtypeStruct((width, width), F32)
    vector = jax.ShapeDtypeStruct((width,), F32)
    shapes = [matrix, vector, matrix, matrix, vector, matrix, vector, vector, vector]
    shapes += [matrix, vector, matrix, vector, vector, vector]
    return pl.pallas_call(
        finish_kernel,
        in_specs=[hbm, hbm, vmem] + [hbm] * len(back_mats),
        out_specs=[hbm] + [hbm if shape is matrix else vmem for shape in shapes],
        out_shape=[jax.ShapeDtypeStruct(grad.shape, BF)] + shapes,
        scratch_shapes=[pltpu.VMEM(piece.shape, BF) for piece in back_mats]
        + [
            pltpu.VMEM(grad.shape, BF),
            pltpu.VMEM(dense_mats.shape, BF),
            pltpu.VMEM((6, width, width), F32),
            pltpu.SemaphoreType.DMA((1 + len(back_mats) + cells,)),
            pltpu.SemaphoreType.DMA((6 + cells,)),
        ],
        compiler_params=params(),
        name="finish",
    )(grad, dense_mats, vecs, *back_mats)


def passed_along(value, axis, by):
    count = lax.axis_size(axis)
    pairs = [(i, i + by) for i in range(count) if 0 <= i + by < count]
    return lax.ppermute(value, axis, pairs)


def local(
    tokens,
    known_len,
    unknown_len,
    query_weight,
    query_bias,
    key_weight,
    value_weight,
    value_bias,
    output_weight,
    output_bias,
    first_gain,
    first_shift,
    hidden_weight,
    hidden_bias,
    return_weight,
    return_bias,
    second_gain,
    second_shift,
    cotangent,
):
    _, cells, slots, width = tokens.shape
    is_known = lax.axis_index("half") == 0
    x = tokens.reshape(cells, slots, width)
    cot = cotangent.reshape(cells, slots, width)
    own_len = jnp.where(is_known, known_len, unknown_len)
    info = jnp.concatenate([is_known.astype(jnp.int32)[None], known_len, own_len])

    def row(vector):
        return vector.reshape(1, width)

    qt, skt, svt, last_tokens, own_norm, far, pt, kt, vt, ot, inverse = project_own(
        known_len, x, query_weight, row(query_bias), key_weight, value_weight, row(value_bias)
    )
    fars = [far] + [
        passed_along(last_tokens if c == cells - 1 else x[c], "half", 1) for c in range(1, cells)
    ]
    weights = (key_weight, value_weight, output_weight, hidden_weight, return_weight)
    vectors = [
        row(vector)
        for vector in (
            value_bias,
            output_bias,
            first_gain,
            first_shift,
            hidden_bias,
            return_bias,
            second_gain,
            second_shift,
        )
    ]
    carried = ()
    kept = []
    for c in range(cells):
        layer_out, sums, vecs, pt, kt, vt, dot_t, gres, *stats = run_cell(
            info, c, own_norm, x, fars[c], cot, qt, skt, svt, weights, vectors, carried, () if carried else (ot, inverse, pt, kt, vt)
        )
        carried = (layer_out, sums, vecs)
        kept.append((pt, kt, vt, dot_t, gres, *stats))
    weights = (query_weight, key_weight, value_weight)
    grad, *sums = backward(sums, x, qt, skt, svt, weights, vecs, fars, kept)
    grad, *summed = finish(grad, *sums)
    out_shape = (1, cells, slots, width)
    return (layer_out.reshape(out_shape), grad.reshape(out_shape), *summed)


def solution(mesh):
    placed = (
        (P("half", "cells", None, None), P("cells"), P("cells"))
        + (P(),) * 15
        + (P("half", "cells", None, None),)
    )
    return jax.shard_map(
        local,
        mesh=mesh,
        in_specs=placed,
        out_specs=(P("half", "cells", None, None),) * 2 + (P(),) * 15,
        check_vma=False,
    )
```

```python
import functools

import jax
import jax.numpy as jnp
from jax import lax
from jax.experimental import pallas as pl
from jax.experimental.pallas import tpu as pltpu
from jax.sharding import PartitionSpec as P

HEADS = 8
EPS = 1e-05
NEGATIVE = -1e30
LOG2E = 1.4426950408889634
BF = jnp.bfloat16
F32 = jnp.float32
SAFE = 60.0
DENSE_TURNS = (0, 2, 7, 9, 15)
PIECES = ((0, 8),)
VMEM_LIMIT = 58 * 2**20
STEP = 256


def nn(a, b):
    return lax.dot_general(a, b, (((1,), (0,)), ((), ())), preferred_element_type=F32)


def nt(a, b):
    return lax.dot_general(a, b, (((1,), (1,)), ((), ())), preferred_element_type=F32)


def tn(a, b):
    return lax.dot_general(a, b, (((0,), (0,)), ((), ())), preferred_element_type=F32)


def cells_of(info):
    return (info.shape[0] - 1) // 2


def params(**more):
    return pltpu.CompilerParams(vmem_limit_bytes=VMEM_LIMIT, **more)


def column(vector, lanes):
    n = vector.shape[1]
    tile = jnp.broadcast_to(vector, (128, n)).T
    return jnp.concatenate([tile] * (lanes // 128), axis=1)


def head_norms(array, head_dim):
    width, tokens = array.shape
    squares = (array * array).reshape(width // head_dim, head_dim, tokens)
    return jnp.max(jnp.sum(squares, axis=1))


def own_kernel(head_dim, key_len, x_hbm, x, wq_hbm, bq, wk_hbm, wv_hbm, bv, *refs):
    take = taker(refs)
    qt, kt, vt, again, norm, far, pt_hbm, kt_hbm, vt_hbm, ot_hbm, inverse = take(11)
    wqt, wkt, wvt, bqc, bvc, first_qt, first_kt, first_vt, first_ot, pt, wq, wk, wv = take(13)
    sent, arrived, out_sem, pt_sem, in_sem = take(5)
    cell, block = pl.program_id(0), pl.program_id(1)
    rows = x.shape[1]
    half_at = lax.axis_index("half")
    is_known = half_at == 0
    other = {"half": 1 - half_at, "cells": lax.axis_index("cells")}
    copy = pltpu.make_async_remote_copy(
        src_ref=x_hbm.at[0],
        dst_ref=far,
        send_sem=sent,
        recv_sem=arrived,
        device_id=other,
        device_id_type=pl.DeviceIdType.MESH,
    )

    @pl.when((cell == 0) & (block == 0))
    def _():
        barrier = pltpu.get_barrier_semaphore()
        pl.semaphore_signal(barrier, inc=1, device_id=other, device_id_type=pl.DeviceIdType.MESH)
        loads = fetch([(wq_hbm, wq), (wk_hbm, wk), (wv_hbm, wv)], in_sem)
        pl.semaphore_wait(barrier, 1)

        @pl.when(is_known)
        def _():
            copy.start()

        wait(*loads)
        wqt[...] = wq[...].T
        wkt[...] = wk[...].T
        wvt[...] = wv[...].T
        bqc[...] = column(bq[...], rows)
        bvc[...] = column(bv[...], rows)

    @pl.when(block == 0)
    def _():
        norm[0, cell] = 0.0
        norm[1, cell] = 0.0

    again[...] = x[0]
    queries = (nt(wqt[...], x[0]) + bqc[...]) * (LOG2E * head_dim**-0.5)
    qt[0] = queries.astype(BF)
    norm[0, cell] = jnp.maximum(norm[0, cell], head_norms(queries, head_dim))

    @pl.when(jnp.logical_not(is_known))
    def _():
        keys = nt(wkt[...], x[0])
        kt[0] = keys.astype(BF)
        norm[1, cell] = jnp.maximum(norm[1, cell], head_norms(keys, head_dim))
        vt[0] = (nt(wvt[...], x[0]) + bvc[...]).astype(BF)

    @pl.when(is_known & (cell == 0))
    def _():
        part = pl.ds(pl.multiple_of(block * rows, rows), rows)
        first_qt[:, part] = queries.astype(BF)
        first_kt[:, part] = nt(wkt[...], x[0]).astype(BF)
        first_vt[:, part] = (nt(wvt[...], x[0]) + bvc[...]).astype(BF)

    def keep(head):
        slot = lax.rem(head, 2)
        return pltpu.make_async_copy(pt.at[slot], pt_hbm.at[head], pt_sem.at[slot])

    def attend(head, carry):
        slots = first_kt.shape[1]

        @pl.when(head >= 2)
        def _():
            keep(head - 2).wait()

        band = pl.ds(pl.multiple_of(head * head_dim, head_dim), head_dim)
        index = lax.broadcasted_iota(jnp.int32, (16, slots), 1)
        first_row = lax.broadcasted_iota(jnp.int32, (16, slots), 0) == 0
        masked = jnp.where(first_row & (index >= key_len[0]), NEGATIVE, 0.0).astype(BF)
        ones = jnp.ones((16, slots), BF)
        scores = tn(
            jnp.concatenate([first_kt[band], masked], axis=0), jnp.concatenate([first_qt[band], ones], axis=0)
        )
        weights = jnp.exp2(scores - jnp.max(scores, axis=0, keepdims=True)).astype(BF)
        pt[lax.rem(head, 2)] = weights
        total = nn(jnp.concatenate([first_vt[band], ones], axis=0), weights)
        inv = 1.0 / total[head_dim : head_dim + 1]
        first_ot[band] = (total[:head_dim] * inv).astype(BF)
        inverse[pl.ds(head, 1)] = inv
        keep(head).start()
        return carry

    @pl.when((cell == pl.num_programs(0) - 1) & (block == pl.num_programs(1) - 1))
    def _():
        @pl.when(is_known)
        def _():
            results = fetch([(first_kt, kt_hbm), (first_vt, vt_hbm)], out_sem)
            lax.fori_loop(0, HEADS, attend, 0)
            results += fetch([(first_ot, ot_hbm)], out_sem.at[pl.ds(2, 1)])
            for head in (HEADS - 2, HEADS - 1):
                keep(head).wait()
            wait(*results)
            copy.wait_send()

        @pl.when(jnp.logical_not(is_known))
        def _():
            inverse[...] = jnp.zeros_like(inverse)
            copy.wait_recv()


def project_own(known_len, x, wq, bq, wk, wv, bv, rows=512):
    cells, slots, width = x.shape
    head_dim = width // HEADS
    bias = pl.BlockSpec((1, width), lambda c, i: (0, 0))
    out = pl.BlockSpec((1, width, rows), lambda c, i: (c, 0, i))
    hbm = pl.BlockSpec(memory_space=pl.ANY)
    last = cells - 1
    return pl.pallas_call(
        functools.partial(own_kernel, head_dim),
        grid=(cells, slots // rows),
        in_specs=[
            pl.BlockSpec(memory_space=pltpu.SMEM),
            hbm,
            pl.BlockSpec((1, rows, width), lambda c, i: (c, i, 0)),
            hbm,
            bias,
            hbm,
            hbm,
            bias,
        ],
        out_specs=[
            out,
            out,
            out,
            pl.BlockSpec((rows, width), lambda c, i: (lax.div(c, last) * i, 0)),
            pl.BlockSpec(memory_space=pltpu.SMEM),
            hbm,
            hbm,
            hbm,
            hbm,
            hbm,
            pl.BlockSpec((HEADS, slots), lambda c, i: (0, 0)),
        ],
        out_shape=[jax.ShapeDtypeStruct((cells, width, slots), BF)] * 3
        + [
            jax.ShapeDtypeStruct((slots, width), BF),
            jax.ShapeDtypeStruct((2, cells), F32),
            jax.ShapeDtypeStruct((slots, width), BF),
            jax.ShapeDtypeStruct((HEADS, slots, slots), BF),
        ]
        + [jax.ShapeDtypeStruct((width, slots), BF)] * 3
        + [jax.ShapeDtypeStruct((HEADS, slots), F32)],
        scratch_shapes=[pltpu.VMEM((width, width), BF)] * 3
        + [pltpu.VMEM((width, rows), F32)] * 2
        + [pltpu.VMEM((width, slots), BF)] * 4
        + [pltpu.VMEM((2, slots, slots), BF)]
        + [pltpu.VMEM((width, width), BF)] * 3
        + [pltpu.SemaphoreType.DMA] * 2
        + [pltpu.SemaphoreType.DMA((3,)), pltpu.SemaphoreType.DMA((2,)), pltpu.SemaphoreType.DMA((3,))],
        compiler_params=params(collective_id=1, has_side_effects=True),
        name="project_own",
    )(known_len, x, x, wq, bq, wk, wv, bv)


def steps_in(length):
    return lax.div(length + STEP - 1, STEP)


def sized(count, steps, body):
    for n in range(1, count + 1):
        pl.when(steps == n)(functools.partial(body, n * STEP))


def sized_pair(count, key_steps, own_steps, body):
    for a in range(1, count + 1):
        for b in range(1, count + 1):
            pl.when((key_steps == a) & (own_steps == b))(functools.partial(body, a * STEP, b * STEP))


def in_turns(chains):
    waiting = [iter(chain) for chain in chains]
    running = []
    while waiting or running:
        if waiting:
            running.append(waiting.pop(0))
        running = [chain for chain in running if next(chain, None) is not None]


def fold_rows(values):
    rows, width = values.shape
    return jnp.sum(values.reshape(rows // 8, 8, width), axis=0)


def fetch(pairs, semaphores):
    copies = [
        pltpu.make_async_copy(source, target, semaphores.at[i]) for i, (source, target) in enumerate(pairs)
    ]
    for copy in copies:
        copy.start()
    return copies


def wait(*copies):
    for copy in copies:
        copy.wait()


def taker(refs):
    place = 0

    def take(count):
        nonlocal place
        place += count
        return refs[place - count : place]

    return take


def cell_kernel(cell, first, *refs):
    take = taker(refs)
    info, own_norm, x_hbm, far_hbm, cot_hbm, qt_hbm, skt_hbm, svt_hbm = take(8)
    wk_hbm, wv_hbm, wo_hbm, wh_hbm, wr_hbm = take(5)
    bv, bo, g1, s1, bh, br, g2, s2 = take(8)
    _, sums_before, vecs_before = (None, None, None) if first else take(3)
    given_ot, given_inverse, *_ = take(5) if first else (None, None)
    out_hbm, sums_hbm, vecs, pt_hbm, kt_hbm, vt_hbm, dot_hbm, gres_hbm, inverse, self_exp, delta = take(11)
    x, source, cot, qt, skt, svt, wk, wv, wo, wh, wr = take(11)
    kt, vt, ot, dot_t, low1, act, gb, gpre, gres, out, sums, pt, wkt, wvt, bvc = take(15)
    in_sem, out_sem, block_sem, pt_sem = take(4)

    slots, width = x.shape
    head_dim = width // HEADS
    is_known = info[0] == 1
    cells = (info.shape[0] - 1) // 2
    key_len, own_len = info[1 + cell], info[1 + cells + cell]
    key_steps, own_steps = steps_in(key_len), steps_in(own_len)
    blocks = slots // STEP

    ready = is_known if first else jnp.bool_(False)
    heads = jnp.where(ready, 0, HEADS)

    if first:
        ot_load = pltpu.make_async_copy(given_ot, ot, in_sem.at[12])

        @pl.when(ready)
        def _():
            ot_load.start()
            inverse[...] = given_inverse[...]
            self_exp[...] = jnp.zeros_like(self_exp)

    known_source = pltpu.make_async_copy(x_hbm.at[cell], source, in_sem.at[0])
    far_source = pltpu.make_async_copy(far_hbm, source, in_sem.at[0])
    own_keys = [
        pltpu.make_async_copy(skt_hbm.at[cell], skt, in_sem.at[1]),
        pltpu.make_async_copy(svt_hbm.at[cell], svt, in_sem.at[2]),
    ]

    @pl.when(is_known)
    def _():
        known_source.start()

    @pl.when(jnp.logical_not(is_known))
    def _():
        far_source.start()

    loads = fetch([(wk_hbm, wk), (wv_hbm, wv)], in_sem.at[pl.ds(3, 2)])

    @pl.when(is_known)
    def _():
        known_source.wait()

    @pl.when(jnp.logical_not(is_known))
    def _():
        far_source.wait()
        for copy in own_keys:
            copy.start()

    wait(*loads)
    loads = fetch(
        [(qt_hbm.at[cell], qt), (wo_hbm, wo), (x_hbm.at[cell], x), (wh_hbm, wh), (wr_hbm, wr), (cot_hbm.at[cell], cot)]
        + ([] if first else [(sums_before, sums)]),
        in_sem.at[pl.ds(5, 7)],
    )

    def block_copies(block):
        part = pl.ds(block * STEP if isinstance(block, int) else pl.multiple_of(block * STEP, STEP), STEP)
        return [
            pltpu.make_async_copy(out.at[part], out_hbm.at[cell, part], block_sem.at[0, block]),
            pltpu.make_async_copy(dot_t.at[:, part], dot_hbm.at[:, part], block_sem.at[1, block]),
            pltpu.make_async_copy(gres.at[part], gres_hbm.at[part], block_sem.at[2, block]),
        ]

    wkt[...] = wk[...].T
    wvt[...] = wv[...].T
    bvc[...] = column(bv[...], STEP)

    def project(block, largest):
        part = pl.ds(pl.multiple_of(block * STEP, STEP), STEP)
        tokens = source[part]
        keys = nt(wkt[...], tokens)
        kt[:, part] = keys.astype(BF)
        vt[:, part] = (nt(wvt[...], tokens) + bvc[...]).astype(BF)
        return jnp.maximum(largest, head_norms(keys, head_dim))

    def blank(targets, block, carry):
        part = pl.ds(pl.multiple_of(block * STEP, STEP), STEP)
        for target in targets:
            if target.shape[0] == slots:
                target[part] = jnp.zeros((STEP, width), BF)
            else:
                target[:, part] = jnp.zeros((target.shape[0], STEP), target.dtype)
        return carry

    largest = lax.fori_loop(0, jnp.where(ready, 0, key_steps), project, jnp.float32(0.0))
    lax.fori_loop(key_steps, blocks, functools.partial(blank, (kt, vt)), 0)

    out_copies = []
    key_copies = [
        pltpu.make_async_copy(source, target, out_sem.at[i])
        for i, (source, target) in enumerate(((kt, kt_hbm), (vt, vt_hbm)))
    ]

    @pl.when(jnp.logical_not(ready))
    def _():
        for copy in key_copies:
            copy.start()

    @pl.when((key_steps < blocks) | (own_steps < blocks))
    def _():
        pt[...] = jnp.zeros_like(pt)

    def blank_block(block, carry):
        blank((out, gres, dot_t, delta), block, carry)

        @pl.when(jnp.logical_not(ready))
        def _():
            blank((inverse, self_exp), block, carry)

        for copy in block_copies(block):
            copy.start()
        return carry

    lax.fori_loop(own_steps, blocks, blank_block, 0)
    if first:
        pl.when(ready)(ot_load.wait)

    wait(loads[0])

    @pl.when(jnp.logical_not(is_known))
    def _():
        wait(*own_keys)

    largest = jnp.maximum(largest, own_norm[1, cell])
    safe = own_norm[0, cell] * largest < SAFE * SAFE

    def attend(head, slot, use_max, keys, queries):
        band = pl.ds(pl.multiple_of(head * head_dim, head_dim), head_dim)
        index = lax.broadcasted_iota(jnp.int32, (16, keys), 1)
        first_row = lax.broadcasted_iota(jnp.int32, (16, keys), 0) == 0
        masked = jnp.where(first_row & (index >= key_len), NEGATIVE, 0.0).astype(BF)
        key_part = jnp.concatenate([kt[band, :keys], masked], axis=0)
        q = qt[band, :queries]
        query_part = jnp.concatenate([q, jnp.ones((16, queries), BF)], axis=0)
        value_part = jnp.concatenate([vt[band, :keys], jnp.ones((16, keys), BF)], axis=0)
        scores = tn(key_part, query_part)
        own = jnp.sum(q.astype(F32) * skt[band, :queries].astype(F32), axis=0, keepdims=True)
        own = jnp.where(is_known, NEGATIVE, own)
        if use_max:
            top = jnp.maximum(jnp.max(scores, axis=0, keepdims=True), own)
            scores = scores - top
            own = own - top
        weights = jnp.exp2(scores).astype(BF)
        pt[slot, :keys, :queries] = weights
        own = jnp.exp2(own)
        total = nn(value_part, weights)
        inv = 1.0 / (total[head_dim : head_dim + 1] + own)
        own_values = jnp.where(is_known, 0.0, svt[band, :queries].astype(F32))
        ot[band, :queries] = ((total[:head_dim] + own * own_values) * inv).astype(BF)
        row = pl.ds(head, 1)
        inverse[row, :queries] = inv
        self_exp[row, :queries] = own

    def keep(head, slot):
        return pltpu.make_async_copy(pt.at[slot], pt_hbm.at[head], pt_sem.at[slot])

    def one_head(head, carry):
        slot = lax.rem(head, 2)

        @pl.when(head >= 2)
        def _():
            keep(head - 2, slot).wait()

        @pl.when(safe)
        def _():
            sized_pair(blocks, key_steps, own_steps, functools.partial(attend, head, slot, False))

        @pl.when(jnp.logical_not(safe))
        def _():
            attend(head, slot, True, slots, slots)

        keep(head, slot).start()
        return carry

    lax.fori_loop(0, heads, one_head, 0)

    wait(*loads[1:6])
    scale = 1.0 / width
    if first:
        vecs[...] = jnp.zeros_like(vecs)
    else:
        vecs[...] = vecs_before[...]

    def mean(values):
        return jnp.sum(values, axis=1, keepdims=True) * scale

    def chain(block):
        start = pl.multiple_of(block * STEP, STEP)
        part = pl.ds(start, STEP)
        slot_index = lax.broadcasted_iota(jnp.int32, (STEP, 1), 0) + start
        live = (slot_index < own_len).astype(F32)
        context = ot[:, part]
        r1 = tn(context, wo[...])
        yield 1
        r1 = r1 + x[part].astype(F32) + bo[...]
        centred = r1 - mean(r1)
        inv1 = lax.rsqrt(mean(centred * centred) + EPS)
        hat1 = centred * inv1
        norm1 = hat1 * g1[...] + s1[...]
        low = norm1.astype(BF)
        low1[part] = low
        yield 2
        pre = nn(low, wh[...])
        yield 3
        pre = pre + bh[...]
        cdf = 0.5 + 0.5 * lax.erf(pre * (0.5**0.5))
        active = (pre * cdf).astype(BF)
        act[part] = active
        slope = cdf + pre * (jnp.exp(-0.5 * pre * pre) * 0.3989422804014327)
        yield 4
        r2 = nn(active, wr[...])
        yield 5
        r2 = r2 + norm1 + br[...]
        centred = r2 - mean(r2)
        inv2 = lax.rsqrt(mean(centred * centred) + EPS)
        hat2 = centred * inv2
        out[part] = ((hat2 * g2[...] + s2[...]) * live).astype(BF)
        go = cot[part].astype(F32) * live
        vecs[0] += fold_rows(go * hat2)
        vecs[1] += fold_rows(go)
        gx = go * g2[...]
        gr2 = inv2 * (gx - mean(gx) - hat2 * mean(gx * hat2))
        grad_branch = gr2.astype(BF)
        gb[part] = grad_branch
        vecs[2] += fold_rows(grad_branch.astype(F32))
        yield 6
        grad_act = nt(grad_branch, wr[...])
        yield 7
        grad_pre = (grad_act * slope).astype(BF)
        gpre[part] = grad_pre
        vecs[3] += fold_rows(grad_pre.astype(F32))
        yield 8
        gn = nt(grad_pre, wh[...])
        yield 9
        gn = gr2 + gn
        vecs[4] += fold_rows(gn * hat1)
        vecs[5] += fold_rows(gn)
        gx = gn * g1[...]
        gr1 = inv1 * (gx - mean(gx) - hat1 * mean(gx * hat1))
        grad_attn = gr1.astype(BF)
        gres[part] = grad_attn
        vecs[6] += fold_rows(grad_attn.astype(F32))
        yield 10
        back = nt(wo[...], grad_attn)
        yield 11
        low_back = back.astype(BF)
        dot_t[:, part] = low_back
        product = low_back.astype(F32) * context.astype(F32)
        delta[:, part] = jnp.sum(product.reshape(HEADS, head_dim, STEP), axis=1)
        for copy in block_copies(block):
            copy.start()

    def pair(index, carry):
        in_turns([chain(2 * index), chain(2 * index + 1)])
        return carry

    lax.fori_loop(0, lax.div(own_steps, 2), pair, 0)

    @pl.when(lax.rem(own_steps, 2) == 1)
    def _():
        in_turns([chain(own_steps - 1)])

    if not first:
        wait(loads[6])

    def weight_sum(i, rows):
        if i == 0:
            value = nn(ot[:, :rows], gres[:rows])
        elif i == 1:
            value = tn(low1[:rows], gpre[:rows])
        else:
            value = tn(act[:rows], gb[:rows])
        sums[i] = value if first else sums[i] + value

    for i in range(3):
        sized(blocks, own_steps, functools.partial(weight_sum, i))
        out_copies += fetch([(sums.at[i], sums_hbm.at[i])], out_sem.at[pl.ds(2 + i, 1)])

    @pl.when(jnp.logical_not(ready))
    def _():
        for slot in range(2):
            keep(HEADS - 2 + slot, slot).wait()
        wait(*key_copies)

    for block in range(blocks):
        wait(*block_copies(block))
    wait(*out_copies)


def run_cell(info, cell, own_norm, x, far, cot, qt, skt, svt, weights, vectors, carried, given):
    cells, slots, width = x.shape
    smem = pl.BlockSpec(memory_space=pltpu.SMEM)
    vmem = pl.BlockSpec(memory_space=pltpu.VMEM)
    hbm = pl.BlockSpec(memory_space=pl.ANY)
    first = not carried
    across, along = (width, slots), (slots, width)
    square = (width, width)
    stats = (HEADS, slots)
    scratch = [along] * 3 + [across] * 3 + [square] * 5 + [across] * 4 + [along] * 6
    return pl.pallas_call(
        functools.partial(cell_kernel, cell, first),
        in_specs=[smem, smem] + [hbm] * 11 + [vmem] * 8 + ([hbm, vmem, hbm, hbm, hbm] if first else [hbm, hbm, vmem]),
        out_specs=[hbm, hbm, vmem] + [hbm] * 5 + [vmem] * 3,
        out_shape=[
            jax.ShapeDtypeStruct((cells, slots, width), BF),
            jax.ShapeDtypeStruct((3, width, width), F32),
            jax.ShapeDtypeStruct((8, 8, width), F32),
            jax.ShapeDtypeStruct((HEADS, slots, slots), BF),
        ]
        + [jax.ShapeDtypeStruct(across, BF)] * 3
        + [jax.ShapeDtypeStruct(along, BF)]
        + [jax.ShapeDtypeStruct(stats, F32)] * 3,
        scratch_shapes=[pltpu.VMEM(shape, BF) for shape in scratch]
        + [
            pltpu.VMEM((3, width, width), F32),
            pltpu.VMEM((2, slots, slots), BF),
            pltpu.VMEM(square, BF),
            pltpu.VMEM(square, BF),
            pltpu.VMEM((width, STEP), F32),
            pltpu.SemaphoreType.DMA((13,)),
            pltpu.SemaphoreType.DMA((5,)),
            pltpu.SemaphoreType.DMA((3, slots // STEP)),
            pltpu.SemaphoreType.DMA((2,)),
        ],
        input_output_aliases={23: 3, 24: 4, 25: 5} if first else {21: 0},
        compiler_params=params(),
        name="cell_forward",
    )(info, own_norm, x, far, cot, qt, skt, svt, *weights, *vectors, *carried, *given)


class Places:
    def __init__(self):
        cells = lax.axis_size("cells")
        self.half, self.cell = lax.axis_index("half"), lax.axis_index("cells")
        bits = [lax.rem(lax.div(self.cell, 2**power), 2) for power in range(cells.bit_length() - 1)]
        self.bits = [bits[0], self.half] + bits[1:]
        self.spans = [1, 0] + [2**power for power in range(1, len(bits))]

    def partner(self, flips):
        cell = self.cell
        for dim in flips:
            cell = cell + (1 - 2 * self.bits[dim]) * self.spans[dim]
        return {"half": 1 - self.half if 1 in flips else self.half, "cells": cell}

    def member(self, group, flips=()):
        index = 0
        for dim in group:
            index = 2 * index + (1 - self.bits[dim] if dim in flips else self.bits[dim])
        return index

    def send(self, flips, source, target, sent, arrived):
        copy = pltpu.make_async_remote_copy(
            src_ref=source,
            dst_ref=target,
            send_sem=sent,
            recv_sem=arrived,
            device_id=self.partner(flips),
            device_id_type=pl.DeviceIdType.MESH,
        )
        copy.start()
        return copy


def dims_of():
    return 1 + lax.axis_size("cells").bit_length() - 1


def groups_of(dims):
    rest = list(range(2, dims)) + [1]
    return [[0]] + [rest[start : start + 2] for start in range(0, len(rest), 2)]


def flips_of(group):
    return [tuple(group)] if len(group) == 1 else [(group[1],), (group[0],), tuple(group)]


def plan_of(order, rows):
    plan, base = [], 0
    for group in order:
        split = rows % (16 * 2 ** len(group)) == 0
        rows = rows // 2 ** len(group) if split else rows
        plan.append((group, rows, split, base))
        base += rows * len(flips_of(group))
    return plan, base


def room_for(rows, dims):
    return plan_of(groups_of(dims), rows)[1]


def total_of(own, came):
    return own + came[0] if len(came) == 1 else (own + came[0]) + (came[1] + came[2])


def summed_over_devices(places, mats, out, sent, got, semaphores):
    send_sem, recv_sem, back_send, back_recv = semaphores
    count, rows = mats.shape[0], mats.shape[1]
    plans = [plan_of(order, rows)[0] for order in [groups_of(len(places.bits))] * count]
    steps = len(plans[0])
    at_row = [jnp.int32(0)] * count
    started = [()] * count

    def at(place, length):
        return pl.ds(pl.multiple_of(place, 16), length)

    def finish(i, step):
        group, length, split, base = plans[i][step]
        wait(*started[i])
        here = at(at_row[i], length)
        kept = mats[i, here] if split else sent[i, base : base + length].astype(F32)
        came = [
            got[i, base + k * length : base + (k + 1) * length].astype(F32) for k in range(len(flips_of(group)))
        ]
        mats[i, here] = total_of(kept, came)

    for step in range(steps):
        for i in range(count):
            if step > 0:
                finish(i, step - 1)
            group, length, split, base = plans[i][step]
            copies = []
            if not split:
                sent[i, base : base + length] = mats[i, at(at_row[i], length)].astype(BF)
            for k, flips in enumerate(flips_of(group)):
                part = pl.ds(base + k * length, length)
                if split:
                    away = at_row[i] + places.member(group, flips) * length
                    sent[i, part] = mats[i, at(away, length)].astype(BF)
                source = part if split else pl.ds(base, length)
                copies.append(
                    places.send(
                        flips, sent.at[i, source], got.at[i, part], send_sem.at[i, step, k], recv_sem.at[i, step, k]
                    )
                )
            started[i] = copies
            if split:
                at_row[i] = at_row[i] + places.member(group) * length
        yield step
    for i in range(count):
        finish(i, steps - 1)
        here = at(at_row[i], plans[i][-1][1])
        out[i, here] = mats[i, here].astype(BF)
        started[i] = ()
    remaining = [[step for step in reversed(range(steps)) if plan[step][2]] for plan in plans]
    while any(remaining):
        for i in range(count):
            if not remaining[i]:
                continue
            step = remaining[i].pop(0)
            group, length, _, _ = plans[i][step]
            wait(*started[i])
            part = at(at_row[i], length)
            started[i] = [
                places.send(
                    flips, out.at[i, part], out.at[i, part], back_send.at[i, step, k], back_recv.at[i, step, k]
                )
                for k, flips in enumerate(flips_of(group))
            ]
            at_row[i] = at_row[i] - places.member(group) * length
        yield 0
    for i in range(count):
        wait(*started[i])


def vectors_over_devices(places, vec, out, sent, got, send_sem, recv_sem):
    for step, group in enumerate(groups_of(len(places.bits))):
        sent[step] = vec
        copies = [
            places.send(flips, sent.at[step], got.at[step, k], send_sem.at[step, k], recv_sem.at[step, k])
            for k, flips in enumerate(flips_of(group))
        ]
        yield step
        wait(*copies)
        vec = total_of(vec, [got[step, k] for k in range(len(copies))])
    out[...] = vec


def backward_kernel(cells, *refs):
    take = taker(refs)
    mats_hbm, x_hbm, qt_hbm, skt_hbm, svt_hbm, wq_hbm, wk_hbm, wv_hbm, dense_vecs = take(9)
    far_hbm, pt_hbm, kt_hbm, vt_hbm, dot_hbm, gres_hbm, inverse, self_exp, delta = (
        take(cells) for _ in range(9)
    )
    grad_hbm, dense_hbm, vecs_out = take(3)
    back_out = take(len(PIECES))
    x, far, far_grad, grad, qt, skt, svt, kt, vt, dot_t, dq, pt = take(12)
    wq, wk, wv, wqt, wkt, wvt, dense_mats, vecs = take(8)
    back_mats = take(len(PIECES))
    dense_bufs, vec_bufs, dense_sems, vec_sems = take(2), take(2), take(4), take(2)
    back_bufs = [take(2) for _ in PIECES]
    back_sems = [take(4) for _ in PIECES]
    in_sem, out_sem, pt_sem, far_send, far_recv, dense_out = take(6)

    _, slots, width = x.shape
    head_dim = width // HEADS
    halfway = slots // 2
    half_at = lax.axis_index("half")
    is_known = half_at == 0

    places = Places()
    barrier = pltpu.get_barrier_semaphore()
    neighbours = [flips for group in groups_of(len(places.bits)) for flips in flips_of(group)]
    if (1,) not in neighbours:
        neighbours.append((1,))
    for flips in neighbours:
        pl.semaphore_signal(
            barrier, inc=1, device_id=places.partner(flips), device_id_type=pl.DeviceIdType.MESH
        )

    steps = cells * 2 * HEADS
    slots_kept = pt.shape[0]

    def bring(n, begin):
        head, slot = lax.rem(n, HEADS), lax.rem(n, slots_kept)
        part = pl.ds(pl.multiple_of(lax.rem(lax.div(n, HEADS), 2) * halfway, halfway), halfway)
        for cell in range(cells):

            @pl.when(lax.div(n, 2 * HEADS) == cell)
            def _():
                copy = pltpu.make_async_copy(
                    pt_hbm[cell].at[head, part], pt.at[slot], pt_sem.at[slot]
                )
                if begin:
                    copy.start()
                else:
                    copy.wait()

    for n in range(slots_kept - 1):
        bring(jnp.int32(n), True)
    urgent = fetch(
        [
            (vt_hbm[0], vt.at[0]),
            (dot_hbm[0], dot_t.at[0]),
            (kt_hbm[0], kt.at[0]),
            (qt_hbm.at[0], qt.at[0]),
        ],
        in_sem,
    )
    wait(*urgent)
    pairs = [(mats_hbm, dense_mats), (skt_hbm.at[0], skt.at[0]), (svt_hbm.at[0], svt.at[0])]
    pairs += [(wk_hbm, wk), (wv_hbm, wv), (wq_hbm, wq)]
    for cell in range(1, cells):
        pairs += [
            (vt_hbm[cell], vt.at[cell]),
            (dot_hbm[cell], dot_t.at[cell]),
            (kt_hbm[cell], kt.at[cell]),
            (qt_hbm.at[cell], qt.at[cell]),
            (skt_hbm.at[cell], skt.at[cell]),
            (svt_hbm.at[cell], svt.at[cell]),
        ]
    pairs.append((x_hbm, x))
    pairs += [(gres_hbm[cell], grad.at[cell]) for cell in range(cells)]
    loads = fetch(pairs, in_sem.at[pl.ds(4, len(pairs))])

    def far_loads():
        return [
            pltpu.make_async_copy(far_hbm[cell], far.at[cell], in_sem.at[4 + len(pairs) + cell])
            for cell in range(cells)
        ]

    @pl.when(jnp.logical_not(is_known))
    def _():
        for copy in far_loads():
            copy.start()

    pl.semaphore_wait(barrier, len(neighbours))
    dense_sum = summed_over_devices(places, dense_mats, dense_out, *dense_bufs, dense_sems)
    back_sums = [
        summed_over_devices(places, back_mats[i], back_out[i], *back_bufs[i], back_sems[i])
        for i in range(len(PIECES))
    ]

    def attend(cell, half, n):
        head, slot = lax.rem(n, HEADS), lax.rem(n, slots_kept)
        band = pl.ds(pl.multiple_of(head * head_dim, head_dim), head_dim)
        row = pl.ds(head, 1)
        q = qt[cell, band]
        inv = inverse[cell][row]
        grads = dot_t[cell, band].astype(F32)
        scaled = (grads * inv).astype(BF)
        inner = delta[cell][row]
        inner_scaled = inner * inv
        high = inner_scaled.astype(BF)
        rest = (inner_scaled - high.astype(F32)).astype(BF)
        wide = jnp.concatenate(
            [scaled, jnp.broadcast_to(high, (8, slots)), jnp.broadcast_to(rest, (8, slots))], axis=0
        )
        signs = jnp.where(lax.broadcasted_iota(jnp.int32, (16, STEP), 0) % 8 == 0, -1.0, 0.0).astype(BF)
        total = dq[band] if half == 1 else 0.0
        for start in range(0, halfway, STEP):
            part = slice(half * halfway + start, half * halfway + start + STEP)
            weights = pt[slot, start : start + STEP]
            grad_probs = tn(jnp.concatenate([vt[cell, band, part], signs], axis=0), wide)
            grad_scores = (weights.astype(F32) * grad_probs).astype(BF)
            keys = kt[cell, band, part]
            vt[cell, band, part] = nt(scaled, weights).astype(BF)
            kt[cell, band, part] = (nt(q, grad_scores) * (1.0 / LOG2E)).astype(BF)
            total = total + nn(keys, grad_scores)
        if half == 0:
            dq[band] = total
            return
        prob = self_exp[cell][row] * inv
        own_keys = jnp.where(is_known, 0.0, skt[cell, band].astype(F32))
        own_values = jnp.where(is_known, 0.0, svt[cell, band].astype(F32))
        grad_prob = jnp.sum(grads * own_values, axis=0, keepdims=True)
        grad_score = prob * (grad_prob - inner)
        qt[cell, band] = ((total + grad_score * own_keys) * head_dim**-0.5).astype(BF)
        skt[cell, band] = (q.astype(F32) * (grad_score * (1.0 / LOG2E))).astype(BF)
        svt[cell, band] = (grads * prob).astype(BF)

    def far_copy(cell, half):
        part = pl.ds(half * halfway, halfway)
        return pltpu.make_async_remote_copy(
            src_ref=far_grad.at[cell, part],
            dst_ref=far.at[cell, part],
            send_sem=far_send.at[cell, half],
            recv_sem=far_recv.at[cell, half],
            device_id=places.partner((1,)),
            device_id_type=pl.DeviceIdType.MESH,
        )

    def send_far(cell, half):
        @pl.when(jnp.logical_not(is_known))
        def _():
            for start in range(half * halfway, (half + 1) * halfway, STEP):
                part = slice(start, start + STEP)
                total = tn(kt[cell, :, part], wkt[...]) + tn(vt[cell, :, part], wvt[...])
                far_grad[cell, part] = total.astype(BF)
            far_copy(cell, half).start()

    def weight_sums(cell, pieces):
        begin = PIECES[pieces[0]][0] * head_dim
        band = slice(begin, (PIECES[pieces[-1]][0] + PIECES[pieces[-1]][1]) * head_dim)

        def add(i, value, anew):
            for piece in pieces:
                start = PIECES[piece][0] * head_dim - begin
                part = value[start : start + PIECES[piece][1] * head_dim]
                back_mats[piece][i] = part if anew else back_mats[piece][i] + part

        grad_k = jnp.where(is_known, kt[cell, band], skt[cell, band])
        grad_v = jnp.where(is_known, vt[cell, band], svt[cell, band])
        for i, part in enumerate((qt[cell, band], grad_k, grad_v)):
            add(i, nn(part, x[cell]), cell == 0)

        @pl.when(jnp.logical_not(is_known))
        def _():
            add(1, nn(kt[cell, band], far[cell]), False)
            add(2, nn(vt[cell, band], far[cell]), False)

    def bias_sums(cell):
        ones = jnp.ones((8, slots), BF)
        grad_v = jnp.where(is_known, vt[cell], svt[cell])
        vecs[8:9] += nt(ones, qt[cell])[:1]
        vecs[9:10] += nt(ones, grad_v)[:1]

        @pl.when(jnp.logical_not(is_known))
        def _():
            vecs[9:10] += nt(ones, vt[cell])[:1]

    def own_rows(cell, start):
        part = slice(start, start + STEP)
        grad_k = jnp.where(is_known, kt[cell, :, part], skt[cell, :, part])
        grad_v = jnp.where(is_known, vt[cell, :, part], svt[cell, :, part])
        total = grad[cell, part].astype(F32) + tn(qt[cell, :, part], wqt[...])
        total = total + tn(grad_k, wkt[...]) + tn(grad_v, wvt[...])
        grad[cell, part] = total.astype(BF)

    group = 2
    per_pass = HEADS // group
    for index in range(steps // group):
        cell, half, turn = index // (2 * per_pass), (index // per_pass) % 2, index % per_pass

        def one(i, carry):
            n = index * group + i

            @pl.when(n + slots_kept - 1 < steps)
            def _():
                bring(n + slots_kept - 1, True)

            bring(n, False)
            attend(cell, half, n)
            return carry

        lax.fori_loop(0, group, one, 0)
        if index == 0:
            wait(loads[0])
        if index in DENSE_TURNS:
            next(dense_sum, None)
        if index == 0:
            vecs[:8] = jnp.sum(dense_vecs[...], axis=1)
            vecs[8:] = jnp.zeros((8, width), F32)
            wait(*loads[1:])

            @pl.when(jnp.logical_not(is_known))
            def _():
                wait(*far_loads())

            wqt[...] = wq[...].T
            wkt[...] = wk[...].T
            wvt[...] = wv[...].T
        every = list(range(len(PIECES)))
        if half == 1 and cell < cells - 1 and turn == per_pass - 1:
            weight_sums(cell, every)
            bias_sums(cell)
        if half == 1 and cell == cells - 1:
            for piece in every:
                if sum(PIECES[piece]) == (turn + 1) * group:
                    weight_sums(cell, [piece])
                    next(back_sums[piece])
        if turn == per_pass - 1:
            send_far(cell, half)
    next(back_sums[0])
    bias_sums(cells - 1)
    vec_sum = vectors_over_devices(places, vecs[...], vecs_out, *vec_bufs, *vec_sems)
    next(vec_sum)
    running = [*back_sums[::-1], vec_sum, dense_sum]
    out_copies = []
    for cell in range(cells):
        for start in range(0, slots, STEP):
            own_rows(cell, start)
            if start % halfway > 0:
                running = [chain for chain in running if next(chain, None) is not None]
        if cell == 0:
            for _ in dense_sum:
                pass
            out_copies += fetch([(dense_out, dense_hbm)], out_sem.at[pl.ds(cells, 1)])
        if cell == cells - 1:
            while running:
                running = [chain for chain in running if next(chain, None) is not None]

        @pl.when(is_known)
        def _():
            for half in range(2):
                far_copy(cell, half).wait_recv()
            grad[cell] = (grad[cell].astype(F32) + far[cell].astype(F32)).astype(BF)

        out_copies += fetch([(grad.at[cell], grad_hbm.at[cell])], out_sem.at[pl.ds(cell, 1)])

    @pl.when(jnp.logical_not(is_known))
    def _():
        for cell in range(cells):
            for half in range(2):
                far_copy(cell, half).wait_send()

    wait(*out_copies)


def backward(mats, x, qt, skt, svt, weights, dense_vecs, fars, kept):
    cells, slots, width = x.shape
    dims = dims_of()
    turns = len(groups_of(dims))
    vmem = pl.BlockSpec(memory_space=pltpu.VMEM)
    hbm = pl.BlockSpec(memory_space=pl.ANY)
    across, along = (cells, width, slots), (cells, slots, width)
    square = (width, width)
    head_dim = width // HEADS
    rows = [count * head_dim for _, count in PIECES]
    sums = pltpu.SemaphoreType.DMA((3, turns, 3))
    loads = 6 * cells + 5 + 2 * cells
    return pl.pallas_call(
        functools.partial(backward_kernel, cells),
        in_specs=[hbm] * 8 + [vmem] + [hbm] * (6 * cells) + [vmem] * (3 * cells),
        out_specs=[hbm, hbm] + [vmem] * (1 + len(rows)),
        out_shape=[
            jax.ShapeDtypeStruct((cells, slots, width), BF),
            jax.ShapeDtypeStruct((3, width, width), BF),
            jax.ShapeDtypeStruct((16, width), F32),
        ]
        + [jax.ShapeDtypeStruct((3, n, width), BF) for n in rows],
        scratch_shapes=[pltpu.VMEM(along, BF)] * 4
        + [pltpu.VMEM(across, BF)] * 6
        + [pltpu.VMEM((width, slots), F32), pltpu.VMEM((4, slots // 2, slots), BF)]
        + [pltpu.VMEM(square, BF)] * 6
        + [pltpu.VMEM((3, width, width), F32), pltpu.VMEM((16, width), F32)]
        + [pltpu.VMEM((3, n, width), F32) for n in rows]
        + [pltpu.VMEM((3, room_for(width, dims), width), BF)] * 2
        + [pltpu.VMEM((turns, 16, width), F32), pltpu.VMEM((turns, 3, 16, width), F32)]
        + [sums] * 4
        + [pltpu.SemaphoreType.DMA((turns, 3))] * 2
        + [pltpu.VMEM((3, room_for(n, dims), width), BF) for n in rows for _ in range(2)]
        + [sums] * (4 * len(rows))
        + [
            pltpu.SemaphoreType.DMA((loads,)),
            pltpu.SemaphoreType.DMA((cells + 1,)),
            pltpu.SemaphoreType.DMA((4,)),
            pltpu.SemaphoreType.DMA((cells, 2)),
            pltpu.SemaphoreType.DMA((cells, 2)),
            pltpu.VMEM((3, width, width), BF),
        ],
        compiler_params=params(collective_id=0, has_side_effects=True),
        name="backward",
    )(mats, x, qt, skt, svt, *weights, dense_vecs, *fars, *(kept_of for column_of in zip(*kept) for kept_of in column_of))


def finish_kernel(grad, dense_mats, vecs, *refs):
    take = taker(refs)
    back_mats = take(len(PIECES))
    grad_out, wq, bq, wk, wv, bv, wo, bo, g1, s1, wh, bh, wr, br, g2, s2 = take(16)
    back_in = take(len(PIECES))
    kept, dense_in, results, in_sem, out_sem = take(5)
    cells = kept.shape[0]
    loads = fetch(
        list(zip(back_mats, back_in)) + [(dense_mats, dense_in)] + [(grad.at[c], kept.at[c]) for c in range(cells)],
        in_sem,
    )
    pieces = len(PIECES)
    wait(*loads[:pieces])
    copies = []
    for i, target in enumerate((wq, wk, wv, wo, wh, wr)):
        if i == 3:
            wait(loads[pieces])
        if i < 3:
            whole = jnp.concatenate([piece[i] for piece in back_in], axis=0).astype(F32).T
        else:
            whole = dense_in[i - 3].astype(F32)
        results[i] = whole
        copies += fetch([(results.at[i], target)], out_sem.at[pl.ds(i, 1)])
    for c in range(cells):
        wait(loads[pieces + 1 + c])
        copies += fetch([(kept.at[c], grad_out.at[c])], out_sem.at[pl.ds(6 + c, 1)])
    for i, target in enumerate((g2, s2, br, bh, g1, s1, bo, None, bq, bv)):
        if target is not None:
            target[...] = vecs[i]
    wait(*copies)


def finish(grad, dense_mats, vecs, *back_mats):
    cells = grad.shape[0]
    width = vecs.shape[1]
    vmem = pl.BlockSpec(memory_space=pltpu.VMEM)
    hbm = pl.BlockSpec(memory_space=pl.ANY)
    matrix = jax.ShapeDtypeStruct((width, width), F32)
    vector = jax.ShapeDtypeStruct((width,), F32)
    shapes = [matrix, vector, matrix, matrix, vector, matrix, vector, vector, vector]
    shapes += [matrix, vector, matrix, vector, vector, vector]
    return pl.pallas_call(
        finish_kernel,
        in_specs=[hbm, hbm, vmem] + [hbm] * len(back_mats),
        out_specs=[hbm] + [hbm if shape is matrix else vmem for shape in shapes],
        out_shape=[jax.ShapeDtypeStruct(grad.shape, BF)] + shapes,
        scratch_shapes=[pltpu.VMEM(piece.shape, BF) for piece in back_mats]
        + [
            pltpu.VMEM(grad.shape, BF),
            pltpu.VMEM(dense_mats.shape, BF),
            pltpu.VMEM((6, width, width), F32),
            pltpu.SemaphoreType.DMA((1 + len(back_mats) + cells,)),
            pltpu.SemaphoreType.DMA((6 + cells,)),
        ],
        compiler_params=params(),
        name="finish",
    )(grad, dense_mats, vecs, *back_mats)


def passed_along(value, axis, by):
    count = lax.axis_size(axis)
    pairs = [(i, i + by) for i in range(count) if 0 <= i + by < count]
    return lax.ppermute(value, axis, pairs)


def local(
    tokens,
    known_len,
    unknown_len,
    query_weight,
    query_bias,
    key_weight,
    value_weight,
    value_bias,
    output_weight,
    output_bias,
    first_gain,
    first_shift,
    hidden_weight,
    hidden_bias,
    return_weight,
    return_bias,
    second_gain,
    second_shift,
    cotangent,
):
    _, cells, slots, width = tokens.shape
    is_known = lax.axis_index("half") == 0
    x = tokens.reshape(cells, slots, width)
    cot = cotangent.reshape(cells, slots, width)
    own_len = jnp.where(is_known, known_len, unknown_len)
    info = jnp.concatenate([is_known.astype(jnp.int32)[None], known_len, own_len])

    def row(vector):
        return vector.reshape(1, width)

    qt, skt, svt, last_tokens, own_norm, far, pt, kt, vt, ot, inverse = project_own(
        known_len, x, query_weight, row(query_bias), key_weight, value_weight, row(value_bias)
    )
    fars = [far] + [
        passed_along(last_tokens if c == cells - 1 else x[c], "half", 1) for c in range(1, cells)
    ]
    weights = (key_weight, value_weight, output_weight, hidden_weight, return_weight)
    vectors = [
        row(vector)
        for vector in (
            value_bias,
            output_bias,
            first_gain,
            first_shift,
            hidden_bias,
            return_bias,
            second_gain,
            second_shift,
        )
    ]
    carried = ()
    kept = []
    for c in range(cells):
        layer_out, sums, vecs, pt, kt, vt, dot_t, gres, *stats = run_cell(
            info, c, own_norm, x, fars[c], cot, qt, skt, svt, weights, vectors, carried, () if carried else (ot, inverse, pt, kt, vt)
        )
        carried = (layer_out, sums, vecs)
        kept.append((pt, kt, vt, dot_t, gres, *stats))
    weights = (query_weight, key_weight, value_weight)
    grad, *sums = backward(sums, x, qt, skt, svt, weights, vecs, fars, kept)
    grad, *summed = finish(grad, *sums)
    out_shape = (1, cells, slots, width)
    return (layer_out.reshape(out_shape), grad.reshape(out_shape), *summed)


def solution(mesh):
    placed = (
        (P("half", "cells", None, None), P("cells"), P("cells"))
        + (P(),) * 15
        + (P("half", "cells", None, None),)
    )
    return jax.shard_map(
        local,
        mesh=mesh,
        in_specs=placed,
        out_specs=(P("half", "cells", None, None),) * 2 + (P(),) * 15,
        check_vma=False,
    )
```
